32 devices in a mesh: dp: 32 (over z, y, x, core).
Axes of the slice: x: 2, y: 2, z: 4, core: 2. Of those that a mesh axis runs over, the one named last changes fastest.
Arguments:
- inputs: bfloat16 [3, 32768, 384], P(None, 'dp'), may hold values from -6 to 6
- cotangent: bfloat16 [3, 32768, 384], P(None, 'dp'), may hold values from -6 to 6
- w_qkv: bfloat16 [384, 1152], P('dp'), may hold values from -0.3125 to 0.3125
- w_out: bfloat16 [384, 384], P('dp'), may hold values from -0.875 to 0.875
- w_fc1: bfloat16 [384, 1536], P('dp'), may hold values from -0.3125 to 0.3125
- w_fc2: bfloat16 [1536, 384], P('dp'), may hold values from -0.15625 to 0.15625
- norm1_gain: bfloat16 [384], P('dp'), may hold values from 0.5 to 1.5
- norm1_bias: bfloat16 [384], P('dp'), may hold values from -4 to 4
- query_bias: bfloat16 [384], P('dp'), may hold values from -6 to 6
- value_bias: bfloat16 [384], P('dp'), may hold values from -6 to 6
- out_bias: bfloat16 [384], P('dp'), may hold values from -4 to 4
- norm2_gain: bfloat16 [384], P('dp'), may hold values from 0.5 to 1.5
- norm2_bias: bfloat16 [384], P('dp'), may hold values from -4 to 4
- fc1_bias: bfloat16 [1536], P('dp'), may hold values from -6 to 6
- fc2_bias: bfloat16 [384], P('dp'), may hold values from -4 to 4
- image_tokens: int32 [3, 32], replicated, may hold values from 102 to 326, as said below
- image_count: int32 [3, 32], replicated, may hold values from 2 to 10, as said below
Outputs:
- outputs: bfloat16 [3, 32768, 384], P(None, 'dp')
- input_grad: bfloat16 [3, 32768, 384], P(None, 'dp')
- grad_qkv: float32 [384, 1152], P('dp')
- grad_out: float32 [384, 384], P('dp')
- grad_fc1: float32 [384, 1536], P('dp')
- grad_fc2: float32 [1536, 384], P('dp')
- grad_norm1_gain: float32 [384], P('dp')
- grad_norm1_bias: float32 [384], P('dp')
- grad_query_bias: float32 [384], P('dp')
- grad_value_bias: float32 [384], P('dp')
- grad_out_bias: float32 [384], P('dp')
- grad_norm2_gain: float32 [384], P('dp')
- grad_norm2_bias: float32 [384], P('dp')
- grad_fc1_bias: float32 [1536], P('dp')
- grad_fc2_bias: float32 [384], P('dp')
The draws below stay inside these ranges and needn't reach their ends.
Inputs may be any that keep to these rules, and one draw needn't show every extreme that they name: `image_tokens`: each entry is one of 102, 198, 326. image_count times the matching image_tokens entry is at most 1024; the images fill the first slots of their block.
All inputs are finite; a program needn't handle non-finite values.
Results may differ from the reference program's by a relative error of at most 0.012.
Values may be sent and summed in bfloat16 or wider, within the bound.
A program may use at most 192 MiB of HBM per device.

```python
import jax
import jax.numpy as jnp
from jax import lax

D = 384
HEADS = 6
FF = 1536
ROWS = 1024
MICRO = 3
LEN_A = 102
LEN_B = 198
LEN_C = 326
SLOTS = 32768
N_DP = 32


def draw_layout(key):
    resolution = jax.random.randint(jax.random.fold_in(key, 101), (MICRO, N_DP), 0, 3)
    resolution = resolution.at[0, 0].set(0).at[MICRO - 1, N_DP - 1].set(2)
    tokens = jnp.where(resolution == 0, LEN_A, jnp.where(resolution == 1, LEN_B, LEN_C)).astype(jnp.int32)
    most = (ROWS // tokens).astype(jnp.int32)
    least = (most // 2 + 1).astype(jnp.int32)
    counts = jax.random.randint(jax.random.fold_in(key, 202), (MICRO, N_DP), least, most + 1)
    counts = counts.at[0, 0].set(most[0, 0])
    counts = counts.at[MICRO - 1, N_DP - 1].set(least[MICRO - 1, N_DP - 1]).astype(jnp.int32)
    return (tokens, counts)


def draw_image_tokens(key, part):
    tokens, counts = draw_layout(key)
    return tokens


def draw_image_count(key, part):
    tokens, counts = draw_layout(key)
    return counts


def level_of(key, dims, cuts, low, largest):
    def one(dim, parts):
        draws = jax.random.uniform(jax.random.fold_in(jax.random.fold_in(key, 6), dim), (parts,), jnp.float32, low / len(cuts), largest / len(cuts))
        return jnp.repeat(jnp.exp(draws), dims[dim] // parts).reshape((-1,) + (1,) * (len(dims) - dim - 1))

    factor_of = one(*cuts[0])
    for cut in cuts[1:]:
        factor_of = factor_of * one(*cut)
    return factor_of


def centred(own_key, shape, scale, limit, shards=(), held_as=jnp.bfloat16):
    factor_of = level_of(own_key, shape, shards, -0.22, 0.18) if shards else 1.0
    drawn = jax.random.normal(own_key, shape, jnp.float32) * scale * factor_of
    return jnp.minimum(jnp.maximum(drawn, -limit), limit).astype(held_as)


def setup_inputs(seed: int = 0) -> dict:
    keys = jax.random.split(jax.random.key(seed), 18)
    return {
        "inputs": centred(keys[0], (MICRO, SLOTS, D), 1.0, 6.0, ((1, 32),)),
        "cotangent": centred(keys[1], (MICRO, SLOTS, D), 1.0, 6.0, ((1, 32),)),
        "w_qkv": centred(keys[2], (D, 3 * D), D ** -0.5, 0.3125, ((0, 32),)),
        "w_out": centred(keys[3], (D, D), (D // 8) ** -0.5, 0.875, ((0, 32),)),
        "w_fc1": centred(keys[4], (D, FF), D ** -0.5, 0.3125, ((0, 32),)),
        "w_fc2": centred(keys[5], (FF, D), FF ** -0.5, 0.15625, ((0, 32),)),
        "norm1_gain": jnp.clip(1.0 + 0.1 * jax.random.normal(keys[6], (D,), jnp.float32), 0.5, 1.5).astype(jnp.bfloat16),
        "norm1_bias": centred(keys[7], (D,), 0.3, 4.0, ((0, 32),)),
        "query_bias": centred(keys[8], (D,), 0.5, 6.0, ((0, 32),)),
        "value_bias": centred(keys[9], (D,), 0.5, 6.0, ((0, 32),)),
        "out_bias": centred(keys[10], (D,), 0.3, 4.0, ((0, 32),)),
        "norm2_gain": jnp.clip(1.0 + 0.1 * jax.random.normal(keys[11], (D,), jnp.float32), 0.5, 1.5).astype(jnp.bfloat16),
        "norm2_bias": centred(keys[12], (D,), 0.3, 4.0, ((0, 32),)),
        "fc1_bias": centred(keys[13], (FF,), 0.5, 6.0, ((0, 32),)),
        "fc2_bias": centred(keys[14], (D,), 0.3, 4.0, ((0, 32),)),
        "image_tokens": draw_image_tokens(jax.random.fold_in(keys[17], 71), 0),
        "image_count": draw_image_count(jax.random.fold_in(keys[17], 71), 0),
    }


norm_eps = 1e-06
masked_score = -1000000000.0

@jax.custom_vjp
def low(v):
    return lax.optimization_barrier(v.astype(jnp.bfloat16)).astype(jnp.float32)

@jax.custom_vjp
def low_back(v):
    return v

def low_keep(v):
    return (low(v), None)

def low_pass(kept, grad):
    return (grad,)

def back_keep(v):
    return (v, None)

def back_low(kept, grad):
    return (low(grad),)
low.defvjp(low_keep, low_pass)
low_back.defvjp(back_keep, back_low)

def normalize(values, gain, shift):
    center = lax.optimization_barrier(jnp.mean(values, axis=-1, keepdims=True))
    offset = values - center
    spread = lax.optimization_barrier(jnp.mean(offset * offset, axis=-1, keepdims=True))
    return offset * lax.rsqrt(spread + norm_eps) * gain + shift

def product(left, right):
    return jnp.dot(left, right, precision=lax.Precision.HIGHEST)

def segments(length, count, row_count):
    places = jnp.arange(row_count, dtype=jnp.int32)
    image_of = (places // length).astype(jnp.int32)
    valid = image_of < count
    return (jnp.where(valid, image_of, row_count + places).astype(jnp.int32), valid)

def layer_forward(parameters, states, segment_ids, valid):
    w_qkv, w_out, w_fc1, w_fc2, norm1_gain, norm1_bias, query_bias, value_bias, out_bias, norm2_gain, norm2_bias, fc1_bias, fc2_bias = parameters
    row_count = states.shape[0]
    width = states.shape[1]
    head_dim = width // HEADS
    scale = head_dim ** (-0.5)
    normed = low(normalize(states, norm1_gain, norm1_bias))
    qkv_bias = jnp.concatenate([query_bias, jnp.zeros_like(query_bias), value_bias])
    qkv = low_back(low(product(normed, w_qkv) + qkv_bias)).reshape(row_count, 3, HEADS, head_dim)
    scores = jnp.einsum('qhd,khd->hqk', qkv[:, 0], qkv[:, 1], precision=lax.Precision.HIGHEST) * scale
    scores = low_back(scores)
    same_image = segment_ids[:, None] == segment_ids[None, :]
    weights = jax.nn.softmax(jnp.where(same_image[None], scores, masked_score), axis=-1)
    attended = jnp.einsum('hqk,khd->qhd', low(weights), qkv[:, 2], precision=lax.Precision.HIGHEST)
    attended = low_back(low(attended.reshape(row_count, width)))
    branch = low_back(product(attended, w_out) + out_bias)
    mixed = states + branch
    normed_two = low(normalize(mixed, norm2_gain, norm2_bias))
    pre_act = low_back(product(normed_two, w_fc1) + fc1_bias)
    activated = low(jax.nn.gelu(pre_act, approximate=False))
    final = mixed + low_back(product(activated, w_fc2) + fc2_bias)
    return jnp.where(valid[:, None], final, 0.0)

def reference(inputs, cotangent, w_qkv, w_out, w_fc1, w_fc2, norm1_gain, norm1_bias, query_bias, value_bias, out_bias, norm2_gain, norm2_bias, fc1_bias, fc2_bias, image_tokens, image_count):
    parameters = tuple((weight_item.astype(jnp.float32) for weight_item in (w_qkv, w_out, w_fc1, w_fc2, norm1_gain, norm1_bias, query_bias, value_bias, out_bias, norm2_gain, norm2_bias, fc1_bias, fc2_bias)))
    width = inputs.shape[2]
    blocks = inputs.astype(jnp.float32).reshape(MICRO * N_DP, ROWS, width)
    grad_blocks = cotangent.astype(jnp.float32).reshape(MICRO * N_DP, ROWS, width)
    lengths = image_tokens.reshape(MICRO * N_DP).astype(jnp.int32)
    counts = image_count.reshape(MICRO * N_DP).astype(jnp.int32)

    def one_block(running, block_item):
        states, grad_states, length, count = block_item
        segment_ids, valid = segments(length, count, ROWS)

        def apply_layer(params_in, states_in):
            return layer_forward(params_in, states_in, segment_ids, valid)
        result, pull_back = jax.vjp(apply_layer, parameters, states)
        grad_params, grad_rows = pull_back(grad_states)
        running = jax.tree.map(jnp.add, running, grad_params)
        return (running, (result.astype(jnp.bfloat16), grad_rows.astype(jnp.bfloat16)))
    start_sums = jax.tree.map(jnp.zeros_like, parameters)
    summed, (results, grad_rows) = lax.scan(one_block, start_sums, (blocks, grad_blocks, lengths, counts))
    outputs = results.reshape(MICRO, N_DP * ROWS, width)
    input_grad = grad_rows.reshape(MICRO, N_DP * ROWS, width)
    return (outputs, input_grad, summed[0], summed[1], summed[2], summed[3], summed[4], summed[5], summed[6], summed[7], summed[8], summed[9], summed[10], summed[11], summed[12])
```

```python
import functools
import jax
import jax.numpy as jnp
from jax import lax
from jax.experimental import pallas as pl
from jax.experimental.pallas import tpu as pltpu

F32, BF16 = jnp.float32, jnp.bfloat16
HEADS = 6
EPS = 1e-06
FAR = -1e30
V_GAIN1, V_SHIFT1, V_QKV, V_OUT, V_GAIN2, V_SHIFT2, V_FC1, V_FC2 = range(8)
G_GAIN1, G_SHIFT1, G_QKV, G_OUT, G_GAIN2, G_SHIFT2, G_FC1, G_FC2 = range(8)


def mm(a, b):
    return jnp.dot(a, b, preferred_element_type=F32)

def mm_t(a, b):
    return lax.dot_general(a, b, (((1,), (1,)), ((), ())), preferred_element_type=F32)

def t_mm(a, b):
    return lax.dot_general(a, b, (((0,), (0,)), ((), ())), preferred_element_type=F32)


def norm_rows(v):
    width = v.shape[1]
    off = v - jnp.sum(v, axis=1, keepdims=True) * (1.0 / width)
    inv = lax.rsqrt(jnp.sum(off * off, axis=1, keepdims=True) * (1.0 / width) + EPS)
    return off * inv, inv


def norm_back(n, inv, t):
    width = n.shape[1]
    a = jnp.sum(t, axis=1, keepdims=True) * (1.0 / width)
    b = jnp.sum(t * n, axis=1, keepdims=True) * (1.0 / width)
    return inv * (t - a - n * b)


def col_sum(v):
    return jnp.sum(v, axis=0, keepdims=True)


def window(meta, m, w, group, wq, wk, rows):
    length, count = meta[m, 0], meta[m, 1]
    lo = w * (length * group)
    hi = jnp.minimum(lo + length * group, length * count)
    base = (lo // 16) * 16
    sq = pl.multiple_of(jnp.minimum(base, rows - wq), 16)
    sk = pl.multiple_of(jnp.minimum(base, rows - wk), 16)
    return lo, hi, length, sq, sk


def seg_of(start, n, lo, hi, length):
    r = start + lax.broadcasted_iota(jnp.int32, (n, 128), 0)
    inside = jnp.logical_and(r >= lo, r < hi)
    return inside, jnp.where(inside, jnp.where(r >= lo + length, 1, 0), 2)


def halves(v):
    left = lax.broadcasted_iota(jnp.int32, v.shape, 1) < 64
    zero = jnp.zeros_like(v)
    return jnp.where(left, v, zero), jnp.where(left, zero, v)


def attend_fwd(meta, m, qkv_s, o_s, inv_s, e_s, group, wq, wk, pairs, width):
    rows = qkv_s.shape[0]
    scale = 0.125 * 1.4426950408889634

    def one(w, carry):
        lo, hi, length, sq, sk = window(meta, m, w, group, wq, wk, rows)
        in_q, seg_q = seg_of(sq, wq, lo, hi, length)
        _, seg_k = seg_of(sk, wk, lo, hi, length)
        lane_q = lax.broadcasted_iota(jnp.int32, (wq, 128), 1)
        lane_k = lax.broadcasted_iota(jnp.int32, (wk, 128), 1)
        aug_q = jnp.where(jnp.logical_and(lane_q != seg_q, lane_q < 3), 1.0, 0.0).astype(BF16)
        aug_k = jnp.where(lane_k == seg_k, FAR, 0.0).astype(BF16)
        ones0 = jnp.where(lane_k < 64, 1.0, 0.0).astype(BF16)
        ones1 = jnp.where(lane_k < 64, 0.0, 1.0).astype(BF16)
        for p in range(pairs):
            c = 128 * p
            q2 = qkv_s[pl.ds(sq, wq), c : c + 128]
            k0, k1 = halves(qkv_s[pl.ds(sk, wk), width + c : width + c + 128])
            v0, v1 = halves(qkv_s[pl.ds(sk, wk), 2 * width + c : 2 * width + c + 128])
            left = jnp.concatenate([q2, aug_q], axis=1)
            right = jnp.concatenate(
                [jnp.concatenate([k0, aug_k], axis=1), jnp.concatenate([k1, aug_k], axis=1)], axis=0
            )
            s = mm_t(left, right)
            parts = []
            for h in range(2):
                sh = s[:, h * wk : (h + 1) * wk]
                top = jnp.max(sh, axis=1, keepdims=True)
                parts.append(jnp.exp2((sh - top) * scale).astype(BF16))
            e = jnp.concatenate(parts, axis=1)
            e_s[w * pairs + p] = e
            vals = jnp.concatenate(
                [jnp.concatenate([v0, ones0], axis=1), jnp.concatenate([v1, ones1], axis=1)], axis=0
            )
            both = mm(e, vals)
            inv = 1.0 / both[:, 128:]
            o = (both[:, :128] * inv).astype(BF16)
            dst = (pl.ds(sq, wq), pl.ds(c, 128))
            o_s[dst] = jnp.where(in_q, o, o_s[dst])
            inv_s[dst] = jnp.where(in_q, inv, inv_s[dst])
        return carry

    lax.fori_loop(0, (meta[m, 1] + group - 1) // group, one, 0)


def attend_bwd(meta, m, qkv_s, o_s, inv_s, e_s, go_s, gqkv_s, group, wq, wk, pairs, width):
    rows = qkv_s.shape[0]

    def one(w, carry):
        lo, hi, length, sq, sk = window(meta, m, w, group, wq, wk, rows)
        in_q, _ = seg_of(sq, wq, lo, hi, length)
        in_k, _ = seg_of(sk, wk, lo, hi, length)
        for p in range(pairs):
            c = 128 * p
            e = e_s[w * pairs + p]
            q0, q1 = halves(qkv_s[pl.ds(sq, wq), c : c + 128])
            k0, k1 = halves(qkv_s[pl.ds(sk, wk), width + c : width + c + 128])
            v0, v1 = halves(qkv_s[pl.ds(sk, wk), 2 * width + c : 2 * width + c + 128])
            dst_q = (pl.ds(sq, wq), pl.ds(c, 128))
            go = (go_s[dst_q].astype(F32) * inv_s[dst_q]).astype(BF16)
            prod0, prod1 = halves(go.astype(F32) * o_s[dst_q].astype(F32))
            d = (jnp.sum(prod0, axis=1, keepdims=True), jnp.sum(prod1, axis=1, keepdims=True))
            gp = mm_t(go, jnp.concatenate([v0, v1], axis=0))
            gs = []
            for h in range(2):
                sl = slice(h * wk, (h + 1) * wk)
                gs.append((e[:, sl].astype(F32) * (gp[:, sl] - d[h])).astype(BF16))
            gq = mm(jnp.concatenate(gs, axis=1), jnp.concatenate([k0, k1], axis=0)) * 0.125
            gk = t_mm(jnp.concatenate(gs, axis=0), jnp.concatenate([q0, q1], axis=0)) * 0.125
            gv = t_mm(
                jnp.concatenate([e[:, :wk], e[:, wk:]], axis=0), jnp.concatenate(halves(go), axis=0)
            )
            gqkv_s[dst_q] = jnp.where(in_q, gq.astype(BF16), gqkv_s[dst_q])
            dst_k = (pl.ds(sk, wk), pl.ds(width + c, 128))
            gqkv_s[dst_k] = jnp.where(in_k, gk.astype(BF16), gqkv_s[dst_k])
            dst_v = (pl.ds(sk, wk), pl.ds(2 * width + c, 128))
            gqkv_s[dst_v] = jnp.where(in_k, gv.astype(BF16), gqkv_s[dst_v])
        return carry

    lax.fori_loop(0, (meta[m, 1] + group - 1) // group, one, 0)


WIDE = (1, 352, 384)
NARROW1 = (1, 224, 256)
NARROW2 = (2, 224, 256)


def layer_kernel(
    meta, x_ref, cot_ref, wqkv, wout, w1, w2, vec,
    out_ref, ig_ref, a_qkv, a_out, a_fc1, a_fc2, a_vec,
    h1_s, qkv_s, o_s, inv_s, e1_s, e2_s, h2_s, act_s, gpre_s, gy_s, gb_s, go_s, gmix_s, gqkv_s,
    phases=("p1", "af", "mlp", "wg", "ab", "p5"), tile=512, chunk=384,
):
    m = pl.program_id(0)
    rows, width = x_ref.shape[1], x_ref.shape[2]
    hidden = w1.shape[1]
    pairs = HEADS // 2
    length, count = meta[m, 0], meta[m, 1]
    total = length * count

    @pl.when(m == 0)
    def _():
        for ref in (a_qkv, a_out, a_fc1, a_fc2, a_vec):
            ref[...] = jnp.zeros_like(ref)

    def v(i, n=width):
        return vec[i : i + 1, 0:n]

    def add_vec(i, val):
        a_vec[i : i + 1, 0 : val.shape[1]] += val

    if "p1" in phases:
        def p1(i, c):
            r = pl.ds(pl.multiple_of(i * tile, tile), tile)
            n1, _ = norm_rows(x_ref[0, r, :].astype(F32))
            h1 = (n1 * v(V_GAIN1) + v(V_SHIFT1)).astype(BF16)
            h1_s[r, :] = h1
            qkv_s[r, :] = (mm(h1, wqkv[...]) + v(V_QKV, 3 * width)).astype(BF16)
            return c
        lax.fori_loop(0, rows // tile, p1, 0)

    o_s[...] = qkv_s[:, 2 * width :]

    if "af" in phases:
        fwd = functools.partial(attend_fwd, meta, m, qkv_s, o_s, inv_s)
        @pl.when(length > 256)
        def _():
            fwd(e1_s, *WIDE, pairs, width)
        @pl.when(jnp.logical_and(length <= 256, length > 128))
        def _():
            fwd(e2_s, *NARROW1, pairs, width)
        @pl.when(length <= 128)
        def _():
            fwd(e2_s, *NARROW2, pairs, width)

    if "mlp" in phases:
        def mlp(i, c):
            r = pl.ds(pl.multiple_of(i * tile, tile), tile)
            valid = (i * tile + lax.broadcasted_iota(jnp.int32, (tile, 1), 0)) < total
            mixed = x_ref[0, r, :].astype(F32) + mm(o_s[r, :], wout[...]) + v(V_OUT)
            n2, r2 = norm_rows(mixed)
            h2 = (n2 * v(V_GAIN2) + v(V_SHIFT2)).astype(BF16)
            h2_s[r, :] = h2
            gy = jnp.where(valid, cot_ref[0, r, :].astype(F32), 0.0)
            gyl = gy.astype(BF16)
            gy_s[r, :] = gyl
            add_vec(G_FC2, col_sum(gy))
            for f in range(0, hidden, chunk):
                fs = slice(f, f + chunk)
                pre = mm(h2, w1[:, fs]) + vec[V_FC1 : V_FC1 + 1, fs]
                cdf = 0.5 * lax.erf(pre * 0.7071067811865476) + 0.5
                act_s[r, fs] = (pre * cdf).astype(BF16)
                slope = cdf + pre * (jnp.exp(pre * pre * -0.5) * 0.3989422804014327)
                gpre = (slope * mm_t(gyl, w2[fs, :])).astype(BF16)
                gpre_s[r, fs] = gpre
                a_vec[G_FC1 : G_FC1 + 1, fs] += col_sum(gpre.astype(F32))
            final = mixed + mm(act_s[r, :], w2[...]) + v(V_FC2)
            out_ref[0, r, :] = jnp.where(valid, final, 0.0).astype(BF16)
            gh2 = mm_t(gpre_s[r, :], w1[...])
            add_vec(G_GAIN2, col_sum(gh2 * n2))
            add_vec(G_SHIFT2, col_sum(gh2))
            gmix = gy + norm_back(n2, r2, gh2 * v(V_GAIN2))
            gmix_s[r, :] = gmix
            gb = gmix.astype(BF16)
            gb_s[r, :] = gb
            add_vec(G_OUT, col_sum(gb.astype(F32)))
            go_s[r, :] = mm_t(gb, wout[...]).astype(BF16)
            return c
        lax.fori_loop(0, rows // tile, mlp, 0)

    if "wg" in phases:
        a_fc1[...] += t_mm(h2_s[...], gpre_s[...])
        a_fc2[...] += t_mm(act_s[...], gy_s[...])
        a_out[...] += t_mm(o_s[...], gb_s[...])

    gqkv_s[:, : 2 * width] = jnp.zeros((rows, 2 * width), BF16)
    gqkv_s[:, 2 * width :] = go_s[...]

    if "ab" in phases:
        bwd = functools.partial(attend_bwd, meta, m, qkv_s, o_s, inv_s)
        @pl.when(length > 256)
        def _():
            bwd(e1_s, go_s, gqkv_s, *WIDE, pairs, width)
        @pl.when(jnp.logical_and(length <= 256, length > 128))
        def _():
            bwd(e2_s, go_s, gqkv_s, *NARROW1, pairs, width)
        @pl.when(length <= 128)
        def _():
            bwd(e2_s, go_s, gqkv_s, *NARROW2, pairs, width)

    if "p5" in phases:
        def p5(i, c):
            r = pl.ds(pl.multiple_of(i * tile, tile), tile)
            gqkv = gqkv_s[r, :]
            gh1 = mm_t(gqkv, wqkv[...])
            n1, r1 = norm_rows(x_ref[0, r, :].astype(F32))
            add_vec(G_QKV, col_sum(gqkv.astype(F32)))
            add_vec(G_GAIN1, col_sum(gh1 * n1))
            add_vec(G_SHIFT1, col_sum(gh1))
            ig_ref[0, r, :] = (gmix_s[r, :] + norm_back(n1, r1, gh1 * v(V_GAIN1))).astype(BF16)
            return c
        lax.fori_loop(0, rows // tile, p5, 0)
        a_qkv[...] += t_mm(h1_s[...], gqkv_s[...])


def layer_call(meta, x, cot, wqkv, wout, w1, w2, vec, **kw):
    micro, rows, width = x.shape
    hidden = w1.shape[1]
    row_block = pl.BlockSpec((1, rows, width), lambda m: (m, 0, 0))
    def whole(a):
        return pl.BlockSpec(a.shape, lambda m: (0, 0), pipeline_mode=pl.Buffered(1))
    def kept(shape):
        return pl.BlockSpec(shape, lambda m: (0, 0), pipeline_mode=pl.Buffered(1))
    grads = [wqkv.shape, wout.shape, w1.shape, w2.shape, vec.shape]
    bf = lambda n: pltpu.VMEM((rows, n), BF16)
    return pl.pallas_call(
        functools.partial(layer_kernel, **kw),
        grid=(micro,),
        in_specs=[pl.BlockSpec(memory_space=pltpu.SMEM), row_block, row_block]
        + [whole(a) for a in (wqkv, wout, w1, w2, vec)],
        out_specs=[row_block, row_block] + [kept(s) for s in grads],
        out_shape=[jax.ShapeDtypeStruct(x.shape, BF16)] * 2 + [jax.ShapeDtypeStruct(s, F32) for s in grads],
        scratch_shapes=[
            bf(width), bf(3 * width), bf(width), pltpu.VMEM((rows, width), F32),
            pltpu.VMEM((9, 352, 768), BF16), pltpu.VMEM((15, 224, 512), BF16),
            bf(width), bf(hidden), bf(hidden), bf(width), bf(width), bf(width),
            pltpu.VMEM((rows, width), F32), bf(3 * width),
        ],
        compiler_params=pltpu.CompilerParams(vmem_limit_bytes=63 * 2**20),
    )(meta, x, cot, wqkv, wout, w1, w2, vec)


def body(inputs, cotangent, w_qkv, w_out, w_fc1, w_fc2, gain1, shift1, q_bias, v_bias, out_bias, gain2, shift2,
         fc1_bias, fc2_bias, image_tokens, image_count):
    j = lax.axis_index("dp")
    n = lax.axis_size("dp")
    width = w_qkv.shape[1] // 3
    hidden = w_fc1.shape[1]
    gather = functools.partial(lax.all_gather, axis_name="dp", axis=0, tiled=True)
    mats = [gather(w) for w in (w_qkv, w_out, w_fc1, w_fc2)]
    small = (gain1, shift1, q_bias, v_bias, out_bias, gain2, shift2, fc2_bias)
    packed = jnp.concatenate([jnp.stack(small).reshape(-1), fc1_bias])[None]
    packed = gather(packed).astype(F32)
    part = width // n
    cols = [packed[:, i * part : (i + 1) * part].reshape(-1) for i in range(8)]
    fc1_full = packed[:, 8 * part :].reshape(-1)
    pad = lambda a: jnp.pad(a, (0, hidden - a.shape[0]))
    qkv_bias = jnp.concatenate([cols[2], jnp.zeros_like(cols[2]), cols[3]])
    vec = jnp.stack([pad(cols[0]), pad(cols[1]), pad(qkv_bias), pad(cols[4]), pad(cols[5]), pad(cols[6]), fc1_full, pad(cols[7])])
    meta = jnp.stack([image_tokens[:, j], image_count[:, j]], axis=1)
    out, ig, g_qkv, g_out, g_fc1, g_fc2, g_vec = layer_call(meta, inputs, cotangent, *mats, vec)
    scatter = functools.partial(lax.psum_scatter, axis_name="dp", scatter_dimension=0, tiled=True)
    grads = [scatter(g) for g in (g_qkv, g_out, g_fc1, g_fc2)]
    own = [g_vec[0, :width], g_vec[1, :width], g_vec[2, :width], g_vec[2, 2 * width : 3 * width], g_vec[3, :width],
           g_vec[4, :width], g_vec[5, :width], g_vec[7, :width]]
    rows = jnp.concatenate([o.reshape(n, part) for o in own] + [g_vec[6].reshape(n, -1)], axis=1)
    mine = scatter(rows)[0]
    vs = [mine[i * part : (i + 1) * part] for i in range(8)]
    return (out, ig, *grads, vs[0], vs[1], vs[2], vs[3], vs[4], vs[5], vs[6], mine[8 * part :], vs[7])


def solution(mesh):
    from jax.sharding import PartitionSpec as P
    big, mat, one = P(None, "dp", None), P("dp", None), P("dp")
    return jax.shard_map(
        body, mesh=mesh,
        in_specs=(big, big) + (mat,) * 4 + (one,) * 9 + (P(), P()),
        out_specs=(big, big) + (mat,) * 4 + (one,) * 9,
        check_vma=False,
    )
```

```python
import functools

import jax
import jax.numpy as jnp
from jax import lax
from jax.experimental import pallas as pl
from jax.experimental.pallas import tpu as pltpu
from jax.sharding import PartitionSpec as P

F32, BF16 = jnp.float32, jnp.bfloat16
MESH = pl.DeviceIdType.MESH

HEADS = 6
EPS = 1e-06
FAR = -1e30
V_GAIN1, V_SHIFT1, V_QKV, V_OUT, V_GAIN2, V_SHIFT2, V_FC1, V_FC2 = range(8)
G_GAIN1, G_SHIFT1, G_QKV, G_OUT, G_GAIN2, G_SHIFT2, G_FC1, G_FC2 = range(8)


def mm(a, b):
    return jnp.dot(a, b, preferred_element_type=F32)

def mm_t(a, b):
    return lax.dot_general(a, b, (((1,), (1,)), ((), ())), preferred_element_type=F32)

def t_mm(a, b):
    return lax.dot_general(a, b, (((0,), (0,)), ((), ())), preferred_element_type=F32)


def norm_rows(v):
    width = v.shape[1]
    off = v - jnp.sum(v, axis=1, keepdims=True) * (1.0 / width)
    inv = lax.rsqrt(jnp.sum(off * off, axis=1, keepdims=True) * (1.0 / width) + EPS)
    return off * inv, inv


def norm_back(n, inv, t):
    width = n.shape[1]
    a = jnp.sum(t, axis=1, keepdims=True) * (1.0 / width)
    b = jnp.sum(t * n, axis=1, keepdims=True) * (1.0 / width)
    return inv * (t - a - n * b)


def col_sum(v):
    return jnp.sum(v, axis=0, keepdims=True)


def window(meta, m, w, group, wq, wk, rows):
    length, count = meta[m, 0], meta[m, 1]
    lo = w * (length * group)
    hi = jnp.minimum(lo + length * group, length * count)
    base = (lo // 16) * 16
    sq = pl.multiple_of(jnp.minimum(base, rows - wq), 16)
    sk = pl.multiple_of(jnp.minimum(base, rows - wk), 16)
    return lo, hi, length, sq, sk


def seg_of(start, n, lo, hi, length):
    r = start + lax.broadcasted_iota(jnp.int32, (n, 128), 0)
    inside = jnp.logical_and(r >= lo, r < hi)
    return inside, jnp.where(inside, jnp.where(r >= lo + length, 1, 0), 2)


def halves(v):
    left = lax.broadcasted_iota(jnp.int32, v.shape, 1) < 64
    zero = jnp.zeros_like(v)
    return jnp.where(left, v, zero), jnp.where(left, zero, v)


def attend_fwd(meta, m, qkv_s, o_s, inv_s, e_s, group, wq, wk, pairs, width):
    rows = qkv_s.shape[0]
    scale = 0.125 * 1.4426950408889634

    def one(w, carry):
        lo, hi, length, sq, sk = window(meta, m, w, group, wq, wk, rows)
        in_q, seg_q = seg_of(sq, wq, lo, hi, length)
        _, seg_k = seg_of(sk, wk, lo, hi, length)
        lane_q = lax.broadcasted_iota(jnp.int32, (wq, 128), 1)
        lane_k = lax.broadcasted_iota(jnp.int32, (wk, 128), 1)
        aug_q = jnp.where(jnp.logical_and(lane_q != seg_q, lane_q < 3), 1.0, 0.0).astype(BF16)
        aug_k = jnp.where(lane_k == seg_k, FAR, 0.0).astype(BF16)
        ones0 = jnp.where(lane_k < 64, 1.0, 0.0).astype(BF16)
        ones1 = jnp.where(lane_k < 64, 0.0, 1.0).astype(BF16)
        for p in range(pairs):
            c = 128 * p
            q2 = qkv_s[pl.ds(sq, wq), c : c + 128]
            k0, k1 = halves(qkv_s[pl.ds(sk, wk), width + c : width + c + 128])
            v0, v1 = halves(qkv_s[pl.ds(sk, wk), 2 * width + c : 2 * width + c + 128])
            left = jnp.concatenate([q2, aug_q], axis=1)
            right = jnp.concatenate(
                [jnp.concatenate([k0, aug_k], axis=1), jnp.concatenate([k1, aug_k], axis=1)], axis=0
            )
            s = mm_t(left, right)
            parts = []
            for h in range(2):
                sh = s[:, h * wk : (h + 1) * wk]
                top = jnp.max(sh, axis=1, keepdims=True)
                parts.append(jnp.exp2((sh - top) * scale).astype(BF16))
            e = jnp.concatenate(parts, axis=1)
            e_s[w * pairs + p] = e
            vals = jnp.concatenate(
                [jnp.concatenate([v0, ones0], axis=1), jnp.concatenate([v1, ones1], axis=1)], axis=0
            )
            both = mm(e, vals)
            inv = 1.0 / both[:, 128:]
            o = (both[:, :128] * inv).astype(BF16)
            dst = (pl.ds(sq, wq), pl.ds(c, 128))
            o_s[dst] = jnp.where(in_q, o, o_s[dst])
            inv_s[dst] = jnp.where(in_q, inv, inv_s[dst])
        return carry

    lax.fori_loop(0, (meta[m, 1] + group - 1) // group, one, 0)


def attend_bwd(meta, m, qkv_s, o_s, inv_s, e_s, go_s, gqkv_s, group, wq, wk, pairs, width):
    rows = qkv_s.shape[0]

    def one(w, carry):
        lo, hi, length, sq, sk = window(meta, m, w, group, wq, wk, rows)
        in_q, _ = seg_of(sq, wq, lo, hi, length)
        in_k, _ = seg_of(sk, wk, lo, hi, length)
        for p in range(pairs):
            c = 128 * p
            e = e_s[w * pairs + p]
            q0, q1 = halves(qkv_s[pl.ds(sq, wq), c : c + 128])
            k0, k1 = halves(qkv_s[pl.ds(sk, wk), width + c : width + c + 128])
            v0, v1 = halves(qkv_s[pl.ds(sk, wk), 2 * width + c : 2 * width + c + 128])
            dst_q = (pl.ds(sq, wq), pl.ds(c, 128))
            go = (go_s[dst_q].astype(F32) * inv_s[dst_q]).astype(BF16)
            prod0, prod1 = halves(go.astype(F32) * o_s[dst_q].astype(F32))
            d = (jnp.sum(prod0, axis=1, keepdims=True), jnp.sum(prod1, axis=1, keepdims=True))
            gp = mm_t(go, jnp.concatenate([v0, v1], axis=0))
            gs = []
            for h in range(2):
                sl = slice(h * wk, (h + 1) * wk)
                gs.append((e[:, sl].astype(F32) * (gp[:, sl] - d[h])).astype(BF16))
            gq = mm(jnp.concatenate(gs, axis=1), jnp.concatenate([k0, k1], axis=0)) * 0.125
            gk = t_mm(jnp.concatenate(gs, axis=0), jnp.concatenate([q0, q1], axis=0)) * 0.125
            gv = t_mm(
                jnp.concatenate([e[:, :wk], e[:, wk:]], axis=0), jnp.concatenate(halves(go), axis=0)
            )
            gqkv_s[dst_q] = jnp.where(in_q, gq.astype(BF16), gqkv_s[dst_q])
            dst_k = (pl.ds(sk, wk), pl.ds(width + c, 128))
            gqkv_s[dst_k] = jnp.where(in_k, gk.astype(BF16), gqkv_s[dst_k])
            dst_v = (pl.ds(sk, wk), pl.ds(2 * width + c, 128))
            gqkv_s[dst_v] = jnp.where(in_k, gv.astype(BF16), gqkv_s[dst_v])
        return carry

    lax.fori_loop(0, (meta[m, 1] + group - 1) // group, one, 0)


WIDE = (1, 352, 384)
NARROW1 = (1, 224, 256)
NARROW2 = (2, 224, 256)


def fold_matrix(part, count, high):
    rows, cols = 4 * count * part, count * high
    r = lax.broadcasted_iota(jnp.int32, (rows, cols), 0).astype(F32)
    c = lax.broadcasted_iota(jnp.int32, (rows, cols), 1).astype(F32)
    block = jnp.floor((c + 0.5) * (1.0 / high))
    inner = c - block * high
    piece = jnp.floor((inner + 0.5) * (1.0 / part))
    want = piece * (count * part) + block * part + (inner - piece * part)
    return jnp.where(jnp.logical_and(want == r, piece < 4), 1.0, 0.0).astype(BF16)


def unfold(src, dsts, part):
    width = dsts[0].shape[0]
    n = width // part
    high = src.shape[0] // n
    count = 96 // part
    pick = fold_matrix(part, count, high)
    for t in range(n // count):
        full = mm(pick, src[t * count * high : (t + 1) * count * high, :]).astype(BF16)
        for a in range(4):
            dsts[a][96 * t : 96 * (t + 1), :] = full[96 * a : 96 * (a + 1), :]


def fold(srcs, dst, part):
    width = srcs[0].shape[0]
    n = width // part
    high = dst.shape[0] // n
    count = 96 // part
    pick = fold_matrix(part, count, high)
    for t in range(n // count):
        rows = slice(96 * t, 96 * (t + 1))
        four = jnp.concatenate([s[rows, :].astype(BF16) for s in srcs], axis=0)
        dst[t * count * high : (t + 1) * count * high, :] = t_mm(pick, four).astype(BF16)


def unfold_vectors(src, vec, part):
    n = src.shape[0]
    width = part * n
    lane = lax.broadcasted_iota(jnp.int32, (8, 128), 1)
    total = jnp.zeros((8, width), F32)
    wide = jnp.zeros((8, 4 * width), F32)
    for j in range(n):
        one = jnp.where(lane < part, src[j, 0:8, :], 0.0)
        one = jnp.concatenate([one, jnp.zeros((8, width - 128), F32)], axis=1)
        total = total + pltpu.roll(one, j * part, 1)
        one = jnp.where(lane < 4 * part, src[j, 8:16, :], 0.0)
        one = jnp.concatenate([one, jnp.zeros((8, 4 * width - 128), F32)], axis=1)
        wide = wide + pltpu.roll(one, 4 * j * part, 1)
    vec[...] = jnp.zeros_like(vec)
    for i, (row, col) in enumerate(VECTORS):
        vec[row : row + 1, col * width : (col + 1) * width] = total[i : i + 1]
    vec[V_FC1 : V_FC1 + 1, :] = wide[0:1]


def fold_vectors(vec, dst, part):
    n = dst.shape[0]
    width = part * n
    eight = jnp.concatenate(
        [vec[row : row + 1, col * width : (col + 1) * width] for row, col in VECTORS], axis=0
    )
    wide = jnp.broadcast_to(vec[V_FC1 : V_FC1 + 1, :], (8, 4 * width))
    for j in range(n):
        dst[j, 0:8, :] = pltpu.roll(eight, (width - j * part) % width, 1)[:, :128]
        dst[j, 8:16, :] = pltpu.roll(wide, (4 * width - 4 * j * part) % (4 * width), 1)[:, :128]


VECTORS = ((V_GAIN1, 0), (V_SHIFT1, 0), (V_QKV, 0), (V_QKV, 2), (V_OUT, 0), (V_GAIN2, 0), (V_SHIFT2, 0), (V_FC2, 0))


def layer_kernel(
    meta, x_ref, cot_ref, g_attn, g_fc1, w2, g_vec,
    out_ref, ig_ref, p_attn, p_fc1, p_fc2, p_vec,
    wqkv, wout, w1, vec, a_qkv, a_out, a_fc1, a_fc2, a_vec, h1_s, qkv_s, o_s, inv_s, e1_s, e2_s, h2_s, act_s, gpre_s, gy_s, gb_s, go_s, gmix_s, gqkv_s,
    phases=("p1", "af", "mlp", "wg", "ab", "p5"), tile=512, chunk=384,
):
    m = pl.program_id(0)
    rows, width = x_ref.shape[1], x_ref.shape[2]
    hidden = w1.shape[1]
    pairs = HEADS // 2
    length, count = meta[m, 0], meta[m, 1]
    total = length * count
    part = width // g_vec.shape[0]

    @pl.when(m == 0)
    def _():
        unfold(g_attn, [wqkv.at[:, 0:width], wqkv.at[:, width : 2 * width], wqkv.at[:, 2 * width :], wout], part)
        unfold(g_fc1, [w1.at[:, i * width : (i + 1) * width] for i in range(4)], part)
        unfold_vectors(g_vec, vec, part)
        for ref in (a_qkv, a_out, a_fc1, a_fc2, a_vec):
            ref[...] = jnp.zeros_like(ref)

    def v(i, n=width):
        return vec[i : i + 1, 0:n]

    def add_vec(i, val):
        a_vec[i : i + 1, 0 : val.shape[1]] += val

    if "p1" in phases:
        def p1(i, c):
            r = pl.ds(pl.multiple_of(i * tile, tile), tile)
            n1, _ = norm_rows(x_ref[0, r, :].astype(F32))
            h1 = (n1 * v(V_GAIN1) + v(V_SHIFT1)).astype(BF16)
            h1_s[r, :] = h1
            qkv_s[r, :] = (mm(h1, wqkv[...]) + v(V_QKV, 3 * width)).astype(BF16)
            return c
        lax.fori_loop(0, rows // tile, p1, 0)

    o_s[...] = qkv_s[:, 2 * width :]

    if "af" in phases:
        fwd = functools.partial(attend_fwd, meta, m, qkv_s, o_s, inv_s)
        @pl.when(length > 256)
        def _():
            fwd(e1_s, *WIDE, pairs, width)
        @pl.when(jnp.logical_and(length <= 256, length > 128))
        def _():
            fwd(e2_s, *NARROW1, pairs, width)
        @pl.when(length <= 128)
        def _():
            fwd(e2_s, *NARROW2, pairs, width)

    if "mlp" in phases:
        def mlp(i, c):
            r = pl.ds(pl.multiple_of(i * tile, tile), tile)
            valid = (i * tile + lax.broadcasted_iota(jnp.int32, (tile, 1), 0)) < total
            mixed = x_ref[0, r, :].astype(F32) + mm(o_s[r, :], wout[...]) + v(V_OUT)
            n2, r2 = norm_rows(mixed)
            h2 = (n2 * v(V_GAIN2) + v(V_SHIFT2)).astype(BF16)
            h2_s[r, :] = h2
            gy = jnp.where(valid, cot_ref[0, r, :].astype(F32), 0.0)
            gyl = gy.astype(BF16)
            gy_s[r, :] = gyl
            add_vec(G_FC2, col_sum(gy))
            for f in range(0, hidden, chunk):
                fs = slice(f, f + chunk)
                pre = mm(h2, w1[:, fs]) + vec[V_FC1 : V_FC1 + 1, fs]
                cdf = 0.5 * lax.erf(pre * 0.7071067811865476) + 0.5
                act_s[r, fs] = (pre * cdf).astype(BF16)
                slope = cdf + pre * (jnp.exp(pre * pre * -0.5) * 0.3989422804014327)
                gpre = (slope * mm_t(gyl, w2[fs, :])).astype(BF16)
                gpre_s[r, fs] = gpre
                a_vec[G_FC1 : G_FC1 + 1, fs] += col_sum(gpre.astype(F32))
            final = mixed + mm(act_s[r, :], w2[...]) + v(V_FC2)
            out_ref[0, r, :] = jnp.where(valid, final, 0.0).astype(BF16)
            gh2 = mm_t(gpre_s[r, :], w1[...])
            add_vec(G_GAIN2, col_sum(gh2 * n2))
            add_vec(G_SHIFT2, col_sum(gh2))
            gmix = gy + norm_back(n2, r2, gh2 * v(V_GAIN2))
            gmix_s[r, :] = gmix
            gb = gmix.astype(BF16)
            gb_s[r, :] = gb
            add_vec(G_OUT, col_sum(gb.astype(F32)))
            go_s[r, :] = mm_t(gb, wout[...]).astype(BF16)
            return c
        lax.fori_loop(0, rows // tile, mlp, 0)

    if "wg" in phases:
        a_fc1[...] += t_mm(h2_s[...], gpre_s[...])
        a_fc2[...] += t_mm(act_s[...], gy_s[...])
        a_out[...] += t_mm(o_s[...], gb_s[...])

    gqkv_s[:, : 2 * width] = jnp.zeros((rows, 2 * width), BF16)
    gqkv_s[:, 2 * width :] = go_s[...]

    if "ab" in phases:
        bwd = functools.partial(attend_bwd, meta, m, qkv_s, o_s, inv_s)
        @pl.when(length > 256)
        def _():
            bwd(e1_s, go_s, gqkv_s, *WIDE, pairs, width)
        @pl.when(jnp.logical_and(length <= 256, length > 128))
        def _():
            bwd(e2_s, go_s, gqkv_s, *NARROW1, pairs, width)
        @pl.when(length <= 128)
        def _():
            bwd(e2_s, go_s, gqkv_s, *NARROW2, pairs, width)

    if "p5" in phases:
        def p5(i, c):
            r = pl.ds(pl.multiple_of(i * tile, tile), tile)
            gqkv = gqkv_s[r, :]
            gh1 = mm_t(gqkv, wqkv[...])
            n1, r1 = norm_rows(x_ref[0, r, :].astype(F32))
            add_vec(G_QKV, col_sum(gqkv.astype(F32)))
            add_vec(G_GAIN1, col_sum(gh1 * n1))
            add_vec(G_SHIFT1, col_sum(gh1))
            ig_ref[0, r, :] = (gmix_s[r, :] + norm_back(n1, r1, gh1 * v(V_GAIN1))).astype(BF16)
            return c
        lax.fori_loop(0, rows // tile, p5, 0)
        a_qkv[...] += t_mm(h1_s[...], gqkv_s[...])

    @pl.when(m == pl.num_programs(0) - 1)
    def _():
        fold([a_qkv.at[:, 0:width], a_qkv.at[:, width : 2 * width], a_qkv.at[:, 2 * width :], a_out], p_attn, part)
        fold([a_fc1.at[:, i * width : (i + 1) * width] for i in range(4)], p_fc1, part)
        p_fc2[...] = a_fc2[...].astype(BF16)
        fold_vectors(a_vec, p_vec, part)


def layer_call(meta, x, cot, g_attn, g_fc1, w2, g_vec, **kw):
    micro, rows, width = x.shape
    hidden = w2.shape[0]
    row_block = pl.BlockSpec((1, rows, width), lambda m: (m, 0, 0))
    def whole(a):
        zeros = (0,) * len(a.shape)
        return pl.BlockSpec(a.shape, lambda m: zeros, pipeline_mode=pl.Buffered(1))
    gathered = (g_attn, g_fc1, w2, g_vec)
    bf = lambda n: pltpu.VMEM((rows, n), BF16)
    w_shapes = [(width, 3 * width), (width, width), (width, hidden), (hidden, width)]
    return pl.pallas_call(
        functools.partial(layer_kernel, **kw),
        grid=(micro,),
        in_specs=[pl.BlockSpec(memory_space=pltpu.SMEM), row_block, row_block] + [whole(a) for a in gathered],
        out_specs=[row_block, row_block] + [whole(a) for a in gathered],
        out_shape=[jax.ShapeDtypeStruct(x.shape, BF16)] * 2 + [jax.ShapeDtypeStruct(a.shape, a.dtype) for a in gathered],
        scratch_shapes=[pltpu.VMEM(s, BF16) for s in w_shapes[:3]] + [pltpu.VMEM((8, hidden), F32)]
        + [pltpu.VMEM(s, F32) for s in w_shapes] + [pltpu.VMEM((8, hidden), F32)] + [
            bf(width), bf(3 * width), bf(width), pltpu.VMEM((rows, width), F32),
            pltpu.VMEM((9, 352, 768), BF16), pltpu.VMEM((15, 224, 512), BF16),
            bf(width), bf(hidden), bf(hidden), bf(width), bf(width), bf(width),
            pltpu.VMEM((rows, width), F32), bf(3 * width),
        ],
        compiler_params=pltpu.CompilerParams(vmem_limit_bytes=64 * 2**20 - 2**17),
    )(meta, x, cot, g_attn, g_fc1, w2, g_vec)


def bit_of(me, b):
    return (me // (1 << b)) % 2

def partner_of(me, b):
    return me + (1 << b) * (1 - 2 * bit_of(me, b))

def meet(me, bits):
    barrier = pltpu.get_barrier_semaphore()
    for b in range(bits):
        pl.semaphore_signal(barrier, inc=1, device_id=(partner_of(me, b),), device_id_type=MESH)
    pl.semaphore_wait(barrier, bits)

def at_bits(ref, me, bits, free):
    return ref.at[tuple(slice(None) if b in free else bit_of(me, b) for b in reversed(range(bits)))]


def gather_kernel(bits, orders, *refs):
    k = len(orders)
    ins, outs, send, recv = refs[:k], refs[k : 2 * k], refs[2 * k], refs[2 * k + 1]
    me = lax.axis_index("dp")
    for i in range(k):
        at_bits(outs[i], me, bits, ())[...] = ins[i][...]
    meet(me, bits)
    copies = {}
    for stage in range(bits):
        for i in range(k):
            b = orders[i][stage]
            if stage:
                copies[i, stage - 1].wait_recv()
            blocks = at_bits(outs[i], me, bits, orders[i][:stage])
            c = pltpu.make_async_remote_copy(
                src_ref=blocks, dst_ref=blocks, send_sem=send.at[i, stage], recv_sem=recv.at[i, stage],
                device_id=(partner_of(me, b),), device_id_type=MESH)
            c.start()
            copies[i, stage] = c
    for i in range(k):
        copies[i, bits - 1].wait_recv()
    for c in copies.values():
        c.wait_send()


def gather_blocks(n, orders, arrays, collective_id):
    bits = n.bit_length() - 1
    k = len(arrays)
    vmem = pl.BlockSpec(memory_space=pltpu.VMEM)
    outs = pl.pallas_call(
        functools.partial(gather_kernel, bits, orders),
        in_specs=[vmem] * k,
        out_specs=[vmem] * k,
        out_shape=[jax.ShapeDtypeStruct((2,) * bits + a.shape, a.dtype) for a in arrays],
        scratch_shapes=[pltpu.SemaphoreType.DMA((k, bits)), pltpu.SemaphoreType.DMA((k, bits))],
        compiler_params=pltpu.CompilerParams(collective_id=collective_id, has_side_effects=True, vmem_limit_bytes=60 * 2**20),
    )(*arrays)
    return [o.reshape((n,) + a.shape) for o, a in zip(outs, arrays)]


def scatter_kernel(bits, orders, *refs):
    k = len(orders)
    ins, outs = refs[:k], refs[k : 2 * k]
    rest = refs[2 * k :]
    lands = [rest[i * bits : (i + 1) * bits] for i in range(k)]
    rest = rest[k * bits :]
    sums = [rest[i * (bits - 1) : (i + 1) * (bits - 1)] for i in range(k)]
    rest = rest[k * (bits - 1) :]
    send, recv = rest
    me = lax.axis_index("dp")
    meet(me, bits)
    copies = {}
    def idx(left, b, val):
        return tuple(val if x == b else slice(None) for x in left)
    def start(i, stage, src, left):
        b = orders[i][stage]
        mine = bit_of(me, b)
        c = pltpu.make_async_remote_copy(
            src_ref=src.at[idx(left, b, 1 - mine)], dst_ref=lands[i][stage], send_sem=send.at[i, stage], recv_sem=recv.at[i, stage],
            device_id=(partner_of(me, b),), device_id_type=MESH)
        c.start()
        copies[i, stage] = c
    lefts = [list(reversed(range(bits))) for _ in range(k)]
    for i in range(k):
        start(i, 0, ins[i], lefts[i])
    for stage in range(bits):
        for i in range(k):
            b = orders[i][stage]
            src = ins[i] if stage == 0 else sums[i][stage - 1]
            left = lefts[i]
            kept = src.at[idx(left, b, bit_of(me, b))]
            copies[i, stage].wait_recv()
            land = lands[i][stage]
            if stage == bits - 1:
                outs[i][...] = kept[...].astype(F32) + land[...].astype(F32)
                continue
            dst = sums[i][stage]
            if len(dst.shape) == 2:
                dst[...] = (kept[...].astype(F32) + land[...].astype(F32)).astype(dst.dtype)
            else:
                for t in range(2 ** (bits - 1 - stage)):
                    at = tuple((t >> s) % 2 for s in reversed(range(bits - 1 - stage)))
                    dst[at] = (kept[at].astype(F32) + land[at].astype(F32)).astype(dst.dtype)
            lefts[i] = [x for x in left if x != b]
            start(i, stage + 1, dst, lefts[i])
    for c in copies.values():
        c.wait_send()


def scatter_blocks(n, orders, arrays, collective_id):
    bits = n.bit_length() - 1
    k = len(arrays)
    vmem = pl.BlockSpec(memory_space=pltpu.VMEM)
    split = [a.reshape((2,) * bits + a.shape[1:]) for a in arrays]
    lands = [pltpu.VMEM((2,) * (bits - 1 - s) + a.shape[1:], a.dtype) for a in arrays for s in range(bits)]
    sums = [pltpu.VMEM((2,) * (bits - 1 - s) + a.shape[1:], a.dtype) for a in arrays for s in range(bits - 1)]
    return pl.pallas_call(
        functools.partial(scatter_kernel, bits, orders),
        in_specs=[vmem] * k,
        out_specs=[vmem] * k,
        out_shape=[jax.ShapeDtypeStruct(a.shape[1:], F32) for a in arrays],
        scratch_shapes=lands + sums + [pltpu.SemaphoreType.DMA((k, bits)), pltpu.SemaphoreType.DMA((k, bits))],
        compiler_params=pltpu.CompilerParams(collective_id=collective_id, has_side_effects=True, vmem_limit_bytes=60 * 2**20),
    )(*split)


def pieces(shard, high):
    part, cols = shard.shape
    folded = shard.reshape(part, 4, cols // 4).transpose(1, 0, 2).reshape(4 * part, cols // 4)
    return jnp.pad(folded, ((0, high - 4 * part), (0, 0)))


def unpieces(folded, part):
    cols = folded.shape[1]
    return folded[: 4 * part].reshape(4, part, cols).transpose(1, 0, 2).reshape(part, 4 * cols)


def routes(bits):
    if bits == 5:
        return [(4, 3, 2, 1, 0), (4, 3, 1, 2, 0), (2, 1, 4, 3, 0), (4, 3, 2, 1, 0)]
    return [tuple(reversed(range(bits)))] * 4


def body(inputs, cotangent, w_qkv, w_out, w_fc1, w_fc2, gain1, shift1, q_bias, v_bias, out_bias, gain2, shift2,
         fc1_bias, fc2_bias, image_tokens, image_count):
    me = lax.axis_index("dp")
    n = lax.axis_size("dp")
    part, width = w_out.shape
    hidden = w_fc1.shape[1]
    high = -(-4 * part // 16) * 16
    orders = routes(n.bit_length() - 1)
    small = jnp.stack([gain1, shift1, q_bias, v_bias, out_bias, gain2, shift2, fc2_bias]).astype(F32)
    small = jnp.concatenate([
        jnp.pad(small, ((0, 0), (0, 128 - part))),
        jnp.pad(fc1_bias.astype(F32)[None], ((0, 7), (0, 128 - 4 * part))),
    ])
    attn = pieces(jnp.concatenate([w_qkv, w_out], axis=1), high)
    fc2 = jnp.pad(w_fc2, ((0, high - 4 * part), (0, 0)))
    g_attn, g_fc1, g_fc2, g_vec = gather_blocks(n, orders, [attn, pieces(w_fc1, high), fc2, small], 1)
    meta = jnp.stack([
        lax.dynamic_index_in_dim(image_tokens, me, 1, False), lax.dynamic_index_in_dim(image_count, me, 1, False)
    ], axis=1)
    out, ig, p_attn, p_fc1, p_fc2, p_vec = layer_call(
        meta, inputs, cotangent, g_attn.reshape(n * high, width), g_fc1.reshape(n * high, width),
        g_fc2[:, : 4 * part].reshape(hidden, width), g_vec)
    p_fc2 = jnp.pad(p_fc2.reshape(n, 4 * part, width), ((0, 0), (0, high - 4 * part), (0, 0)))
    back = [tuple(reversed(o)) for o in orders]
    s_attn, s_fc1, s_fc2, s_vec = scatter_blocks(
        n, back, [p_attn.reshape(n, high, width), p_fc1.reshape(n, high, width), p_fc2, p_vec], 2)
    s_attn = unpieces(s_attn, part)
    v = [s_vec[i, :part] for i in range(8)]
    return (out, ig, s_attn[:, : 3 * width], s_attn[:, 3 * width :], unpieces(s_fc1, part), s_fc2[: 4 * part],
            v[0], v[1], v[2], v[3], v[4], v[5], v[6], s_vec[8, : 4 * part], v[7])


def solution(mesh):
    big, mat, one = P(None, "dp", None), P("dp", None), P("dp")
    return jax.shard_map(
        body, mesh=mesh,
        in_specs=(big, big) + (mat,) * 4 + (one,) * 9 + (P(), P()),
        out_specs=(big, big) + (mat,) * 4 + (one,) * 9,
        check_vma=False,
    )
```

```python
import functools

import jax
import jax.numpy as jnp
from jax import lax
from jax.experimental import pallas as pl
from jax.experimental.pallas import tpu as pltpu
from jax.sharding import PartitionSpec as P

F32, BF16 = jnp.float32, jnp.bfloat16
MESH = pl.DeviceIdType.MESH

HEADS = 6
EPS = 1e-06
FAR = -1e30
V_GAIN1, V_SHIFT1, V_QKV, V_OUT, V_GAIN2, V_SHIFT2, V_FC1, V_FC2 = range(8)
G_GAIN1, G_SHIFT1, G_QKV, G_OUT, G_GAIN2, G_SHIFT2, G_FC1, G_FC2 = range(8)


def mm(a, b):
    return jnp.dot(a, b, preferred_element_type=F32)

def mm_t(a, b):
    return lax.dot_general(a, b, (((1,), (1,)), ((), ())), preferred_element_type=F32)

def t_mm(a, b):
    return lax.dot_general(a, b, (((0,), (0,)), ((), ())), preferred_element_type=F32)


def norm_rows(v):
    width = v.shape[1]
    off = v - jnp.sum(v, axis=1, keepdims=True) * (1.0 / width)
    inv = lax.rsqrt(jnp.sum(off * off, axis=1, keepdims=True) * (1.0 / width) + EPS)
    return off * inv, inv


def norm_back(n, inv, t):
    width = n.shape[1]
    a = jnp.sum(t, axis=1, keepdims=True) * (1.0 / width)
    b = jnp.sum(t * n, axis=1, keepdims=True) * (1.0 / width)
    return inv * (t - a - n * b)


def col_sum(v):
    return jnp.sum(v, axis=0, keepdims=True)


def window(meta, m, w, group, wq, wk, rows):
    length, count = meta[m, 0], meta[m, 1]
    lo = w * (length * group)
    hi = jnp.minimum(lo + length * group, length * count)
    base = (lo // 16) * 16
    sq = pl.multiple_of(jnp.minimum(base, rows - wq), 16)
    sk = pl.multiple_of(jnp.minimum(base, rows - wk), 16)
    return lo, hi, length, sq, sk


def seg_of(start, n, lo, hi, length):
    r = start + lax.broadcasted_iota(jnp.int32, (n, 128), 0)
    inside = jnp.logical_and(r >= lo, r < hi)
    return inside, jnp.where(inside, jnp.where(r >= lo + length, 1, 0), 2)


def halves(v):
    left = lax.broadcasted_iota(jnp.int32, v.shape, 1) < 64
    zero = jnp.zeros_like(v)
    return jnp.where(left, v, zero), jnp.where(left, zero, v)


def attend_fwd(meta, m, qkv_s, o_s, inv_s, e_s, group, wq, wk, pairs, width):
    rows = qkv_s.shape[0]
    scale = 0.125 * 1.4426950408889634

    def one(w, carry):
        lo, hi, length, sq, sk = window(meta, m, w, group, wq, wk, rows)
        in_q, seg_q = seg_of(sq, wq, lo, hi, length)
        _, seg_k = seg_of(sk, wk, lo, hi, length)
        lane_q = lax.broadcasted_iota(jnp.int32, (wq, 128), 1)
        lane_k = lax.broadcasted_iota(jnp.int32, (wk, 128), 1)
        aug_q = jnp.where(jnp.logical_and(lane_q != seg_q, lane_q < 3), 1.0, 0.0).astype(BF16)
        aug_k = jnp.where(lane_k == seg_k, FAR, 0.0).astype(BF16)
        ones0 = jnp.where(lane_k < 64, 1.0, 0.0).astype(BF16)
        ones1 = jnp.where(lane_k < 64, 0.0, 1.0).astype(BF16)
        for p in range(pairs):
            c = 128 * p
            q2 = qkv_s[pl.ds(sq, wq), c : c + 128]
            k0, k1 = halves(qkv_s[pl.ds(sk, wk), width + c : width + c + 128])
            v0, v1 = halves(qkv_s[pl.ds(sk, wk), 2 * width + c : 2 * width + c + 128])
            left = jnp.concatenate([q2, aug_q], axis=1)
            right = jnp.concatenate(
                [jnp.concatenate([k0, aug_k], axis=1), jnp.concatenate([k1, aug_k], axis=1)], axis=0
            )
            s = mm_t(left, right)
            parts = []
            for h in range(2):
                sh = s[:, h * wk : (h + 1) * wk]
                top = jnp.max(sh, axis=1, keepdims=True)
                parts.append(jnp.exp2((sh - top) * scale).astype(BF16))
            e = jnp.concatenate(parts, axis=1)
            e_s[w * pairs + p] = e
            vals = jnp.concatenate(
                [jnp.concatenate([v0, ones0], axis=1), jnp.concatenate([v1, ones1], axis=1)], axis=0
            )
            both = mm(e, vals)
            inv = 1.0 / both[:, 128:]
            o = (both[:, :128] * inv).astype(BF16)
            dst = (pl.ds(sq, wq), pl.ds(c, 128))
            o_s[dst] = jnp.where(in_q, o, o_s[dst])
            inv_s[dst] = jnp.where(in_q, inv, inv_s[dst])
        return carry

    lax.fori_loop(0, (meta[m, 1] + group - 1) // group, one, 0)


def attend_bwd(meta, m, qkv_s, o_s, inv_s, e_s, go_s, gqkv_s, group, wq, wk, pairs, width):
    rows = qkv_s.shape[0]

    def one(w, carry):
        lo, hi, length, sq, sk = window(meta, m, w, group, wq, wk, rows)
        in_q, _ = seg_of(sq, wq, lo, hi, length)
        in_k, _ = seg_of(sk, wk, lo, hi, length)
        for p in range(pairs):
            c = 128 * p
            e = e_s[w * pairs + p]
            q0, q1 = halves(qkv_s[pl.ds(sq, wq), c : c + 128])
            k0, k1 = halves(qkv_s[pl.ds(sk, wk), width + c : width + c + 128])
            v0, v1 = halves(qkv_s[pl.ds(sk, wk), 2 * width + c : 2 * width + c + 128])
            dst_q = (pl.ds(sq, wq), pl.ds(c, 128))
            go = (go_s[dst_q].astype(F32) * inv_s[dst_q]).astype(BF16)
            prod0, prod1 = halves(go.astype(F32) * o_s[dst_q].astype(F32))
            d = (jnp.sum(prod0, axis=1, keepdims=True), jnp.sum(prod1, axis=1, keepdims=True))
            gp = mm_t(go, jnp.concatenate([v0, v1], axis=0))
            gs = []
            for h in range(2):
                sl = slice(h * wk, (h + 1) * wk)
                gs.append((e[:, sl].astype(F32) * (gp[:, sl] - d[h])).astype(BF16))
            gq = mm(jnp.concatenate(gs, axis=1), jnp.concatenate([k0, k1], axis=0)) * 0.125
            gk = t_mm(jnp.concatenate(gs, axis=0), jnp.concatenate([q0, q1], axis=0)) * 0.125
            gv = t_mm(
                jnp.concatenate([e[:, :wk], e[:, wk:]], axis=0), jnp.concatenate(halves(go), axis=0)
            )
            gqkv_s[dst_q] = jnp.where(in_q, gq.astype(BF16), gqkv_s[dst_q])
            dst_k = (pl.ds(sk, wk), pl.ds(width + c, 128))
            gqkv_s[dst_k] = jnp.where(in_k, gk.astype(BF16), gqkv_s[dst_k])
            dst_v = (pl.ds(sk, wk), pl.ds(2 * width + c, 128))
            gqkv_s[dst_v] = jnp.where(in_k, gv.astype(BF16), gqkv_s[dst_v])
        return carry

    lax.fori_loop(0, (meta[m, 1] + group - 1) // group, one, 0)


WIDE = (1, 352, 384)
NARROW1 = (1, 224, 256)
NARROW2 = (2, 224, 256)


def fold_matrix(part, count, high):
    rows, cols = 4 * count * part, count * high
    r = lax.broadcasted_iota(jnp.int32, (rows, cols), 0).astype(F32)
    c = lax.broadcasted_iota(jnp.int32, (rows, cols), 1).astype(F32)
    block = jnp.floor((c + 0.5) * (1.0 / high))
    inner = c - block * high
    piece = jnp.floor((inner + 0.5) * (1.0 / part))
    want = piece * (count * part) + block * part + (inner - piece * part)
    return jnp.where(jnp.logical_and(want == r, piece < 4), 1.0, 0.0).astype(BF16)


def unfold(blocks, dsts, part, high):
    count = 96 // part
    pick = fold_matrix(part, count, high)
    for t in range(len(blocks) // count):
        group = jnp.concatenate([blocks[j][...] for j in range(t * count, (t + 1) * count)], axis=0)
        full = mm(pick, group).astype(BF16)
        for a in range(4):
            dsts[a][96 * t : 96 * (t + 1), :] = full[96 * a : 96 * (a + 1), :]


def fold(srcs, blocks, part, high):
    count = 96 // part
    pick = fold_matrix(part, count, high)
    for t in range(len(blocks) // count):
        rows = slice(96 * t, 96 * (t + 1))
        four = jnp.concatenate([s[rows, :].astype(BF16) for s in srcs], axis=0)
        full = t_mm(pick, four).astype(BF16)
        for i in range(count):
            blocks[t * count + i][...] = full[i * high : (i + 1) * high, :]


def unfold_vectors(blocks, vec, part):
    n = len(blocks)
    width = part * n
    lane = lax.broadcasted_iota(jnp.int32, (8, 128), 1)
    total = jnp.zeros((8, width), F32)
    wide = jnp.zeros((8, 4 * width), F32)
    for j in range(n):
        pair = blocks[j][...].astype(F32)
        one = jnp.where(lane < part, pair[0:8], 0.0)
        one = jnp.concatenate([one, jnp.zeros((8, width - 128), F32)], axis=1)
        total = total + pltpu.roll(one, j * part, 1)
        one = jnp.where(lane < 4 * part, pair[8:16], 0.0)
        one = jnp.concatenate([one, jnp.zeros((8, 4 * width - 128), F32)], axis=1)
        wide = wide + pltpu.roll(one, 4 * j * part, 1)
    vec[...] = jnp.zeros_like(vec)
    for i, (row, col) in enumerate(VECTORS):
        vec[row : row + 1, col * width : (col + 1) * width] = total[i : i + 1]
    vec[V_FC1 : V_FC1 + 1, :] = wide[0:1]


def fold_vectors(vec, blocks, part):
    n = len(blocks)
    width = part * n
    eight = jnp.concatenate(
        [vec[row : row + 1, col * width : (col + 1) * width] for row, col in VECTORS], axis=0
    )
    wide = jnp.broadcast_to(vec[V_FC1 : V_FC1 + 1, :], (8, 4 * width))
    for j in range(n):
        blocks[j][0:8, :] = pltpu.roll(eight, (width - j * part) % width, 1)[:, :128]
        blocks[j][8:16, :] = pltpu.roll(wide, (4 * width - 4 * j * part) % (4 * width), 1)[:, :128]


VECTORS = ((V_GAIN1, 0), (V_SHIFT1, 0), (V_QKV, 0), (V_QKV, 2), (V_OUT, 0), (V_GAIN2, 0), (V_SHIFT2, 0), (V_FC2, 0))


def layer_kernel(
    meta, x_ref, cot_ref, qkv_ref, wout, w1, w2, vec,
    out_ref, gqkv_ref, gmix_ref, p_fc1, p_fc2, a_out, a_vec,
    a_fc1, a_fc2, o_s, inv_s, e1_s, e2_s, h2_s, act_s, gpre_s, gy_s, gb_s, go_s,
    part, phases=("af", "mlp", "wg", "ab"), tile=1024, chunk=256,
):
    m = pl.program_id(0)
    rows, width = x_ref.shape[1], x_ref.shape[2]
    hidden = w1.shape[1]
    pairs = HEADS // 2
    length, count = meta[m, 0], meta[m, 1]
    total = length * count
    qkv_s, gqkv_s, gmix_s = qkv_ref.at[0], gqkv_ref.at[0], gmix_ref.at[0]

    @pl.when(m == 0)
    def _():
        for ref in (a_out, a_fc1, a_fc2, a_vec):
            ref[...] = jnp.zeros_like(ref)

    def v(i, n=width):
        return vec[i : i + 1, 0:n]

    def add_vec(i, val):
        a_vec[i : i + 1, 0 : val.shape[1]] += val

    o_s[...] = qkv_s[:, 2 * width :]

    if "af" in phases:
        fwd = functools.partial(attend_fwd, meta, m, qkv_s, o_s, inv_s)
        @pl.when(length > 256)
        def _():
            fwd(e1_s, *WIDE, pairs, width)
        @pl.when(jnp.logical_and(length <= 256, length > 128))
        def _():
            fwd(e2_s, *NARROW1, pairs, width)
        @pl.when(length <= 128)
        def _():
            fwd(e2_s, *NARROW2, pairs, width)

    if "mlp" in phases:
        def mlp(i, c):
            r = pl.ds(pl.multiple_of(i * tile, tile), tile)
            valid = (i * tile + lax.broadcasted_iota(jnp.int32, (tile, 1), 0)) < total
            mixed = x_ref[0, r, :].astype(F32) + mm(o_s[r, :], wout[...]) + v(V_OUT)
            n2, r2 = norm_rows(mixed)
            h2 = (n2 * v(V_GAIN2) + v(V_SHIFT2)).astype(BF16)
            h2_s[r, :] = h2
            gy = jnp.where(valid, cot_ref[0, r, :].astype(F32), 0.0)
            gyl = gy.astype(BF16)
            gy_s[r, :] = gyl
            add_vec(G_FC2, col_sum(gy))
            for f in range(0, hidden, chunk):
                fs = slice(f, f + chunk)
                pre = mm(h2, w1[:, fs]) + vec[V_FC1 : V_FC1 + 1, fs]
                cdf = 0.5 * lax.erf(pre * 0.7071067811865476) + 0.5
                act_s[r, fs] = (pre * cdf).astype(BF16)
                slope = cdf + pre * (jnp.exp(pre * pre * -0.5) * 0.3989422804014327)
                gpre = (slope * mm_t(gyl, w2[fs, :])).astype(BF16)
                gpre_s[r, fs] = gpre
                a_vec[G_FC1 : G_FC1 + 1, fs] += col_sum(gpre.astype(F32))
            final = mixed + mm(act_s[r, :], w2[...]) + v(V_FC2)
            out_ref[0, r, :] = jnp.where(valid, final, 0.0).astype(BF16)
            gh2 = mm_t(gpre_s[r, :], w1[...])
            add_vec(G_GAIN2, col_sum(gh2 * n2))
            add_vec(G_SHIFT2, col_sum(gh2))
            gmix = gy + norm_back(n2, r2, gh2 * v(V_GAIN2))
            gmix_s[r, :] = gmix
            gb = gmix.astype(BF16)
            gb_s[r, :] = gb
            add_vec(G_OUT, col_sum(gb.astype(F32)))
            go_s[r, :] = mm_t(gb, wout[...]).astype(BF16)
            return c
        lax.fori_loop(0, rows // tile, mlp, 0)

    if "wg" in phases:
        a_fc1[...] += t_mm(h2_s[...], gpre_s[...])
        a_fc2[...] += t_mm(act_s[...], gy_s[...])
        a_out[...] += t_mm(o_s[...], gb_s[...])

    gqkv_s[:, : 2 * width] = jnp.zeros((rows, 2 * width), BF16)
    gqkv_s[:, 2 * width :] = go_s[...]

    if "ab" in phases:
        bwd = functools.partial(attend_bwd, meta, m, qkv_s, o_s, inv_s)
        @pl.when(length > 256)
        def _():
            bwd(e1_s, go_s, gqkv_s, *WIDE, pairs, width)
        @pl.when(jnp.logical_and(length <= 256, length > 128))
        def _():
            bwd(e2_s, go_s, gqkv_s, *NARROW1, pairs, width)
        @pl.when(length <= 128)
        def _():
            bwd(e2_s, go_s, gqkv_s, *NARROW2, pairs, width)

    @pl.when(m == pl.num_programs(0) - 1)
    def _():
        high = p_fc1.shape[0] // (width // part)
        blocks = [p_fc1.at[j * high : (j + 1) * high, :] for j in range(width // part)]
        fold([a_fc1.at[:, i * width : (i + 1) * width] for i in range(4)], blocks, part, high)
        p_fc2[...] = a_fc2[...].astype(BF16)


def layer_call(meta, x, cot, qkv, wout, w1, w2, vec, n, **kw):
    micro, rows, width = x.shape
    hidden = w2.shape[0]
    part = width // n
    high = -(-4 * part // 16) * 16
    def per_step(cols):
        return pl.BlockSpec((1, rows, cols), lambda m: (m, 0, 0))
    def whole(shape):
        return pl.BlockSpec(shape, lambda m: (0, 0), pipeline_mode=pl.Buffered(1))
    bf = lambda n: pltpu.VMEM((rows, n), BF16)
    outs = [(x.shape, BF16), ((micro, rows, 3 * width), BF16), (x.shape, F32)]
    kept = [((n * high, width), BF16), ((hidden, width), BF16), ((width, width), F32), (vec.shape, F32)]
    return pl.pallas_call(
        functools.partial(layer_kernel, part=part, **kw),
        grid=(micro,),
        in_specs=[pl.BlockSpec(memory_space=pltpu.SMEM), per_step(width), per_step(width), per_step(3 * width)]
        + [whole(a.shape) for a in (wout, w1, w2, vec)],
        out_specs=[per_step(s[2]) for s, _ in outs] + [whole(s) for s, _ in kept],
        out_shape=[jax.ShapeDtypeStruct(s, d) for s, d in outs + kept],
        scratch_shapes=[
            pltpu.VMEM((width, hidden), F32), pltpu.VMEM((hidden, width), F32),
            bf(width), pltpu.VMEM((rows, width), F32),
            pltpu.VMEM((9, 352, 768), BF16), pltpu.VMEM((15, 224, 512), BF16),
            bf(width), bf(hidden), bf(hidden), bf(width), bf(width), bf(width),
        ],
        compiler_params=pltpu.CompilerParams(vmem_limit_bytes=64 * 2**20 - 2**17),
    )(meta, x, cot, qkv, wout, w1, w2, vec)


def bit_of(me, b):
    return (me // (1 << b)) % 2


class Place:
    def __init__(self, n):
        self.me = lax.axis_index("dp")
        self.count = n // 8
        self.z, self.y, self.x, self.c = self.me // 8, bit_of(self.me, 2), bit_of(self.me, 1), bit_of(self.me, 0)
        self.over_y = self.me + 4 * (1 - 2 * self.y)
        self.over_x = self.me + 2 * (1 - 2 * self.x)
        self.twin = self.me + (1 - 2 * self.c)
        self.steps = sorted(range(1, self.count), key=lambda k: min(k, self.count - k))

    def ahead(self, k):
        return (self.z + k) % self.count

    def behind(self, k):
        return (self.z + self.count - k) % self.count

    def at(self, z):
        return self.me + 8 * (z - self.z)

    def meet(self):
        barrier = pltpu.get_barrier_semaphore()
        others = [self.over_y, self.over_x, self.twin] + [self.at(self.ahead(k)) for k in range(1, self.count)]
        for device in others:
            pl.semaphore_signal(barrier, inc=1, device_id=(device,), device_id_type=MESH)
        pl.semaphore_wait(barrier, len(others))


LINE, ALONG_X, ALONG_Y, DIAG_X, DIAG_Y, TWIN = range(6)


class Wire:
    def __init__(self, place, cut, send, recv):
        self.place, self.cut, self.send, self.recv, self.started = place, cut, send, recv, []

    def copy(self, kind, k, src, dst, device):
        return pltpu.make_async_remote_copy(
            src_ref=src, dst_ref=dst, send_sem=self.send.at[kind, k], recv_sem=self.recv.at[kind, k],
            device_id=(device,), device_id_type=MESH)

    def push(self, kind, k, src, dst, device):
        copy = self.copy(kind, k, src, dst, device)
        copy.start()
        self.started.append(copy)

    def arrive(self, kind, k, dst):
        self.copy(kind, k, dst, dst, self.place.twin).wait_recv()

    def finish(self):
        for copy in self.started:
            copy.wait_send()

    def columns(self, k, width):
        if self.cut is None:
            return slice(0, width), None
        cut = 128 if (k + self.cut) % 2 else width - 128
        return slice(0, cut), slice(cut, width)


class Gather(Wire):
    def __init__(self, place, ref, cut, send, recv):
        super().__init__(place, cut, send, recv)
        self.ref = ref

    def block(self, k, over_y, over_x, cols=slice(None)):
        p = self.place
        y = 1 - p.y if over_y else p.y
        x = 1 - p.x if over_x else p.x
        return self.ref.at[p.behind(k), y, x, p.c, :, cols]

    def same(self, kind, k, view, device):
        self.push(kind, k, view, view, device)

    def begin(self):
        p = self.place
        for k in p.steps:
            self.same(LINE, k, self.block(0, False, False), p.at(p.ahead(k)))

    def line(self, k):
        view = self.block(k, False, False)
        if k:
            self.arrive(LINE, k, view)
        self.same(ALONG_X, k, view, self.place.over_x)
        self.same(ALONG_Y, k, view, self.place.over_y)

    def plane(self, k):
        first, second = self.columns(k, self.ref.shape[-1])
        self.arrive(ALONG_X, k, self.block(k, False, True))
        self.same(DIAG_Y, k, self.block(k, False, True, first), self.place.over_y)
        self.arrive(ALONG_Y, k, self.block(k, True, False))
        if second is not None:
            self.same(DIAG_X, k, self.block(k, True, False, second), self.place.over_x)

    def corner(self, k):
        first, second = self.columns(k, self.ref.shape[-1])
        self.arrive(DIAG_Y, k, self.block(k, True, True, first))
        if second is not None:
            self.arrive(DIAG_X, k, self.block(k, True, True, second))
        p = self.place
        self.same(TWIN, k, self.ref.at[p.behind(k), :, :, p.c], p.twin)

    def last(self):
        p = self.place
        for k in range(p.count):
            self.arrive(TWIN, k, self.ref.at[p.behind(k), :, :, 1 - p.c])


class Scatter(Wire):
    def __init__(self, place, src, cut, scratch, out, send, recv):
        super().__init__(place, cut, send, recv)
        self.src, self.out = src, out
        self.twins, self.diag_x, self.diag_y, self.from_x, self.from_y, self.lines, self.sums = scratch

    def half(self, k, y, x):
        p = self.place
        z = p.ahead(k)
        return self.src[z, y, x, p.c].astype(F32) + self.twins[z, y, x].astype(F32)

    def begin(self):
        p = self.place
        for k in p.steps + [0]:
            z = p.ahead(k)
            self.push(TWIN, k, self.src.at[z, :, :, 1 - p.c], self.twins.at[z], p.twin)

    def corner(self, k):
        p = self.place
        self.arrive(TWIN, k, self.twins.at[p.ahead(k)])
        first, second = self.columns(k, self.src.shape[-1])
        held = self.sums.at[0, k]
        held[...] = self.half(k, 1 - p.y, 1 - p.x).astype(held.dtype)
        self.push(DIAG_Y, k, held.at[:, first], self.diag_x.at[k, :, first], p.over_y)
        if second is not None:
            self.push(DIAG_X, k, held.at[:, second], self.diag_y.at[k, :, second], p.over_x)

    def plane(self, k):
        p = self.place
        first, second = self.columns(k, self.src.shape[-1])
        self.arrive(DIAG_Y, k, self.diag_x.at[k, :, first])
        held = self.sums.at[1, k]
        total = self.half(k, p.y, 1 - p.x)
        held[:, first] = (total[:, first] + self.diag_x[k, :, first].astype(F32)).astype(held.dtype)
        if second is not None:
            held[:, second] = total[:, second].astype(held.dtype)
        self.push(ALONG_X, k, held, self.from_x.at[k], p.over_x)
        held = self.sums.at[2, k]
        total = self.half(k, 1 - p.y, p.x)
        if second is None:
            held[...] = total.astype(held.dtype)
        else:
            self.arrive(DIAG_X, k, self.diag_y.at[k, :, second])
            held[:, first] = total[:, first].astype(held.dtype)
            held[:, second] = (total[:, second] + self.diag_y[k, :, second].astype(F32)).astype(held.dtype)
        self.push(ALONG_Y, k, held, self.from_y.at[k], p.over_y)

    def line(self, k):
        p = self.place
        self.arrive(ALONG_X, k, self.from_x.at[k])
        self.arrive(ALONG_Y, k, self.from_y.at[k])
        total = self.half(k, p.y, p.x) + self.from_x[k].astype(F32) + self.from_y[k].astype(F32)
        if k == 0:
            self.out[...] = total
            return
        held = self.sums.at[3, k]
        held[...] = total.astype(held.dtype)
        self.push(LINE, k, held, self.lines.at[k], p.at(p.ahead(k)))

    def last(self):
        total = self.out[...]
        for k in self.place.steps:
            self.arrive(LINE, k, self.lines.at[k])
            total = total + self.lines[k].astype(F32)
        self.out[...] = total


def gather_kernel(
    n, tile, x_ref, attn, fc1, fc2, small, qkv_ref, wqkv, wout, w1, g_fc2, vec,
    x_s, qkv_s, g_attn, g_fc1, g_vec, x_sem, qkv_sem, send, recv,
):
    place = Place(n)
    micro, rows, width = x_s.shape
    part = width // n
    height = attn.shape[0]
    loads = [pltpu.make_async_copy(x_ref.at[m], x_s.at[m], x_sem.at[m]) for m in range(micro)]
    for load in loads:
        load.start()
    own = (place.z, place.y, place.x, place.c)
    g_vec[own] = small[...]
    g_attn[own] = attn[...]
    g_fc1[own] = fc1[...]
    g_fc2[own] = fc2[...]
    place.meet()

    refs = (g_vec, g_attn, g_fc1, g_fc2)
    parts = [Gather(place, ref, cut, send.at[i], recv.at[i]) for i, (ref, cut) in enumerate(zip(refs, (None, 0, 1, 0)))]
    urgent, rest = parts[:2], parts[2:]
    order = [0] + place.steps
    todo = [(p, "line", k) for k in order for p in rest]
    todo += [(p, "plane", k) for k in order for p in rest]
    todo += [(p, "corner", k) for k in order for p in rest]

    def some(count):
        for p, stage, k in todo[:count]:
            getattr(p, stage)(k)
        del todo[:count]

    for p in urgent:
        p.begin()
    for p in urgent:
        p.line(0)
    for p in rest:
        p.begin()
    for k in place.steps:
        for p in urgent:
            p.line(k)
    for k in order:
        for p in urgent:
            p.plane(k)
        some(2)
    for k in order:
        for p in urgent:
            p.corner(k)
        some(2)
    for p in urgent:
        p.last()
    flat = lambda ref: [ref.at[j // 8, (j // 4) % 2, (j // 2) % 2, j % 2] for j in range(n)]
    unfold_vectors(flat(g_vec), vec, part)
    unfold(flat(g_attn), [wqkv.at[:, 0:width], wqkv.at[:, width : 2 * width], wqkv.at[:, 2 * width :], wout], part, height)

    def qkv_part(m, i):
        r = pl.ds(i * tile, tile)
        n1, _ = norm_rows(x_s[m, r, :].astype(F32))
        h1 = (n1 * vec[V_GAIN1 : V_GAIN1 + 1, 0:width] + vec[V_SHIFT1 : V_SHIFT1 + 1, 0:width]).astype(BF16)
        qkv_s[m, r, :] = (mm(h1, wqkv[...]) + vec[V_QKV : V_QKV + 1, 0 : 3 * width]).astype(BF16)

    stores = [pltpu.make_async_copy(qkv_s.at[m], qkv_ref.at[m], qkv_sem.at[m]) for m in range(micro)]
    turns = micro * (rows // tile)
    each = -(-len(todo) // max(turns, 1))
    for m in range(micro):
        loads[m].wait()
        for i in range(rows // tile):
            qkv_part(m, i)
            some(each)
        stores[m].start()
    some(len(todo))
    rest[0].last()
    unfold(flat(g_fc1), [w1.at[:, i * width : (i + 1) * width] for i in range(4)], part, height)
    rest[1].last()
    for p in parts:
        p.finish()
    for store in stores:
        store.wait()


def gather_call(n, x, attn, fc1, fc2, small, collective_id, tile=512):
    micro, rows, width = x.shape
    vmem, hbm = pl.BlockSpec(memory_space=pltpu.VMEM), pl.BlockSpec(memory_space=pl.ANY)
    grid = (n // 8, 2, 2, 2)
    sems = pltpu.SemaphoreType.DMA((4, 6, n // 8))
    shapes = [((micro, rows, 3 * width), BF16), ((width, 3 * width), BF16), ((width, width), BF16),
              ((width, 4 * width), BF16), (grid + fc2.shape, BF16), ((8, 4 * width), F32)]
    return pl.pallas_call(
        functools.partial(gather_kernel, n, tile),
        in_specs=[hbm] + [vmem] * 4,
        out_specs=[hbm] + [vmem] * 5,
        out_shape=[jax.ShapeDtypeStruct(s, d) for s, d in shapes],
        scratch_shapes=[
            pltpu.VMEM(x.shape, BF16), pltpu.VMEM((micro, rows, 3 * width), BF16),
            pltpu.VMEM(grid + attn.shape, BF16), pltpu.VMEM(grid + fc1.shape, BF16), pltpu.VMEM(grid + small.shape, BF16),
            pltpu.SemaphoreType.DMA((micro,)), pltpu.SemaphoreType.DMA((micro,)), sems, sems,
        ],
        compiler_params=pltpu.CompilerParams(
            collective_id=collective_id, has_side_effects=True, vmem_limit_bytes=60 * 2**20),
    )(x, attn, fc1, fc2, small)


def scatter_kernel(
    n, tile, x_ref, gqkv_ref, gmix_ref, wqkv, vec, p_fc1, p_fc2, p_out, gvec,
    ig_ref, o_attn, o_fc1, o_fc2, o_vec,
    x_s, gqkv_s, gmix_s, ig_s, h1_s, acc, acc_vec, p_attn, p_vec, in_sem, out_sem, send, recv, *rest,
):
    place = Place(n)
    micro, rows, width = x_s.shape
    part = width // n
    height = p_fc1.shape[-2]
    loads = []
    for m in range(micro):
        pairs = ((x_ref, x_s), (gqkv_ref, gqkv_s), (gmix_ref, gmix_s))
        loads.append([pltpu.make_async_copy(a.at[m], b.at[m], in_sem.at[i, m]) for i, (a, b) in enumerate(pairs)])
        for load in loads[m]:
            load.start()
    place.meet()

    def stream(i, src, cut, out):
        return Scatter(place, src, cut, rest[7 * i : 7 * i + 7], out, send.at[i], recv.at[i])
    fc = [stream(0, p_fc1, 0, o_fc1), stream(1, p_fc2, 1, o_fc2)]
    attn, vecs = stream(2, p_attn, 0, o_attn), stream(3, p_vec, None, o_vec)
    order = place.steps + [0]
    def stages(streams):
        return [(s, stage, k) for stage in ("corner", "plane", "line") for k in order for s in streams]
    todo = stages(fc)

    def some(count):
        for s, stage, k in todo[:count]:
            getattr(s, stage)(k)
        del todo[:count]

    for s in fc:
        s.begin()

    def v(i, cols=width):
        return vec[i : i + 1, 0:cols]

    acc_vec[...] = gvec[...]
    for m in range(micro):
        for load in loads[m][:2]:
            load.wait()
        for i in range(rows // tile):
            r = pl.ds(i * tile, tile)
            n1, _ = norm_rows(x_s[m, r, :].astype(F32))
            h1_s[m, r, :] = (n1 * v(V_GAIN1) + v(V_SHIFT1)).astype(BF16)
        g = t_mm(h1_s[m], gqkv_s[m])
        acc[...] = g if m == 0 else acc[...] + g
        some(len(order) * 2 if m == 0 else len(order))
    flat = lambda ref: [ref.at[j // 8, (j // 4) % 2, (j // 2) % 2, j % 2] for j in range(n)]
    fold([acc.at[:, 0:width], acc.at[:, width : 2 * width], acc.at[:, 2 * width :], p_out], flat(p_attn), part, height)
    attn.begin()
    late = stages([attn])
    todo = [t for pair in zip(todo, late) for t in pair] + todo[len(late) :] + late[len(todo) :]

    stores = [pltpu.make_async_copy(ig_s.at[m], ig_ref.at[m], out_sem.at[m]) for m in range(micro)]
    turns = micro * (rows // tile)
    each = -(-len(todo) // turns)
    for m in range(micro):
        loads[m][2].wait()
        for i in range(rows // tile):
            r = pl.ds(i * tile, tile)
            gqkv = gqkv_s[m, r, :]
            gh1 = mm_t(gqkv, wqkv[...])
            n1, r1 = norm_rows(x_s[m, r, :].astype(F32))
            acc_vec[V_QKV : V_QKV + 1, 0 : 3 * width] += col_sum(gqkv.astype(F32))
            acc_vec[V_GAIN1 : V_GAIN1 + 1, 0:width] += col_sum(gh1 * n1)
            acc_vec[V_SHIFT1 : V_SHIFT1 + 1, 0:width] += col_sum(gh1)
            ig_s[m, r, :] = (gmix_s[m, r, :] + norm_back(n1, r1, gh1 * v(V_GAIN1))).astype(BF16)
            some(each)
        stores[m].start()
    fold_vectors(acc_vec, flat(p_vec), part)
    vecs.begin()
    todo += stages([vecs])
    some(len(todo))
    for s in fc + [attn, vecs]:
        s.last()
    for s in fc + [attn, vecs]:
        s.finish()
    for store in stores:
        store.wait()


def scatter_call(n, x, gqkv, gmix, wqkv, vec, p_fc1, p_fc2, p_out, gvec, collective_id, tile=512):
    micro, rows, width = x.shape
    height = p_fc1.shape[0] // n
    vmem, hbm = pl.BlockSpec(memory_space=pltpu.VMEM), pl.BlockSpec(memory_space=pl.ANY)
    places = n // 8
    grid = (places, 2, 2, 2)
    scratch = []
    for shape, dtype in [((height, width), BF16)] * 3 + [((16, 128), F32)]:
        scratch += [pltpu.VMEM((places, 2, 2) + shape, dtype)]
        scratch += [pltpu.VMEM((places,) + shape, dtype) for _ in range(5)]
        scratch += [pltpu.VMEM((4, places) + shape, dtype)]
    block = jax.ShapeDtypeStruct((height, width), F32)
    sems = pltpu.SemaphoreType.DMA((4, 6, places))
    return pl.pallas_call(
        functools.partial(scatter_kernel, n, tile),
        in_specs=[hbm] * 3 + [vmem] * 6,
        out_specs=[hbm] + [vmem] * 4,
        out_shape=[jax.ShapeDtypeStruct(x.shape, BF16), block, block, block, jax.ShapeDtypeStruct((16, 128), F32)],
        scratch_shapes=[
            pltpu.VMEM(x.shape, BF16), pltpu.VMEM(gqkv.shape, BF16), pltpu.VMEM(gmix.shape, F32), pltpu.VMEM(x.shape, BF16),
            pltpu.VMEM(x.shape, BF16), pltpu.VMEM((width, 3 * width), F32), pltpu.VMEM(vec.shape, F32),
            pltpu.VMEM(grid + (height, width), BF16), pltpu.VMEM(grid + (16, 128), F32),
            pltpu.SemaphoreType.DMA((3, micro)), pltpu.SemaphoreType.DMA((micro,)), sems, sems,
        ] + scratch,
        compiler_params=pltpu.CompilerParams(
            collective_id=collective_id, has_side_effects=True, vmem_limit_bytes=62 * 2**20),
    )(x, gqkv, gmix, wqkv, vec, p_fc1.reshape(grid + (height, width)), p_fc2.reshape(grid + (height, width)), p_out, gvec)


def finish_kernel(part, ig_in, s_attn, s_fc1, s_fc2, s_vec, ig, g_qkv, g_out, g_fc1, g_fc2, *rest):
    vectors, held, sems = rest[:9], rest[9], rest[10]
    width = s_attn.shape[1]
    micro, rows = held.shape[:2]
    cuts = [(m, pl.ds(h * (rows // 2), rows // 2)) for m in range(micro) for h in range(2)]
    loads = [pltpu.make_async_copy(ig_in.at[c], held.at[c], sems.at[0, i]) for i, c in enumerate(cuts)]
    stores = [pltpu.make_async_copy(held.at[c], ig.at[c], sems.at[1, i]) for i, c in enumerate(cuts)]
    for load in loads:
        load.start()
    for a in range(4):
        own = slice(a * part, (a + 1) * part)
        if a < 3:
            g_qkv[:, a * width : (a + 1) * width] = s_attn[own, :]
        else:
            g_out[...] = s_attn[own, :]
        g_fc1[:, a * width : (a + 1) * width] = s_fc1[own, :]
    g_fc2[...] = s_fc2[0 : 4 * part, :]
    for i in range(8):
        vectors[i][...] = s_vec[i, 0:part]
    vectors[8][...] = s_vec[8, 0 : 4 * part]
    for load, store in zip(loads, stores):
        load.wait()
        store.start()
    for store in stores:
        store.wait()


def finish_call(part, ig, s_attn, s_fc1, s_fc2, s_vec):
    width = s_attn.shape[1]
    vmem, hbm = pl.BlockSpec(memory_space=pltpu.VMEM), pl.BlockSpec(memory_space=pl.ANY)
    shapes = [(part, 3 * width), (part, width), (part, 4 * width), (4 * part, width)] + [(part,)] * 8 + [(4 * part,)]
    return pl.pallas_call(
        functools.partial(finish_kernel, part),
        in_specs=[hbm] + [vmem] * 4,
        out_specs=[hbm] + [vmem] * 13,
        out_shape=[jax.ShapeDtypeStruct(ig.shape, ig.dtype)] + [jax.ShapeDtypeStruct(s, F32) for s in shapes],
        scratch_shapes=[pltpu.VMEM(ig.shape, ig.dtype), pltpu.SemaphoreType.DMA((2, 2 * ig.shape[0]))],
    )(ig, s_attn, s_fc1, s_fc2, s_vec)


def pieces(shard, high):
    part, cols = shard.shape
    folded = shard.reshape(part, 4, cols // 4).transpose(1, 0, 2).reshape(4 * part, cols // 4)
    return jnp.pad(folded, ((0, high - 4 * part), (0, 0)))


def body(inputs, cotangent, w_qkv, w_out, w_fc1, w_fc2, gain1, shift1, q_bias, v_bias, out_bias, gain2, shift2,
         fc1_bias, fc2_bias, image_tokens, image_count):
    me = lax.axis_index("dp")
    n = lax.axis_size("dp")
    part, width = w_out.shape
    hidden = w_fc1.shape[1]
    high = -(-4 * part // 16) * 16
    small = jnp.stack([gain1, shift1, q_bias, v_bias, out_bias, gain2, shift2, fc2_bias])
    small = jnp.concatenate([
        jnp.pad(small, ((0, 0), (0, 128 - part))),
        jnp.pad(fc1_bias[None], ((0, 7), (0, 128 - 4 * part))),
    ])
    attn = pieces(jnp.concatenate([w_qkv, w_out], axis=1), high)
    fc2 = jnp.pad(w_fc2, ((0, high - 4 * part), (0, 0)))
    qkv, wqkv, wout, w1, g_fc2, vec = gather_call(n, inputs, attn, pieces(w_fc1, high), fc2, small, 1)
    w2 = g_fc2.reshape(n, high, width)[:, : 4 * part].reshape(hidden, width)
    meta = jnp.stack([
        lax.dynamic_index_in_dim(image_tokens, me, 1, False), lax.dynamic_index_in_dim(image_count, me, 1, False)
    ], axis=1)
    out, gqkv, gmix, p_fc1, p_fc2, a_out, a_vec = layer_call(
        meta, inputs, cotangent, qkv, wout, w1, w2, vec, n)
    p_fc2 = jnp.pad(p_fc2.reshape(n, 4 * part, width), ((0, 0), (0, high - 4 * part), (0, 0))).reshape(n * high, width)
    ig, s_attn, s_fc1, s_fc2, s_vec = scatter_call(
        n, inputs, gqkv, gmix, wqkv, vec, p_fc1, p_fc2, a_out, a_vec, 2)
    ig, g_qkv, g_out, g_fc1, g_fc2, *v = finish_call(part, ig, s_attn, s_fc1, s_fc2, s_vec)
    return (out, ig, g_qkv, g_out, g_fc1, g_fc2, *v[:7], v[8], v[7])


def solution(mesh):
    big, mat, one = P(None, "dp", None), P("dp", None), P("dp")
    return jax.shard_map(
        body, mesh=mesh,
        in_specs=(big, big) + (mat,) * 4 + (one,) * 9 + (P(), P()),
        out_specs=(big, big) + (mat,) * 4 + (one,) * 9,
        check_vma=False,
    )
```

```python
import functools

import jax
import jax.numpy as jnp
from jax import lax
from jax.experimental import pallas as pl
from jax.experimental.pallas import tpu as pltpu
from jax.sharding import PartitionSpec as P

F32, BF16 = jnp.float32, jnp.bfloat16
MESH = pl.DeviceIdType.MESH

HEADS = 6
EPS = 1e-06
FAR = -1e30
V_GAIN1, V_SHIFT1, V_QKV, V_OUT, V_GAIN2, V_SHIFT2, V_FC1, V_FC2 = range(8)
G_GAIN1, G_SHIFT1, G_QKV, G_OUT, G_GAIN2, G_SHIFT2, G_FC1, G_FC2 = range(8)


def mm(a, b):
    return jnp.dot(a, b, preferred_element_type=F32)

def mm_t(a, b):
    return lax.dot_general(a, b, (((1,), (1,)), ((), ())), preferred_element_type=F32)

def t_mm(a, b):
    return lax.dot_general(a, b, (((0,), (0,)), ((), ())), preferred_element_type=F32)


def norm_rows(v):
    width = v.shape[1]
    off = v - jnp.sum(v, axis=1, keepdims=True) * (1.0 / width)
    inv = lax.rsqrt(jnp.sum(off * off, axis=1, keepdims=True) * (1.0 / width) + EPS)
    return off * inv, inv


def norm_back(n, inv, t):
    width = n.shape[1]
    a = jnp.sum(t, axis=1, keepdims=True) * (1.0 / width)
    b = jnp.sum(t * n, axis=1, keepdims=True) * (1.0 / width)
    return inv * (t - a - n * b)


def col_sum(v):
    return jnp.sum(v, axis=0, keepdims=True)


def images_per_window(length):
    return jnp.where(length <= 128, 2, 1)


def window(meta, w, wq, wk, rows):
    length, count = meta
    group = images_per_window(length)
    lo = w * (length * group)
    hi = jnp.minimum(lo + length * group, length * count)
    base = (lo // 16) * 16
    sq = pl.multiple_of(jnp.minimum(base, rows - wq), 16)
    sk = pl.multiple_of(jnp.minimum(base, rows - wk), 16)
    return lo, hi, length, sq, sk


def seg_of(start, n, lo, hi, length):
    r = start + lax.broadcasted_iota(jnp.int32, (n, 128), 0)
    inside = jnp.logical_and(r >= lo, r < hi)
    return inside, jnp.where(inside, jnp.where(r >= lo + length, 1, 0), 2)


def halves(v):
    left = lax.broadcasted_iota(jnp.int32, v.shape, 1) < 64
    zero = jnp.zeros_like(v)
    return jnp.where(left, v, zero), jnp.where(left, zero, v)


def attend_fwd(meta, qkv_s, o_s, inv_s, e_s, wq, wk, pairs, width):
    rows = qkv_s.shape[0]
    scale = 0.125 * 1.4426950408889634

    def one(w, carry):
        lo, hi, length, sq, sk = window(meta, w, wq, wk, rows)
        in_q, seg_q = seg_of(sq, wq, lo, hi, length)
        _, seg_k = seg_of(sk, wk, lo, hi, length)
        lane_q = lax.broadcasted_iota(jnp.int32, (wq, 128), 1)
        lane_k = lax.broadcasted_iota(jnp.int32, (wk, 128), 1)
        aug_q = jnp.where(jnp.logical_and(lane_q != seg_q, lane_q < 3), 1.0, 0.0).astype(BF16)
        aug_k = jnp.where(lane_k == seg_k, FAR, 0.0).astype(BF16)
        ones0 = jnp.where(lane_k < 64, 1.0, 0.0).astype(BF16)
        ones1 = jnp.where(lane_k < 64, 0.0, 1.0).astype(BF16)
        for p in range(pairs):
            c = 128 * p
            q2 = qkv_s[pl.ds(sq, wq), c : c + 128]
            k0, k1 = halves(qkv_s[pl.ds(sk, wk), width + c : width + c + 128])
            v0, v1 = halves(qkv_s[pl.ds(sk, wk), 2 * width + c : 2 * width + c + 128])
            left = jnp.concatenate([q2, aug_q], axis=1)
            right = jnp.concatenate(
                [jnp.concatenate([k0, aug_k], axis=1), jnp.concatenate([k1, aug_k], axis=1)], axis=0
            )
            s = mm_t(left, right)
            parts = []
            for h in range(2):
                sh = s[:, h * wk : (h + 1) * wk]
                top = jnp.max(sh, axis=1, keepdims=True)
                parts.append(jnp.exp2((sh - top) * scale).astype(BF16))
            e = jnp.concatenate(parts, axis=1)
            e_s[w * pairs + p] = e
            vals = jnp.concatenate(
                [jnp.concatenate([v0, ones0], axis=1), jnp.concatenate([v1, ones1], axis=1)], axis=0
            )
            both = mm(e, vals)
            inv = 1.0 / both[:, 128:]
            o = (both[:, :128] * inv).astype(BF16)
            dst = (pl.ds(sq, wq), pl.ds(c, 128))
            o_s[dst] = jnp.where(in_q, o, o_s[dst])
            inv_s[dst] = jnp.where(in_q, inv, inv_s[dst])
        return carry

    length, count = meta
    lax.fori_loop(0, jnp.where(length <= 128, (count + 1) // 2, count), one, 0)


def attend_bwd(meta, qkv_s, o_s, inv_s, e_s, go_s, gqkv_s, wq, wk, pairs, width):
    rows = qkv_s.shape[0]

    def one(w, carry):
        lo, hi, length, sq, sk = window(meta, w, wq, wk, rows)
        in_q, _ = seg_of(sq, wq, lo, hi, length)
        in_k, _ = seg_of(sk, wk, lo, hi, length)
        for p in range(pairs):
            c = 128 * p
            e = e_s[w * pairs + p]
            q0, q1 = halves(qkv_s[pl.ds(sq, wq), c : c + 128])
            k0, k1 = halves(qkv_s[pl.ds(sk, wk), width + c : width + c + 128])
            v0, v1 = halves(qkv_s[pl.ds(sk, wk), 2 * width + c : 2 * width + c + 128])
            dst_q = (pl.ds(sq, wq), pl.ds(c, 128))
            go = (go_s[dst_q].astype(F32) * inv_s[dst_q]).astype(BF16)
            prod0, prod1 = halves(go.astype(F32) * o_s[dst_q].astype(F32))
            d = (jnp.sum(prod0, axis=1, keepdims=True), jnp.sum(prod1, axis=1, keepdims=True))
            gp = mm_t(go, jnp.concatenate([v0, v1], axis=0))
            gs = []
            for h in range(2):
                sl = slice(h * wk, (h + 1) * wk)
                gs.append((e[:, sl].astype(F32) * (gp[:, sl] - d[h])).astype(BF16))
            gq = mm(jnp.concatenate(gs, axis=1), jnp.concatenate([k0, k1], axis=0)) * 0.125
            gk = t_mm(jnp.concatenate(gs, axis=0), jnp.concatenate([q0, q1], axis=0)) * 0.125
            gv = t_mm(
                jnp.concatenate([e[:, :wk], e[:, wk:]], axis=0), jnp.concatenate(halves(go), axis=0)
            )
            gqkv_s[dst_q] = jnp.where(in_q, gq.astype(BF16), gqkv_s[dst_q])
            dst_k = (pl.ds(sk, wk), pl.ds(width + c, 128))
            gqkv_s[dst_k] = jnp.where(in_k, gk.astype(BF16), gqkv_s[dst_k])
            dst_v = (pl.ds(sk, wk), pl.ds(2 * width + c, 128))
            gqkv_s[dst_v] = jnp.where(in_k, gv.astype(BF16), gqkv_s[dst_v])
        return carry

    length, count = meta
    lax.fori_loop(0, jnp.where(length <= 128, (count + 1) // 2, count), one, 0)


WIDE = (352, 384)
NARROW = (224, 256)


def fold_matrix(part, count, high):
    rows, cols = 4 * count * part, count * high
    r = lax.broadcasted_iota(jnp.int32, (rows, cols), 0).astype(F32)
    c = lax.broadcasted_iota(jnp.int32, (rows, cols), 1).astype(F32)
    block = jnp.floor((c + 0.5) * (1.0 / high))
    inner = c - block * high
    piece = jnp.floor((inner + 0.5) * (1.0 / part))
    want = piece * (count * part) + block * part + (inner - piece * part)
    return jnp.where(jnp.logical_and(want == r, piece < 4), 1.0, 0.0).astype(BF16)


def unfold(blocks, dsts, part, high):
    count = 96 // part
    pick = fold_matrix(part, count, high)
    for t in range(len(blocks) // count):
        group = jnp.concatenate([blocks[j][...] for j in range(t * count, (t + 1) * count)], axis=0)
        full = mm(pick, group).astype(BF16)
        for a in range(4):
            dsts[a][96 * t : 96 * (t + 1), :] = full[96 * a : 96 * (a + 1), :]


def fold(srcs, blocks, part, high):
    count = 96 // part
    pick = fold_matrix(part, count, high)
    for t in range(len(blocks) // count):
        rows = slice(96 * t, 96 * (t + 1))
        four = jnp.concatenate([s[rows, :].astype(BF16) for s in srcs], axis=0)
        full = t_mm(pick, four).astype(BF16)
        for i in range(count):
            blocks[t * count + i][...] = full[i * high : (i + 1) * high, :]


def unfold_vectors(blocks, vec, part):
    n = len(blocks)
    width = part * n
    lane = lax.broadcasted_iota(jnp.int32, (8, 128), 1)
    total = jnp.zeros((8, width), F32)
    wide = jnp.zeros((8, 4 * width), F32)
    for j in range(n):
        pair = blocks[j][...].astype(F32)
        one = jnp.where(lane < part, pair[0:8], 0.0)
        one = jnp.concatenate([one, jnp.zeros((8, width - 128), F32)], axis=1)
        total = total + pltpu.roll(one, j * part, 1)
        one = jnp.where(lane < 4 * part, pair[8:16], 0.0)
        one = jnp.concatenate([one, jnp.zeros((8, 4 * width - 128), F32)], axis=1)
        wide = wide + pltpu.roll(one, 4 * j * part, 1)
    vec[...] = jnp.zeros_like(vec)
    for i, (row, col) in enumerate(VECTORS):
        vec[row : row + 1, col * width : (col + 1) * width] = total[i : i + 1]
    vec[V_FC1 : V_FC1 + 1, :] = wide[0:1]


def fold_vectors(vec, blocks, part):
    n = len(blocks)
    width = part * n
    eight = jnp.concatenate(
        [vec[row : row + 1, col * width : (col + 1) * width] for row, col in VECTORS], axis=0
    )
    wide = jnp.broadcast_to(vec[V_FC1 : V_FC1 + 1, :], (8, 4 * width))
    for j in range(n):
        blocks[j][0:8, :] = pltpu.roll(eight, (width - j * part) % width, 1)[:, :128]
        blocks[j][8:16, :] = pltpu.roll(wide, (4 * width - 4 * j * part) % (4 * width), 1)[:, :128]


VECTORS = ((V_GAIN1, 0), (V_SHIFT1, 0), (V_QKV, 0), (V_QKV, 2), (V_OUT, 0), (V_GAIN2, 0), (V_SHIFT2, 0), (V_FC2, 0))


def layer_kernel(
    tokens, counts, x_ref, cot_ref, qkv_ref, wout, w1, w2, vec,
    out_ref, gqkv_ref, gmix_ref, p_fc1, p_fc2, a_out, a_vec,
    a_fc1, a_fc2, o_s, inv_s, e1_s, e2_s, h2_s, act_s, gpre_s, gy_s, gb_s, go_s,
    part, phases=("af", "mlp", "wg", "ab"), tile=512, chunk=256,
):
    m = pl.program_id(0)
    me = lax.axis_index("dp")
    rows, width = x_ref.shape[1], x_ref.shape[2]
    hidden = w1.shape[1]
    pairs = HEADS // 2
    length, count = tokens[m, me], counts[m, me]
    meta = (length, count)
    total = length * count
    qkv_s, gqkv_s, gmix_s = qkv_ref.at[0], gqkv_ref.at[0], gmix_ref.at[0]

    @pl.when(m == 0)
    def _():
        for ref in (a_out, a_fc1, a_fc2, a_vec):
            ref[...] = jnp.zeros_like(ref)

    def v(i, n=width):
        return vec[i : i + 1, 0:n]

    def add_vec(i, val):
        a_vec[i : i + 1, 0 : val.shape[1]] += val

    o_s[...] = qkv_s[:, 2 * width :]

    if "af" in phases:
        fwd = functools.partial(attend_fwd, meta, qkv_s, o_s, inv_s)
        @pl.when(length > 256)
        def _():
            fwd(e1_s, *WIDE, pairs, width)
        @pl.when(length <= 256)
        def _():
            fwd(e2_s, *NARROW, pairs, width)

    if "mlp" in phases:
        def mlp(i, c):
            r = pl.ds(pl.multiple_of(i * tile, tile), tile)
            valid = (i * tile + lax.broadcasted_iota(jnp.int32, (tile, 1), 0)) < total
            mixed = x_ref[0, r, :].astype(F32) + mm(o_s[r, :], wout[...]) + v(V_OUT)
            n2, r2 = norm_rows(mixed)
            h2 = (n2 * v(V_GAIN2) + v(V_SHIFT2)).astype(BF16)
            h2_s[r, :] = h2
            gy = jnp.where(valid, cot_ref[0, r, :].astype(F32), 0.0)
            gyl = gy.astype(BF16)
            gy_s[r, :] = gyl
            add_vec(G_FC2, col_sum(gy))
            for f in range(0, hidden, chunk):
                fs = slice(f, f + chunk)
                pre = mm(h2, w1[:, fs]) + vec[V_FC1 : V_FC1 + 1, fs]
                cdf = 0.5 * lax.erf(pre * 0.7071067811865476) + 0.5
                act_s[r, fs] = (pre * cdf).astype(BF16)
                slope = cdf + pre * (jnp.exp(pre * pre * -0.5) * 0.3989422804014327)
                gpre = (slope * mm_t(gyl, w2[fs, :])).astype(BF16)
                gpre_s[r, fs] = gpre
                a_vec[G_FC1 : G_FC1 + 1, fs] += col_sum(gpre.astype(F32))
            final = mixed + mm(act_s[r, :], w2[...]) + v(V_FC2)
            out_ref[0, r, :] = jnp.where(valid, final, 0.0).astype(BF16)
            gh2 = mm_t(gpre_s[r, :], w1[...])
            add_vec(G_GAIN2, col_sum(gh2 * n2))
            add_vec(G_SHIFT2, col_sum(gh2))
            gmix = gy + norm_back(n2, r2, gh2 * v(V_GAIN2))
            gmix_s[r, :] = gmix
            gb = gmix.astype(BF16)
            gb_s[r, :] = gb
            add_vec(G_OUT, col_sum(gb.astype(F32)))
            go_s[r, :] = mm_t(gb, wout[...]).astype(BF16)
            return c
        lax.fori_loop(0, rows // tile, mlp, 0)

    if "wg" in phases:
        a_fc1[...] += t_mm(h2_s[...], gpre_s[...])
        a_fc2[...] += t_mm(act_s[...], gy_s[...])
        a_out[...] += t_mm(o_s[...], gb_s[...])

    gqkv_s[:, : 2 * width] = jnp.zeros((rows, 2 * width), BF16)
    gqkv_s[:, 2 * width :] = go_s[...]

    if "ab" in phases:
        bwd = functools.partial(attend_bwd, meta, qkv_s, o_s, inv_s)
        @pl.when(length > 256)
        def _():
            bwd(e1_s, go_s, gqkv_s, *WIDE, pairs, width)
        @pl.when(length <= 256)
        def _():
            bwd(e2_s, go_s, gqkv_s, *NARROW, pairs, width)

    @pl.when(m == pl.num_programs(0) - 1)
    def _():
        high = p_fc1.shape[0] // (width // part)
        blocks = [p_fc1.at[j * high : (j + 1) * high, :] for j in range(width // part)]
        fold([a_fc1.at[:, i * width : (i + 1) * width] for i in range(4)], blocks, part, high)
        p_fc2[...] = a_fc2[...].astype(BF16)


def layer_call(tokens, counts, x, cot, qkv, wout, w1, w2, vec, n, **kw):
    micro, rows, width = x.shape
    hidden = w2.shape[0]
    part = width // n
    high = -(-4 * part // 16) * 16
    def per_step(cols):
        return pl.BlockSpec((1, rows, cols), lambda m: (m, 0, 0))
    def whole(shape):
        return pl.BlockSpec(shape, lambda m: (0, 0), pipeline_mode=pl.Buffered(1))
    bf = lambda n: pltpu.VMEM((rows, n), BF16)
    outs = [(x.shape, BF16), ((micro, rows, 3 * width), BF16), (x.shape, F32)]
    kept = [((n * high, width), BF16), ((hidden, width), BF16), ((width, width), F32), (vec.shape, F32)]
    return pl.pallas_call(
        functools.partial(layer_kernel, part=part, **kw),
        grid=(micro,),
        in_specs=[pl.BlockSpec(memory_space=pltpu.SMEM)] * 2 + [per_step(width), per_step(width), per_step(3 * width)]
        + [whole(a.shape) for a in (wout, w1, w2, vec)],
        out_specs=[per_step(s[2]) for s, _ in outs] + [whole(s) for s, _ in kept],
        out_shape=[jax.ShapeDtypeStruct(s, d) for s, d in outs + kept],
        scratch_shapes=[
            pltpu.VMEM((width, hidden), F32), pltpu.VMEM((hidden, width), F32),
            bf(width), pltpu.VMEM((rows, width), F32),
            pltpu.VMEM((9, 352, 768), BF16), pltpu.VMEM((15, 224, 512), BF16),
            bf(width), bf(hidden), bf(hidden), bf(width), bf(width), bf(width),
        ],
        compiler_params=pltpu.CompilerParams(vmem_limit_bytes=64 * 2**20 - 2**17),
    )(tokens, counts, x, cot, qkv, wout, w1, w2, vec)


def bit_of(me, b):
    return (me // (1 << b)) % 2


class Place:
    def __init__(self, n):
        self.me = lax.axis_index("dp")
        self.count = n // 8
        self.z, self.y, self.x, self.c = self.me // 8, bit_of(self.me, 2), bit_of(self.me, 1), bit_of(self.me, 0)
        self.over_y = self.me + 4 * (1 - 2 * self.y)
        self.over_x = self.me + 2 * (1 - 2 * self.x)
        self.twin = self.me + (1 - 2 * self.c)
        self.steps = sorted(range(1, self.count), key=lambda k: min(k, self.count - k))

    def ahead(self, k):
        return (self.z + k) % self.count

    def behind(self, k):
        return (self.z + self.count - k) % self.count

    def at(self, z):
        return self.me + 8 * (z - self.z)

    def meet(self):
        barrier = pltpu.get_barrier_semaphore()
        others = [self.over_y, self.over_x, self.twin] + [self.at(self.ahead(k)) for k in range(1, self.count)]
        for device in others:
            pl.semaphore_signal(barrier, inc=1, device_id=(device,), device_id_type=MESH)
        pl.semaphore_wait(barrier, len(others))


LINE, ALONG_X, ALONG_Y, DIAG_X, DIAG_Y, TWIN = range(6)


class Wire:
    def __init__(self, place, cut, send, recv):
        self.place, self.cut, self.send, self.recv, self.started = place, cut, send, recv, []

    def copy(self, kind, k, src, dst, device):
        return pltpu.make_async_remote_copy(
            src_ref=src, dst_ref=dst, send_sem=self.send.at[kind, k], recv_sem=self.recv.at[kind, k],
            device_id=(device,), device_id_type=MESH)

    def push(self, kind, k, src, dst, device):
        copy = self.copy(kind, k, src, dst, device)
        copy.start()
        self.started.append(copy)

    def arrive(self, kind, k, dst):
        self.copy(kind, k, dst, dst, self.place.twin).wait_recv()

    def finish(self):
        for copy in self.started:
            copy.wait_send()

    def columns(self, k, width):
        if self.cut is None:
            return slice(0, width), None
        cut = 128 if (k + self.cut) % 2 else width - 128
        return slice(0, cut), slice(cut, width)


class Gather(Wire):
    def __init__(self, place, ref, cut, send, recv):
        super().__init__(place, cut, send, recv)
        self.ref = ref

    def block(self, k, over_y, over_x, cols=slice(None)):
        p = self.place
        y = 1 - p.y if over_y else p.y
        x = 1 - p.x if over_x else p.x
        return self.ref.at[p.behind(k), y, x, p.c, :, cols]

    def same(self, kind, k, view, device):
        self.push(kind, k, view, view, device)

    def begin(self):
        p = self.place
        for k in p.steps:
            self.same(LINE, k, self.block(0, False, False), p.at(p.ahead(k)))

    def line(self, k):
        view = self.block(k, False, False)
        if k:
            self.arrive(LINE, k, view)
        self.same(ALONG_X, k, view, self.place.over_x)
        self.same(ALONG_Y, k, view, self.place.over_y)

    def plane(self, k):
        first, second = self.columns(k, self.ref.shape[-1])
        self.arrive(ALONG_X, k, self.block(k, False, True))
        self.same(DIAG_Y, k, self.block(k, False, True, first), self.place.over_y)
        self.arrive(ALONG_Y, k, self.block(k, True, False))
        if second is not None:
            self.same(DIAG_X, k, self.block(k, True, False, second), self.place.over_x)

    def corner(self, k):
        first, second = self.columns(k, self.ref.shape[-1])
        self.arrive(DIAG_Y, k, self.block(k, True, True, first))
        if second is not None:
            self.arrive(DIAG_X, k, self.block(k, True, True, second))
        p = self.place
        self.same(TWIN, k, self.ref.at[p.behind(k), :, :, p.c], p.twin)

    def last(self):
        p = self.place
        for k in range(p.count):
            self.arrive(TWIN, k, self.ref.at[p.behind(k), :, :, 1 - p.c])


class Scatter(Wire):
    def __init__(self, place, src, cut, scratch, out, send, recv):
        super().__init__(place, cut, send, recv)
        self.src, self.out = src, out
        self.twins, self.diag_x, self.diag_y, self.from_x, self.from_y, self.lines, self.sums = scratch

    def half(self, k, y, x):
        p = self.place
        z = p.ahead(k)
        return self.src[z, y, x, p.c].astype(F32) + self.twins[z, y, x].astype(F32)

    def begin(self):
        p = self.place
        for k in p.steps + [0]:
            z = p.ahead(k)
            self.push(TWIN, k, self.src.at[z, :, :, 1 - p.c], self.twins.at[z], p.twin)

    def corner(self, k):
        p = self.place
        self.arrive(TWIN, k, self.twins.at[p.ahead(k)])
        first, second = self.columns(k, self.src.shape[-1])
        held = self.sums.at[0, k]
        held[...] = self.half(k, 1 - p.y, 1 - p.x).astype(held.dtype)
        self.push(DIAG_Y, k, held.at[:, first], self.diag_x.at[k, :, first], p.over_y)
        if second is not None:
            self.push(DIAG_X, k, held.at[:, second], self.diag_y.at[k, :, second], p.over_x)

    def plane(self, k):
        p = self.place
        first, second = self.columns(k, self.src.shape[-1])
        self.arrive(DIAG_Y, k, self.diag_x.at[k, :, first])
        held = self.sums.at[1, k]
        total = self.half(k, p.y, 1 - p.x)
        held[:, first] = (total[:, first] + self.diag_x[k, :, first].astype(F32)).astype(held.dtype)
        if second is not None:
            held[:, second] = total[:, second].astype(held.dtype)
        self.push(ALONG_X, k, held, self.from_x.at[k], p.over_x)
        held = self.sums.at[2, k]
        total = self.half(k, 1 - p.y, p.x)
        if second is None:
            held[...] = total.astype(held.dtype)
        else:
            self.arrive(DIAG_X, k, self.diag_y.at[k, :, second])
            held[:, first] = total[:, first].astype(held.dtype)
            held[:, second] = (total[:, second] + self.diag_y[k, :, second].astype(F32)).astype(held.dtype)
        self.push(ALONG_Y, k, held, self.from_y.at[k], p.over_y)

    def line(self, k):
        p = self.place
        self.arrive(ALONG_X, k, self.from_x.at[k])
        self.arrive(ALONG_Y, k, self.from_y.at[k])
        total = self.half(k, p.y, p.x) + self.from_x[k].astype(F32) + self.from_y[k].astype(F32)
        if k == 0:
            self.out[...] = total
            return
        held = self.sums.at[3, k]
        held[...] = total.astype(held.dtype)
        self.push(LINE, k, held, self.lines.at[k], p.at(p.ahead(k)))

    def last(self):
        total = self.out[...]
        for k in self.place.steps:
            self.arrive(LINE, k, self.lines.at[k])
            total = total + self.lines[k].astype(F32)
        self.out[...] = total


def gather_kernel(
    n, tile, x_ref, w_qkv, w_out, w_fc1, w_fc2, *refs,
):
    small = refs[:9]
    qkv_ref, wqkv, wout, w1, g_fc2, vec, x_s, qkv_s, g_attn, g_fc1, g_vec, pad, pad_vec, x_sem, qkv_sem, send, recv = refs[9:]
    place = Place(n)
    micro, rows, width = x_s.shape
    part = width // n
    height = g_fc1.shape[-2]
    loads = [pltpu.make_async_copy(x_ref.at[m], x_s.at[m], x_sem.at[m]) for m in range(micro)]
    for load in loads:
        load.start()
    own = (place.z, place.y, place.x, place.c)
    if height > 4 * part:
        pad[...] = jnp.zeros_like(pad)
    pad_vec[...] = jnp.zeros_like(pad_vec)
    for i in range(8):
        pad_vec[i : i + 1, 0:part] = small[i][...].astype(F32).reshape(1, part)
    pad_vec[8:9, 0 : 4 * part] = small[8][...].astype(F32).reshape(1, 4 * part)
    g_vec[own] = pad_vec[...].astype(BF16)
    def fold_own(dst, four):
        for a, piece in enumerate(four):
            pad[a * part : (a + 1) * part, :] = piece.astype(F32)
        dst[own] = pad[...].astype(BF16)
    fold_own(g_attn, [w_qkv[:, a * width : (a + 1) * width] for a in range(3)] + [w_out[...]])
    fold_own(g_fc1, [w_fc1[:, a * width : (a + 1) * width] for a in range(4)])
    if height > 4 * part:
        fold_own(g_fc2, [w_fc2[a * part : (a + 1) * part, :] for a in range(4)])
    else:
        g_fc2[own] = w_fc2[...]
    place.meet()

    refs = (g_vec, g_attn, g_fc1, g_fc2)
    parts = [Gather(place, ref, cut, send.at[i], recv.at[i]) for i, (ref, cut) in enumerate(zip(refs, (None, 0, 1, 0)))]
    urgent, rest = parts[:2], parts[2:]
    order = [0] + place.steps
    todo = [(p, "line", k) for k in order for p in rest]
    todo += [(p, "plane", k) for k in order for p in rest]
    todo += [(p, "corner", k) for k in order for p in rest]

    def some(count):
        for p, stage, k in todo[:count]:
            getattr(p, stage)(k)
        del todo[:count]

    for p in urgent:
        p.begin()
    for p in urgent:
        p.line(0)
    for p in rest:
        p.begin()
    for k in place.steps:
        for p in urgent:
            p.line(k)
    for k in order:
        for p in urgent:
            p.plane(k)
        some(2)
    for k in order:
        for p in urgent:
            p.corner(k)
        some(2)
    for p in urgent:
        p.last()
    flat = lambda ref: [ref.at[j // 8, (j // 4) % 2, (j // 2) % 2, j % 2] for j in range(n)]
    unfold_vectors(flat(g_vec), vec, part)
    unfold(flat(g_attn), [wqkv.at[:, 0:width], wqkv.at[:, width : 2 * width], wqkv.at[:, 2 * width :], wout], part, height)

    def qkv_part(m, i):
        r = pl.ds(i * tile, tile)
        n1, _ = norm_rows(x_s[m, r, :].astype(F32))
        h1 = (n1 * vec[V_GAIN1 : V_GAIN1 + 1, 0:width] + vec[V_SHIFT1 : V_SHIFT1 + 1, 0:width]).astype(BF16)
        qkv_s[m, r, :] = (mm(h1, wqkv[...]) + vec[V_QKV : V_QKV + 1, 0 : 3 * width]).astype(BF16)

    stores = [pltpu.make_async_copy(qkv_s.at[m], qkv_ref.at[m], qkv_sem.at[m]) for m in range(micro)]
    turns = micro * (rows // tile)
    each = -(-len(todo) // max(turns, 1))
    for m in range(micro):
        loads[m].wait()
        for i in range(rows // tile):
            qkv_part(m, i)
            some(each)
        stores[m].start()
    some(len(todo))
    rest[0].last()
    unfold(flat(g_fc1), [w1.at[:, i * width : (i + 1) * width] for i in range(4)], part, height)
    rest[1].last()
    for p in parts:
        p.finish()
    for store in stores:
        store.wait()


def gather_call(n, x, w_qkv, w_out, w_fc1, w_fc2, small, collective_id, tile=512):
    micro, rows, width = x.shape
    height = -(-4 * w_out.shape[0] // 16) * 16
    vmem, hbm = pl.BlockSpec(memory_space=pltpu.VMEM), pl.BlockSpec(memory_space=pl.ANY)
    grid = (n // 8, 2, 2, 2)
    sems = pltpu.SemaphoreType.DMA((4, 6, n // 8))
    block = (height, width)
    shapes = [((micro, rows, 3 * width), BF16), ((width, 3 * width), BF16), ((width, width), BF16),
              ((width, 4 * width), BF16), (grid + block, BF16), ((8, 4 * width), F32)]
    return pl.pallas_call(
        functools.partial(gather_kernel, n, tile),
        in_specs=[hbm] + [vmem] * (4 + len(small)),
        out_specs=[hbm] + [vmem] * 5,
        out_shape=[jax.ShapeDtypeStruct(s, d) for s, d in shapes],
        scratch_shapes=[
            pltpu.VMEM(x.shape, BF16), pltpu.VMEM((micro, rows, 3 * width), BF16),
            pltpu.VMEM(grid + block, BF16), pltpu.VMEM(grid + block, BF16), pltpu.VMEM(grid + (16, 128), BF16),
            pltpu.VMEM(block, F32), pltpu.VMEM((16, 128), F32),
            pltpu.SemaphoreType.DMA((micro,)), pltpu.SemaphoreType.DMA((micro,)), sems, sems,
        ],
        compiler_params=pltpu.CompilerParams(
            collective_id=collective_id, has_side_effects=True, vmem_limit_bytes=60 * 2**20),
    )(x, w_qkv, w_out, w_fc1, w_fc2, *small)


def scatter_kernel(
    n, tile, x_ref, gqkv_ref, gmix_ref, wqkv, vec, p_fc1, p_fc2, p_out, gvec,
    ig_ref, o_attn, o_fc1, o_fc2, o_vec,
    x_s, gqkv_s, gmix_s, ig_s, h1_s, acc, acc_vec, p_attn, p_vec, in_sem, out_sem, send, recv, *rest,
):
    place = Place(n)
    micro, rows, width = x_s.shape
    part = width // n
    height = p_fc1.shape[-2]
    loads = []
    for m in range(micro):
        pairs = ((x_ref, x_s), (gqkv_ref, gqkv_s), (gmix_ref, gmix_s))
        loads.append([pltpu.make_async_copy(a.at[m], b.at[m], in_sem.at[i, m]) for i, (a, b) in enumerate(pairs)])
        for load in loads[m]:
            load.start()
    place.meet()

    def stream(i, src, cut, out):
        return Scatter(place, src, cut, rest[7 * i : 7 * i + 7], out, send.at[i], recv.at[i])
    fc = [stream(0, p_fc1, 0, o_fc1), stream(1, p_fc2, 1, o_fc2)]
    attn, vecs = stream(2, p_attn, 0, o_attn), stream(3, p_vec, None, o_vec)
    order = place.steps + [0]
    def stages(streams):
        return [(s, stage, k) for stage in ("corner", "plane", "line") for k in order for s in streams]
    todo = stages(fc)

    def some(count):
        for s, stage, k in todo[:count]:
            getattr(s, stage)(k)
        del todo[:count]

    for s in fc:
        s.begin()

    def v(i, cols=width):
        return vec[i : i + 1, 0:cols]

    acc_vec[...] = gvec[...]
    for m in range(micro):
        for load in loads[m][:2]:
            load.wait()
        for i in range(rows // tile):
            r = pl.ds(i * tile, tile)
            n1, _ = norm_rows(x_s[m, r, :].astype(F32))
            h1_s[m, r, :] = (n1 * v(V_GAIN1) + v(V_SHIFT1)).astype(BF16)
        g = t_mm(h1_s[m], gqkv_s[m])
        acc[...] = g if m == 0 else acc[...] + g
        some(len(order) * 2 if m == 0 else len(order))
    flat = lambda ref: [ref.at[j // 8, (j // 4) % 2, (j // 2) % 2, j % 2] for j in range(n)]
    fold([acc.at[:, 0:width], acc.at[:, width : 2 * width], acc.at[:, 2 * width :], p_out], flat(p_attn), part, height)
    attn.begin()
    late = stages([attn])
    todo = [t for pair in zip(todo, late) for t in pair] + todo[len(late) :] + late[len(todo) :]

    stores = [pltpu.make_async_copy(ig_s.at[m], ig_ref.at[m], out_sem.at[m]) for m in range(micro)]
    turns = micro * (rows // tile)
    each = -(-len(todo) // turns)
    for m in range(micro):
        loads[m][2].wait()
        for i in range(rows // tile):
            r = pl.ds(i * tile, tile)
            gqkv = gqkv_s[m, r, :]
            gh1 = mm_t(gqkv, wqkv[...])
            n1, r1 = norm_rows(x_s[m, r, :].astype(F32))
            acc_vec[V_QKV : V_QKV + 1, 0 : 3 * width] += col_sum(gqkv.astype(F32))
            acc_vec[V_GAIN1 : V_GAIN1 + 1, 0:width] += col_sum(gh1 * n1)
            acc_vec[V_SHIFT1 : V_SHIFT1 + 1, 0:width] += col_sum(gh1)
            ig_s[m, r, :] = (gmix_s[m, r, :] + norm_back(n1, r1, gh1 * v(V_GAIN1))).astype(BF16)
            some(each)
        stores[m].start()
    fold_vectors(acc_vec, flat(p_vec), part)
    vecs.begin()
    todo += stages([vecs])
    some(len(todo))
    for s in fc + [attn, vecs]:
        s.last()
    for s in fc + [attn, vecs]:
        s.finish()
    for store in stores:
        store.wait()


def scatter_call(n, x, gqkv, gmix, wqkv, vec, p_fc1, p_fc2, p_out, gvec, collective_id, tile=512):
    micro, rows, width = x.shape
    height = p_fc1.shape[0] // n
    vmem, hbm = pl.BlockSpec(memory_space=pltpu.VMEM), pl.BlockSpec(memory_space=pl.ANY)
    places = n // 8
    grid = (places, 2, 2, 2)
    scratch = []
    for shape, dtype in [((height, width), BF16)] * 3 + [((16, 128), F32)]:
        scratch += [pltpu.VMEM((places, 2, 2) + shape, dtype)]
        scratch += [pltpu.VMEM((places,) + shape, dtype) for _ in range(5)]
        scratch += [pltpu.VMEM((4, places) + shape, dtype)]
    block = jax.ShapeDtypeStruct((height, width), F32)
    sems = pltpu.SemaphoreType.DMA((4, 6, places))
    return pl.pallas_call(
        functools.partial(scatter_kernel, n, tile),
        in_specs=[hbm] * 3 + [vmem] * 6,
        out_specs=[hbm] + [vmem] * 4,
        out_shape=[jax.ShapeDtypeStruct(x.shape, BF16), block, block, block, jax.ShapeDtypeStruct((16, 128), F32)],
        scratch_shapes=[
            pltpu.VMEM(x.shape, BF16), pltpu.VMEM(gqkv.shape, BF16), pltpu.VMEM(gmix.shape, F32), pltpu.VMEM(x.shape, BF16),
            pltpu.VMEM(x.shape, BF16), pltpu.VMEM((width, 3 * width), F32), pltpu.VMEM(vec.shape, F32),
            pltpu.VMEM(grid + (height, width), BF16), pltpu.VMEM(grid + (16, 128), F32),
            pltpu.SemaphoreType.DMA((3, micro)), pltpu.SemaphoreType.DMA((micro,)), sems, sems,
        ] + scratch,
        compiler_params=pltpu.CompilerParams(
            collective_id=collective_id, has_side_effects=True, vmem_limit_bytes=62 * 2**20),
    )(x, gqkv, gmix, wqkv, vec, p_fc1.reshape(grid + (height, width)), p_fc2.reshape(grid + (height, width)), p_out, gvec)


def finish_kernel(part, ig_in, s_attn, s_fc1, s_fc2, s_vec, ig, g_qkv, g_out, g_fc1, g_fc2, *rest):
    vectors, held, sems = rest[:9], rest[9], rest[10]
    width = s_attn.shape[1]
    micro, rows = held.shape[:2]
    cuts = [(m, pl.ds(h * (rows // 2), rows // 2)) for m in range(micro) for h in range(2)]
    loads = [pltpu.make_async_copy(ig_in.at[c], held.at[c], sems.at[0, i]) for i, c in enumerate(cuts)]
    stores = [pltpu.make_async_copy(held.at[c], ig.at[c], sems.at[1, i]) for i, c in enumerate(cuts)]
    for load in loads:
        load.start()
    for a in range(4):
        own = slice(a * part, (a + 1) * part)
        if a < 3:
            g_qkv[:, a * width : (a + 1) * width] = s_attn[own, :]
        else:
            g_out[...] = s_attn[own, :]
        g_fc1[:, a * width : (a + 1) * width] = s_fc1[own, :]
    g_fc2[...] = s_fc2[0 : 4 * part, :]
    for i in range(8):
        vectors[i][...] = s_vec[i, 0:part]
    vectors[8][...] = s_vec[8, 0 : 4 * part]
    for load, store in zip(loads, stores):
        load.wait()
        store.start()
    for store in stores:
        store.wait()


def finish_call(part, ig, s_attn, s_fc1, s_fc2, s_vec):
    width = s_attn.shape[1]
    vmem, hbm = pl.BlockSpec(memory_space=pltpu.VMEM), pl.BlockSpec(memory_space=pl.ANY)
    shapes = [(part, 3 * width), (part, width), (part, 4 * width), (4 * part, width)] + [(part,)] * 8 + [(4 * part,)]
    return pl.pallas_call(
        functools.partial(finish_kernel, part),
        in_specs=[hbm] + [vmem] * 4,
        out_specs=[hbm] + [vmem] * 13,
        out_shape=[jax.ShapeDtypeStruct(ig.shape, ig.dtype)] + [jax.ShapeDtypeStruct(s, F32) for s in shapes],
        scratch_shapes=[pltpu.VMEM(ig.shape, ig.dtype), pltpu.SemaphoreType.DMA((2, 2 * ig.shape[0]))],
    )(ig, s_attn, s_fc1, s_fc2, s_vec)


def body(inputs, cotangent, w_qkv, w_out, w_fc1, w_fc2, gain1, shift1, q_bias, v_bias, out_bias, gain2, shift2,
         fc1_bias, fc2_bias, image_tokens, image_count):
    n = lax.axis_size("dp")
    part, width = w_out.shape
    hidden = w_fc1.shape[1]
    high = -(-4 * part // 16) * 16
    small = (gain1, shift1, q_bias, v_bias, out_bias, gain2, shift2, fc2_bias, fc1_bias)
    qkv, wqkv, wout, w1, g_fc2, vec = gather_call(n, inputs, w_qkv, w_out, w_fc1, w_fc2, small, 1)
    w2 = g_fc2.reshape(n, high, width)[:, : 4 * part].reshape(hidden, width)
    out, gqkv, gmix, p_fc1, p_fc2, a_out, a_vec = layer_call(
        image_tokens, image_count, inputs, cotangent, qkv, wout, w1, w2, vec, n)
    p_fc2 = jnp.pad(p_fc2.reshape(n, 4 * part, width), ((0, 0), (0, high - 4 * part), (0, 0))).reshape(n * high, width)
    ig, s_attn, s_fc1, s_fc2, s_vec = scatter_call(
        n, inputs, gqkv, gmix, wqkv, vec, p_fc1, p_fc2, a_out, a_vec, 2)
    ig, g_qkv, g_out, g_fc1, g_fc2, *v = finish_call(part, ig, s_attn, s_fc1, s_fc2, s_vec)
    return (out, ig, g_qkv, g_out, g_fc1, g_fc2, *v[:7], v[8], v[7])


def solution(mesh):
    big, mat, one = P(None, "dp", None), P("dp", None), P("dp")
    return jax.shard_map(
        body, mesh=mesh,
        in_specs=(big, big) + (mat,) * 4 + (one,) * 9 + (P(), P()),
        out_specs=(big, big) + (mat,) * 4 + (one,) * 9,
        check_vma=False,
    )
```

```python
import functools

import jax
import jax.numpy as jnp
from jax import lax
from jax.experimental import pallas as pl
from jax.experimental.pallas import tpu as pltpu
from jax.sharding import PartitionSpec as P

F32, BF16 = jnp.float32, jnp.bfloat16
MESH = pl.DeviceIdType.MESH

HEADS = 6
EPS = 1e-06
FAR = -1e30
V_GAIN1, V_SHIFT1, V_QKV, V_OUT, V_GAIN2, V_SHIFT2, V_FC1, V_FC2 = range(8)
G_GAIN1, G_SHIFT1, G_QKV, G_OUT, G_GAIN2, G_SHIFT2, G_FC1, G_FC2 = range(8)


def mm(a, b):
    return jnp.dot(a, b, preferred_element_type=F32)

def mm_t(a, b):
    return lax.dot_general(a, b, (((1,), (1,)), ((), ())), preferred_element_type=F32)

def t_mm(a, b):
    return lax.dot_general(a, b, (((0,), (0,)), ((), ())), preferred_element_type=F32)


def norm_rows(v):
    width = v.shape[1]
    off = v - jnp.sum(v, axis=1, keepdims=True) * (1.0 / width)
    inv = lax.rsqrt(jnp.sum(off * off, axis=1, keepdims=True) * (1.0 / width) + EPS)
    return off * inv, inv


def norm_back(n, inv, t):
    width = n.shape[1]
    a = jnp.sum(t, axis=1, keepdims=True) * (1.0 / width)
    b = jnp.sum(t * n, axis=1, keepdims=True) * (1.0 / width)
    return inv * (t - a - n * b)


def col_sum(v):
    return jnp.sum(v, axis=0, keepdims=True)


def images_per_window(length):
    return jnp.where(length <= 128, 2, 1)


def window(meta, w, wq, wk, rows):
    length, count = meta
    group = images_per_window(length)
    lo = w * (length * group)
    hi = jnp.minimum(lo + length * group, length * count)
    base = (lo // 16) * 16
    sq = pl.multiple_of(jnp.minimum(base, rows - wq), 16)
    sk = pl.multiple_of(jnp.minimum(base, rows - wk), 16)
    return lo, hi, length, sq, sk


def seg_of(start, n, lo, hi, length):
    r = start + lax.broadcasted_iota(jnp.int32, (n, 128), 0)
    inside = jnp.logical_and(r >= lo, r < hi)
    return inside, jnp.where(inside, jnp.where(r >= lo + length, 1, 0), 2)


def halves(v):
    left = lax.broadcasted_iota(jnp.int32, v.shape, 1) < 64
    zero = jnp.zeros_like(v)
    return jnp.where(left, v, zero), jnp.where(left, zero, v)


def attend_fwd(meta, qkv_s, o_s, inv_s, e_s, wq, wk, pairs, width):
    rows = qkv_s.shape[0]
    scale = 0.125 * 1.4426950408889634

    def one(w, carry):
        lo, hi, length, sq, sk = window(meta, w, wq, wk, rows)
        in_q, seg_q = seg_of(sq, wq, lo, hi, length)
        _, seg_k = seg_of(sk, wk, lo, hi, length)
        lane_q = lax.broadcasted_iota(jnp.int32, (wq, 128), 1)
        lane_k = lax.broadcasted_iota(jnp.int32, (wk, 128), 1)
        aug_q = jnp.where(jnp.logical_and(lane_q != seg_q, lane_q < 3), 1.0, 0.0).astype(BF16)
        aug_k = jnp.where(lane_k == seg_k, FAR, 0.0).astype(BF16)
        ones0 = jnp.where(lane_k < 64, 1.0, 0.0).astype(BF16)
        ones1 = jnp.where(lane_k < 64, 0.0, 1.0).astype(BF16)
        for p in range(pairs):
            c = 128 * p
            q2 = qkv_s[pl.ds(sq, wq), c : c + 128]
            k0, k1 = halves(qkv_s[pl.ds(sk, wk), width + c : width + c + 128])
            v0, v1 = halves(qkv_s[pl.ds(sk, wk), 2 * width + c : 2 * width + c + 128])
            left = jnp.concatenate([q2, aug_q], axis=1)
            right = jnp.concatenate(
                [jnp.concatenate([k0, aug_k], axis=1), jnp.concatenate([k1, aug_k], axis=1)], axis=0
            )
            s = mm_t(left, right)
            parts = []
            for h in range(2):
                sh = s[:, h * wk : (h + 1) * wk]
                top = jnp.max(sh, axis=1, keepdims=True)
                parts.append(jnp.exp2((sh - top) * scale).astype(BF16))
            e = jnp.concatenate(parts, axis=1)
            e_s[w * pairs + p] = e
            vals = jnp.concatenate(
                [jnp.concatenate([v0, ones0], axis=1), jnp.concatenate([v1, ones1], axis=1)], axis=0
            )
            both = mm(e, vals)
            inv = 1.0 / both[:, 128:]
            o = (both[:, :128] * inv).astype(BF16)
            dst = (pl.ds(sq, wq), pl.ds(c, 128))
            o_s[dst] = jnp.where(in_q, o, o_s[dst])
            inv_s[dst] = jnp.where(in_q, inv, inv_s[dst])
        return carry

    length, count = meta
    lax.fori_loop(0, jnp.where(length <= 128, (count + 1) // 2, count), one, 0)


def attend_bwd(meta, qkv_s, o_s, inv_s, e_s, go_s, gqkv_s, wq, wk, pairs, width):
    rows = qkv_s.shape[0]

    def one(w, carry):
        lo, hi, length, sq, sk = window(meta, w, wq, wk, rows)
        in_q, _ = seg_of(sq, wq, lo, hi, length)
        in_k, _ = seg_of(sk, wk, lo, hi, length)
        for p in range(pairs):
            c = 128 * p
            e = e_s[w * pairs + p]
            q0, q1 = halves(qkv_s[pl.ds(sq, wq), c : c + 128])
            k0, k1 = halves(qkv_s[pl.ds(sk, wk), width + c : width + c + 128])
            v0, v1 = halves(qkv_s[pl.ds(sk, wk), 2 * width + c : 2 * width + c + 128])
            dst_q = (pl.ds(sq, wq), pl.ds(c, 128))
            go = (go_s[dst_q].astype(F32) * inv_s[dst_q]).astype(BF16)
            prod0, prod1 = halves(go.astype(F32) * o_s[dst_q].astype(F32))
            d = (jnp.sum(prod0, axis=1, keepdims=True), jnp.sum(prod1, axis=1, keepdims=True))
            gp = mm_t(go, jnp.concatenate([v0, v1], axis=0))
            gs = []
            for h in range(2):
                sl = slice(h * wk, (h + 1) * wk)
                gs.append((e[:, sl].astype(F32) * (gp[:, sl] - d[h])).astype(BF16))
            gq = mm(jnp.concatenate(gs, axis=1), jnp.concatenate([k0, k1], axis=0)) * 0.125
            gk = t_mm(jnp.concatenate(gs, axis=0), jnp.concatenate([q0, q1], axis=0)) * 0.125
            gv = t_mm(
                jnp.concatenate([e[:, :wk], e[:, wk:]], axis=0), jnp.concatenate(halves(go), axis=0)
            )
            gqkv_s[dst_q] = jnp.where(in_q, gq.astype(BF16), gqkv_s[dst_q])
            dst_k = (pl.ds(sk, wk), pl.ds(width + c, 128))
            gqkv_s[dst_k] = jnp.where(in_k, gk.astype(BF16), gqkv_s[dst_k])
            dst_v = (pl.ds(sk, wk), pl.ds(2 * width + c, 128))
            gqkv_s[dst_v] = jnp.where(in_k, gv.astype(BF16), gqkv_s[dst_v])
        return carry

    length, count = meta
    lax.fori_loop(0, jnp.where(length <= 128, (count + 1) // 2, count), one, 0)


WIDE = (352, 384)
NARROW = (224, 256)


def fold_matrix(part, count, high):
    rows, cols = 4 * count * part, count * high
    r = lax.broadcasted_iota(jnp.int32, (rows, cols), 0).astype(F32)
    c = lax.broadcasted_iota(jnp.int32, (rows, cols), 1).astype(F32)
    block = jnp.floor((c + 0.5) * (1.0 / high))
    inner = c - block * high
    piece = jnp.floor((inner + 0.5) * (1.0 / part))
    want = piece * (count * part) + block * part + (inner - piece * part)
    return jnp.where(jnp.logical_and(want == r, piece < 4), 1.0, 0.0).astype(BF16)


def unfold(blocks, dsts, part, high):
    count = 96 // part
    pick = fold_matrix(part, count, high)
    for t in range(len(blocks) // count):
        group = jnp.concatenate([blocks[j][...] for j in range(t * count, (t + 1) * count)], axis=0)
        full = mm(pick, group).astype(BF16)
        for a in range(4):
            dsts[a][96 * t : 96 * (t + 1), :] = full[96 * a : 96 * (a + 1), :]


def fold(srcs, blocks, part, high):
    count = 96 // part
    pick = fold_matrix(part, count, high)
    for t in range(len(blocks) // count):
        rows = slice(96 * t, 96 * (t + 1))
        four = jnp.concatenate([s[rows, :].astype(BF16) for s in srcs], axis=0)
        full = t_mm(pick, four).astype(BF16)
        for i in range(count):
            blocks[t * count + i][...] = full[i * high : (i + 1) * high, :]


def unfold_vectors(blocks, vec, part):
    n = len(blocks)
    width = part * n
    lane = lax.broadcasted_iota(jnp.int32, (8, 128), 1)
    total = jnp.zeros((8, width), F32)
    wide = jnp.zeros((8, 4 * width), F32)
    for j in range(n):
        pair = blocks[j][...].astype(F32)
        one = jnp.where(lane < part, pair[0:8], 0.0)
        one = jnp.concatenate([one, jnp.zeros((8, width - 128), F32)], axis=1)
        total = total + pltpu.roll(one, j * part, 1)
        one = jnp.where(lane < 4 * part, pair[8:16], 0.0)
        one = jnp.concatenate([one, jnp.zeros((8, 4 * width - 128), F32)], axis=1)
        wide = wide + pltpu.roll(one, 4 * j * part, 1)
    vec[...] = jnp.zeros_like(vec)
    for i, (row, col) in enumerate(VECTORS):
        vec[row : row + 1, col * width : (col + 1) * width] = total[i : i + 1]
    vec[V_FC1 : V_FC1 + 1, :] = wide[0:1]


def fold_vectors(vec, blocks, part):
    n = len(blocks)
    width = part * n
    eight = jnp.concatenate(
        [vec[row : row + 1, col * width : (col + 1) * width] for row, col in VECTORS], axis=0
    )
    wide = jnp.broadcast_to(vec[V_FC1 : V_FC1 + 1, :], (8, 4 * width))
    for j in range(n):
        blocks[j][0:8, :] = pltpu.roll(eight, (width - j * part) % width, 1)[:, :128]
        blocks[j][8:16, :] = pltpu.roll(wide, (4 * width - 4 * j * part) % (4 * width), 1)[:, :128]


VECTORS = ((V_GAIN1, 0), (V_SHIFT1, 0), (V_QKV, 0), (V_QKV, 2), (V_OUT, 0), (V_GAIN2, 0), (V_SHIFT2, 0), (V_FC2, 0))


def layer_kernel(
    tokens, counts, x_ref, cot_ref, qkv_ref, wout_ref, w1_ref, w2_ref, vec,
    out_ref, gqkv_ref, gmix_ref, p_fc1_ref, p_fc2_ref, a_out, a_vec,
    wout, w1, w2, p_fc1, p_fc2, sems, a_fc1, a_fc2, o_s, inv_s, e1_s, e2_s, h2_s, act_s, gpre_s, gy_s, gb_s, go_s,
    part, phases=("af", "mlp", "wg", "ab"), tile=512, chunk=256,
):
    m = pl.program_id(0)
    me = lax.axis_index("dp")
    rows, width = x_ref.shape[1], x_ref.shape[2]
    hidden = w1.shape[1]
    pairs = HEADS // 2
    length, count = tokens[m, me], counts[m, me]
    meta = (length, count)
    total = length * count
    qkv_s, gqkv_s, gmix_s = qkv_ref.at[0], gqkv_ref.at[0], gmix_ref.at[0]

    loads = [
        pltpu.make_async_copy(a, b, sems.at[i])
        for i, (a, b) in enumerate(((wout_ref, wout), (w1_ref, w1), (w2_ref, w2)))
    ]
    stores = [
        pltpu.make_async_copy(a, b, sems.at[3 + i])
        for i, (a, b) in enumerate(((p_fc1, p_fc1_ref), (p_fc2, p_fc2_ref)))
    ]
    final_step = m == pl.num_programs(0) - 1

    @pl.when(m == 0)
    def _():
        for load in loads:
            load.start()
        for ref in (a_out, a_fc1, a_fc2, a_vec):
            ref[...] = jnp.zeros_like(ref)

    def v(i, n=width):
        return vec[i : i + 1, 0:n]

    def add_vec(i, val):
        a_vec[i : i + 1, 0 : val.shape[1]] += val

    o_s[...] = qkv_s[:, 2 * width :]

    if "af" in phases:
        fwd = functools.partial(attend_fwd, meta, qkv_s, o_s, inv_s)
        @pl.when(length > 256)
        def _():
            fwd(e1_s, *WIDE, pairs, width)
        @pl.when(length <= 256)
        def _():
            fwd(e2_s, *NARROW, pairs, width)

    @pl.when(m == 0)
    def _():
        for load in loads:
            load.wait()

    if "mlp" in phases:
        def mlp(i, c):
            r = pl.ds(pl.multiple_of(i * tile, tile), tile)
            valid = (i * tile + lax.broadcasted_iota(jnp.int32, (tile, 1), 0)) < total
            mixed = x_ref[0, r, :].astype(F32) + mm(o_s[r, :], wout[...]) + v(V_OUT)
            n2, r2 = norm_rows(mixed)
            h2 = (n2 * v(V_GAIN2) + v(V_SHIFT2)).astype(BF16)
            h2_s[r, :] = h2
            gy = jnp.where(valid, cot_ref[0, r, :].astype(F32), 0.0)
            gyl = gy.astype(BF16)
            gy_s[r, :] = gyl
            add_vec(G_FC2, col_sum(gy))
            for f in range(0, hidden, chunk):
                fs = slice(f, f + chunk)
                pre = mm(h2, w1[:, fs]) + vec[V_FC1 : V_FC1 + 1, fs]
                cdf = 0.5 * lax.erf(pre * 0.7071067811865476) + 0.5
                act_s[r, fs] = (pre * cdf).astype(BF16)
                slope = cdf + pre * (jnp.exp(pre * pre * -0.5) * 0.3989422804014327)
                gpre = (slope * mm_t(gyl, w2[fs, :])).astype(BF16)
                gpre_s[r, fs] = gpre
                a_vec[G_FC1 : G_FC1 + 1, fs] += col_sum(gpre.astype(F32))
            final = mixed + mm(act_s[r, :], w2[...]) + v(V_FC2)
            out_ref[0, r, :] = jnp.where(valid, final, 0.0).astype(BF16)
            gh2 = mm_t(gpre_s[r, :], w1[...])
            add_vec(G_GAIN2, col_sum(gh2 * n2))
            add_vec(G_SHIFT2, col_sum(gh2))
            gmix = gy + norm_back(n2, r2, gh2 * v(V_GAIN2))
            gmix_s[r, :] = gmix
            gb = gmix.astype(BF16)
            gb_s[r, :] = gb
            add_vec(G_OUT, col_sum(gb.astype(F32)))
            go_s[r, :] = mm_t(gb, wout[...]).astype(BF16)
            return c
        lax.fori_loop(0, rows // tile, mlp, 0)

    if "wg" in phases:
        a_fc1[...] += t_mm(h2_s[...], gpre_s[...])
        a_fc2[...] += t_mm(act_s[...], gy_s[...])
        a_out[...] += t_mm(o_s[...], gb_s[...])

    @pl.when(final_step)
    def _():
        high = p_fc1.shape[0] // (width // part)
        blocks = [p_fc1.at[j * high : (j + 1) * high, :] for j in range(width // part)]
        fold([a_fc1.at[:, i * width : (i + 1) * width] for i in range(4)], blocks, part, high)
        p_fc2[...] = a_fc2[...].astype(BF16)
        for store in stores:
            store.start()

    gqkv_s[:, : 2 * width] = jnp.zeros((rows, 2 * width), BF16)
    gqkv_s[:, 2 * width :] = go_s[...]

    if "ab" in phases:
        bwd = functools.partial(attend_bwd, meta, qkv_s, o_s, inv_s)
        @pl.when(length > 256)
        def _():
            bwd(e1_s, go_s, gqkv_s, *WIDE, pairs, width)
        @pl.when(length <= 256)
        def _():
            bwd(e2_s, go_s, gqkv_s, *NARROW, pairs, width)

    @pl.when(final_step)
    def _():
        for store in stores:
            store.wait()


def layer_call(tokens, counts, x, cot, qkv, wout, w1, w2, vec, n, **kw):
    micro, rows, width = x.shape
    hidden = w2.shape[0]
    part = width // n
    high = -(-4 * part // 16) * 16
    def per_step(cols):
        return pl.BlockSpec((1, rows, cols), lambda m: (m, 0, 0))
    def whole(shape):
        return pl.BlockSpec(shape, lambda m: (0, 0), pipeline_mode=pl.Buffered(1))
    hbm = pl.BlockSpec(memory_space=pl.ANY)
    bf = lambda n: pltpu.VMEM((rows, n), BF16)
    outs = [(x.shape, BF16), ((micro, rows, 3 * width), BF16), (x.shape, F32)]
    kept = [((n * high, width), BF16), ((hidden, width), BF16), ((width, width), F32), (vec.shape, F32)]
    return pl.pallas_call(
        functools.partial(layer_kernel, part=part, **kw),
        grid=(micro,),
        in_specs=[pl.BlockSpec(memory_space=pltpu.SMEM)] * 2 + [per_step(width), per_step(width), per_step(3 * width)]
        + [hbm] * 3 + [whole(vec.shape)],
        out_specs=[per_step(s[2]) for s, _ in outs] + [hbm] * 2 + [whole(s) for s, _ in kept[2:]],
        out_shape=[jax.ShapeDtypeStruct(s, d) for s, d in outs + kept],
        scratch_shapes=[pltpu.VMEM(a.shape, BF16) for a in (wout, w1, w2)] + [
            pltpu.VMEM(kept[0][0], BF16), pltpu.VMEM(kept[1][0], BF16), pltpu.SemaphoreType.DMA((5,)),
            pltpu.VMEM((width, hidden), F32), pltpu.VMEM((hidden, width), F32),
            bf(width), pltpu.VMEM((rows, width), F32),
            pltpu.VMEM((9, 352, 768), BF16), pltpu.VMEM((15, 224, 512), BF16),
            bf(width), bf(hidden), bf(hidden), bf(width), bf(width), bf(width),
        ],
        compiler_params=pltpu.CompilerParams(vmem_limit_bytes=64 * 2**20 - 2**17),
    )(tokens, counts, x, cot, qkv, wout, w1, w2, vec)


def bit_of(me, b):
    return (me // (1 << b)) % 2


class Place:
    def __init__(self, n):
        self.me = lax.axis_index("dp")
        self.count = n // 8
        self.z, self.y, self.x, self.c = self.me // 8, bit_of(self.me, 2), bit_of(self.me, 1), bit_of(self.me, 0)
        self.over_y = self.me + 4 * (1 - 2 * self.y)
        self.over_x = self.me + 2 * (1 - 2 * self.x)
        self.twin = self.me + (1 - 2 * self.c)
        self.steps = sorted(range(1, self.count), key=lambda k: min(k, self.count - k))

    def ahead(self, k):
        return (self.z + k) % self.count

    def behind(self, k):
        return (self.z + self.count - k) % self.count

    def at(self, z):
        return self.me + 8 * (z - self.z)

    def meet(self):
        barrier = pltpu.get_barrier_semaphore()
        others = [self.over_y, self.over_x, self.twin] + [self.at(self.ahead(k)) for k in range(1, self.count)]
        for device in others:
            pl.semaphore_signal(barrier, inc=1, device_id=(device,), device_id_type=MESH)
        pl.semaphore_wait(barrier, len(others))


LINE, ALONG_X, ALONG_Y, DIAG_X, DIAG_Y, TWIN = range(6)


class Wire:
    def __init__(self, place, cut, send, recv):
        self.place, self.cut, self.send, self.recv, self.started = place, cut, send, recv, []

    def copy(self, kind, k, src, dst, device):
        return pltpu.make_async_remote_copy(
            src_ref=src, dst_ref=dst, send_sem=self.send.at[kind, k], recv_sem=self.recv.at[kind, k],
            device_id=(device,), device_id_type=MESH)

    def push(self, kind, k, src, dst, device):
        copy = self.copy(kind, k, src, dst, device)
        copy.start()
        self.started.append(copy)

    def arrive(self, kind, k, dst):
        self.copy(kind, k, dst, dst, self.place.twin).wait_recv()

    def finish(self):
        for copy in self.started:
            copy.wait_send()

    def columns(self, k, width):
        if self.cut is None:
            return slice(0, width), None
        cut = 128 if (k + self.cut) % 2 else width - 128
        return slice(0, cut), slice(cut, width)


class Gather(Wire):
    def __init__(self, place, ref, cut, send, recv):
        super().__init__(place, cut, send, recv)
        self.ref = ref

    def block(self, k, over_y, over_x, cols=slice(None)):
        p = self.place
        y = 1 - p.y if over_y else p.y
        x = 1 - p.x if over_x else p.x
        return self.ref.at[p.behind(k), y, x, p.c, :, cols]

    def same(self, kind, k, view, device):
        self.push(kind, k, view, view, device)

    def begin(self):
        p = self.place
        for k in p.steps:
            self.same(LINE, k, self.block(0, False, False), p.at(p.ahead(k)))

    def line(self, k):
        view = self.block(k, False, False)
        if k:
            self.arrive(LINE, k, view)
        self.same(ALONG_X, k, view, self.place.over_x)
        self.same(ALONG_Y, k, view, self.place.over_y)

    def plane(self, k):
        first, second = self.columns(k, self.ref.shape[-1])
        self.arrive(ALONG_X, k, self.block(k, False, True))
        self.same(DIAG_Y, k, self.block(k, False, True, first), self.place.over_y)
        self.arrive(ALONG_Y, k, self.block(k, True, False))
        if second is not None:
            self.same(DIAG_X, k, self.block(k, True, False, second), self.place.over_x)

    def corner(self, k):
        first, second = self.columns(k, self.ref.shape[-1])
        self.arrive(DIAG_Y, k, self.block(k, True, True, first))
        if second is not None:
            self.arrive(DIAG_X, k, self.block(k, True, True, second))
        p = self.place
        self.same(TWIN, k, self.ref.at[p.behind(k), :, :, p.c], p.twin)

    def last(self):
        p = self.place
        for k in range(p.count):
            self.arrive(TWIN, k, self.ref.at[p.behind(k), :, :, 1 - p.c])


class Scatter(Wire):
    def __init__(self, place, src, cut, scratch, out, send, recv):
        super().__init__(place, cut, send, recv)
        self.src, self.out = src, out
        self.twins, self.diag_x, self.diag_y, self.from_x, self.from_y, self.lines, self.sums = scratch

    def half(self, k, y, x):
        p = self.place
        z = p.ahead(k)
        return self.src[z, y, x, p.c].astype(F32) + self.twins[z, y, x].astype(F32)

    def begin(self):
        p = self.place
        for k in p.steps + [0]:
            z = p.ahead(k)
            self.push(TWIN, k, self.src.at[z, :, :, 1 - p.c], self.twins.at[z], p.twin)

    def corner(self, k):
        p = self.place
        self.arrive(TWIN, k, self.twins.at[p.ahead(k)])
        first, second = self.columns(k, self.src.shape[-1])
        held = self.sums.at[0, k]
        held[...] = self.half(k, 1 - p.y, 1 - p.x).astype(held.dtype)
        self.push(DIAG_Y, k, held.at[:, first], self.diag_x.at[k, :, first], p.over_y)
        if second is not None:
            self.push(DIAG_X, k, held.at[:, second], self.diag_y.at[k, :, second], p.over_x)

    def plane(self, k):
        p = self.place
        first, second = self.columns(k, self.src.shape[-1])
        self.arrive(DIAG_Y, k, self.diag_x.at[k, :, first])
        held = self.sums.at[1, k]
        total = self.half(k, p.y, 1 - p.x)
        held[:, first] = (total[:, first] + self.diag_x[k, :, first].astype(F32)).astype(held.dtype)
        if second is not None:
            held[:, second] = total[:, second].astype(held.dtype)
        self.push(ALONG_X, k, held, self.from_x.at[k], p.over_x)
        held = self.sums.at[2, k]
        total = self.half(k, 1 - p.y, p.x)
        if second is None:
            held[...] = total.astype(held.dtype)
        else:
            self.arrive(DIAG_X, k, self.diag_y.at[k, :, second])
            held[:, first] = total[:, first].astype(held.dtype)
            held[:, second] = (total[:, second] + self.diag_y[k, :, second].astype(F32)).astype(held.dtype)
        self.push(ALONG_Y, k, held, self.from_y.at[k], p.over_y)

    def line(self, k):
        p = self.place
        self.arrive(ALONG_X, k, self.from_x.at[k])
        self.arrive(ALONG_Y, k, self.from_y.at[k])
        total = self.half(k, p.y, p.x) + self.from_x[k].astype(F32) + self.from_y[k].astype(F32)
        if k == 0:
            self.out[...] = total
            return
        held = self.sums.at[3, k]
        held[...] = total.astype(held.dtype)
        self.push(LINE, k, held, self.lines.at[k], p.at(p.ahead(k)))

    def last(self):
        total = self.out[...]
        for k in self.place.steps:
            self.arrive(LINE, k, self.lines.at[k])
            total = total + self.lines[k].astype(F32)
        self.out[...] = total


def gather_kernel(
    n, tile, x_ref, w_qkv, w_out, w_fc1, w_fc2, *refs,
):
    small = refs[:9]
    qkv_ref, wqkv, wout, w1, g_fc2, vec, x_s, qkv_s, g_attn, g_fc1, g_vec, pad, pad_vec, x_sem, qkv_sem, send, recv = refs[9:]
    place = Place(n)
    micro, rows, width = x_s.shape
    part = width // n
    height = g_fc1.shape[-2]
    loads = [pltpu.make_async_copy(x_ref.at[m], x_s.at[m], x_sem.at[m]) for m in range(micro)]
    for load in loads:
        load.start()
    own = (place.z, place.y, place.x, place.c)
    if height > 4 * part:
        pad[...] = jnp.zeros_like(pad)
    pad_vec[...] = jnp.zeros_like(pad_vec)
    for i in range(8):
        pad_vec[i : i + 1, 0:part] = small[i][...].astype(F32).reshape(1, part)
    pad_vec[8:9, 0 : 4 * part] = small[8][...].astype(F32).reshape(1, 4 * part)
    g_vec[own] = pad_vec[...].astype(BF16)
    def fold_own(dst, four):
        for a, piece in enumerate(four):
            pad[a * part : (a + 1) * part, :] = piece.astype(F32)
        dst[own] = pad[...].astype(BF16)
    fold_own(g_attn, [w_qkv[:, a * width : (a + 1) * width] for a in range(3)] + [w_out[...]])
    fold_own(g_fc1, [w_fc1[:, a * width : (a + 1) * width] for a in range(4)])
    if height > 4 * part:
        fold_own(g_fc2, [w_fc2[a * part : (a + 1) * part, :] for a in range(4)])
    else:
        g_fc2[own] = w_fc2[...]
    place.meet()

    refs = (g_vec, g_attn, g_fc1, g_fc2)
    parts = [Gather(place, ref, cut, send.at[i], recv.at[i]) for i, (ref, cut) in enumerate(zip(refs, (None, 0, 1, 0)))]
    urgent, rest = parts[:2], parts[2:]
    order = [0] + place.steps
    todo = [(p, "line", k) for k in order for p in rest]
    todo += [(p, "plane", k) for k in order for p in rest]
    todo += [(p, "corner", k) for k in order for p in rest]

    def some(count):
        for p, stage, k in todo[:count]:
            getattr(p, stage)(k)
        del todo[:count]

    for p in urgent:
        p.begin()
    for p in urgent:
        p.line(0)
    for k in place.steps:
        for p in urgent:
            p.line(k)
    for p in rest:
        p.begin()
    for k in order:
        for p in urgent:
            p.plane(k)
        some(1)
    for k in order:
        for p in urgent:
            p.corner(k)
        some(1)
    for p in urgent:
        p.last()
    flat = lambda ref: [ref.at[j // 8, (j // 4) % 2, (j // 2) % 2, j % 2] for j in range(n)]
    unfold_vectors(flat(g_vec), vec, part)
    unfold(flat(g_attn), [wqkv.at[:, 0:width], wqkv.at[:, width : 2 * width], wqkv.at[:, 2 * width :], wout], part, height)

    def qkv_part(m, i):
        r = pl.ds(i * tile, tile)
        n1, _ = norm_rows(x_s[m, r, :].astype(F32))
        h1 = (n1 * vec[V_GAIN1 : V_GAIN1 + 1, 0:width] + vec[V_SHIFT1 : V_SHIFT1 + 1, 0:width]).astype(BF16)
        qkv_s[m, r, :] = (mm(h1, wqkv[...]) + vec[V_QKV : V_QKV + 1, 0 : 3 * width]).astype(BF16)

    stores = [pltpu.make_async_copy(qkv_s.at[m], qkv_ref.at[m], qkv_sem.at[m]) for m in range(micro)]
    turns = micro * (rows // tile)
    each = -(-len(todo) // max(turns, 1))
    for m in range(micro):
        loads[m].wait()
        for i in range(rows // tile):
            qkv_part(m, i)
            some(each)
        stores[m].start()
    some(len(todo))
    rest[0].last()
    unfold(flat(g_fc1), [w1.at[:, i * width : (i + 1) * width] for i in range(4)], part, height)
    rest[1].last()
    for p in parts:
        p.finish()
    for store in stores:
        store.wait()


def gather_call(n, x, w_qkv, w_out, w_fc1, w_fc2, small, collective_id, tile=512):
    micro, rows, width = x.shape
    height = -(-4 * w_out.shape[0] // 16) * 16
    vmem, hbm = pl.BlockSpec(memory_space=pltpu.VMEM), pl.BlockSpec(memory_space=pl.ANY)
    grid = (n // 8, 2, 2, 2)
    sems = pltpu.SemaphoreType.DMA((4, 6, n // 8))
    block = (height, width)
    shapes = [((micro, rows, 3 * width), BF16), ((width, 3 * width), BF16), ((width, width), BF16),
              ((width, 4 * width), BF16), (grid + block, BF16), ((8, 4 * width), F32)]
    return pl.pallas_call(
        functools.partial(gather_kernel, n, tile),
        in_specs=[hbm] + [vmem] * (4 + len(small)),
        out_specs=[hbm] + [vmem] * 5,
        out_shape=[jax.ShapeDtypeStruct(s, d) for s, d in shapes],
        scratch_shapes=[
            pltpu.VMEM(x.shape, BF16), pltpu.VMEM((micro, rows, 3 * width), BF16),
            pltpu.VMEM(grid + block, BF16), pltpu.VMEM(grid + block, BF16), pltpu.VMEM(grid + (16, 128), BF16),
            pltpu.VMEM(block, F32), pltpu.VMEM((16, 128), F32),
            pltpu.SemaphoreType.DMA((micro,)), pltpu.SemaphoreType.DMA((micro,)), sems, sems,
        ],
        compiler_params=pltpu.CompilerParams(
            collective_id=collective_id, has_side_effects=True, vmem_limit_bytes=60 * 2**20),
    )(x, w_qkv, w_out, w_fc1, w_fc2, *small)


def scatter_kernel(
    n, tile, x_ref, gqkv_ref, gmix_ref, wqkv, vec, p_fc1, p_fc2, p_out, gvec,
    ig_ref, o_attn, o_fc1, o_fc2, o_vec,
    x_s, gqkv_s, gmix_s, ig_s, n1_s, acc, acc_vec, p_attn, p_vec, in_sem, out_sem, send, recv, *rest,
):
    place = Place(n)
    micro, rows, width = x_s.shape
    part = width // n
    height = p_fc1.shape[-2]
    loads = []
    for m in range(micro):
        pairs = ((x_ref, x_s), (gqkv_ref, gqkv_s), (gmix_ref, gmix_s))
        loads.append([pltpu.make_async_copy(a.at[m], b.at[m], in_sem.at[i, m]) for i, (a, b) in enumerate(pairs)])
        for load in loads[m]:
            load.start()
    place.meet()

    def stream(i, src, cut, out):
        return Scatter(place, src, cut, rest[7 * i : 7 * i + 7], out, send.at[i], recv.at[i])
    fc = [stream(0, p_fc1, 0, o_fc1), stream(1, p_fc2, 1, o_fc2)]
    attn, vecs = stream(2, p_attn, 0, o_attn), stream(3, p_vec, None, o_vec)
    order = place.steps + [0]
    def stages(streams):
        return [(s, stage, k) for stage in ("corner", "plane", "line") for k in order for s in streams]
    todo = stages(fc)

    def some(count):
        for s, stage, k in todo[:count]:
            getattr(s, stage)(k)
        del todo[:count]

    for s in fc:
        s.begin()

    def v(i, cols=width):
        return vec[i : i + 1, 0:cols]

    acc_vec[...] = gvec[...]
    for m in range(micro):
        for load in loads[m][:2]:
            load.wait()
        for i in range(rows // tile):
            r = pl.ds(i * tile, tile)
            n1, _ = norm_rows(x_s[m, r, :].astype(F32))
            n1_s[m, r, :] = n1.astype(BF16)
        g = t_mm(n1_s[m], gqkv_s[m])
        acc[...] = g if m == 0 else acc[...] + g
        acc_vec[V_QKV : V_QKV + 1, 0 : 3 * width] += col_sum(gqkv_s[m].astype(F32))
        some(len(order) * 2 if m == 0 else len(order))
    total = acc[...]
    sums = acc_vec[V_QKV : V_QKV + 1, 0 : 3 * width]
    table = jnp.concatenate([jnp.broadcast_to(v(V_GAIN1), (64, width)), jnp.broadcast_to(v(V_SHIFT1), (64, width))], axis=0)
    table = jnp.transpose(table)
    acc[...] = total * table[:, 0:1] + sums * table[:, 64:65]
    flat = lambda ref: [ref.at[j // 8, (j // 4) % 2, (j // 2) % 2, j % 2] for j in range(n)]
    fold([acc.at[:, 0:width], acc.at[:, width : 2 * width], acc.at[:, 2 * width :], p_out], flat(p_attn), part, height)
    attn.begin()
    dots = jnp.sum(wqkv[...].astype(F32) * total, axis=1, keepdims=True)
    acc_vec[V_GAIN1 : V_GAIN1 + 1, 0:width] += jnp.transpose(jnp.broadcast_to(dots, (width, 128)))[0:1, :]
    one = sums.astype(BF16).astype(F32)
    two = (sums - one).astype(BF16).astype(F32)
    three = sums - one - two
    row = lax.broadcasted_iota(jnp.int32, (16, 3 * width), 0)
    split = jnp.where(row == 0, one, jnp.where(row == 1, two, jnp.where(row == 2, three, 0.0))).astype(BF16)
    acc_vec[V_SHIFT1 : V_SHIFT1 + 1, 0:width] += col_sum(mm_t(split, wqkv[...]))
    fold_vectors(acc_vec, flat(p_vec), part)
    vecs.begin()
    late = [t for pair in zip(stages([attn]), stages([vecs])) for t in pair]
    todo = [t for pair in zip(todo, late) for t in pair] + todo[len(late) :] + late[len(todo) :]

    stores = [pltpu.make_async_copy(ig_s.at[m], ig_ref.at[m], out_sem.at[m]) for m in range(micro)]
    turns = micro * (rows // tile)
    each = -(-len(todo) // turns)
    for m in range(micro):
        loads[m][2].wait()
        for i in range(rows // tile):
            r = pl.ds(i * tile, tile)
            gqkv = gqkv_s[m, r, :]
            gh1 = mm_t(gqkv, wqkv[...])
            n1, r1 = norm_rows(x_s[m, r, :].astype(F32))
            ig_s[m, r, :] = (gmix_s[m, r, :] + norm_back(n1, r1, gh1 * v(V_GAIN1))).astype(BF16)
            some(each)
        stores[m].start()
    some(len(todo))
    for s in fc + [attn, vecs]:
        s.last()
    for s in fc + [attn, vecs]:
        s.finish()
    for store in stores:
        store.wait()


def scatter_call(n, x, gqkv, gmix, wqkv, vec, p_fc1, p_fc2, p_out, gvec, collective_id, tile=512):
    micro, rows, width = x.shape
    height = p_fc1.shape[0] // n
    vmem, hbm = pl.BlockSpec(memory_space=pltpu.VMEM), pl.BlockSpec(memory_space=pl.ANY)
    places = n // 8
    grid = (places, 2, 2, 2)
    scratch = []
    for shape, dtype in [((height, width), BF16)] * 3 + [((16, 128), F32)]:
        scratch += [pltpu.VMEM((places, 2, 2) + shape, dtype)]
        scratch += [pltpu.VMEM((places,) + shape, dtype) for _ in range(5)]
        scratch += [pltpu.VMEM((4, places) + shape, dtype)]
    block = jax.ShapeDtypeStruct((height, width), F32)
    sems = pltpu.SemaphoreType.DMA((4, 6, places))
    return pl.pallas_call(
        functools.partial(scatter_kernel, n, tile),
        in_specs=[hbm] * 3 + [vmem] * 6,
        out_specs=[hbm] + [vmem] * 4,
        out_shape=[jax.ShapeDtypeStruct(x.shape, BF16), block, block, block, jax.ShapeDtypeStruct((16, 128), F32)],
        scratch_shapes=[
            pltpu.VMEM(x.shape, BF16), pltpu.VMEM(gqkv.shape, BF16), pltpu.VMEM(gmix.shape, F32), pltpu.VMEM(x.shape, BF16),
            pltpu.VMEM(x.shape, BF16), pltpu.VMEM((width, 3 * width), F32), pltpu.VMEM(vec.shape, F32),
            pltpu.VMEM(grid + (height, width), BF16), pltpu.VMEM(grid + (16, 128), F32),
            pltpu.SemaphoreType.DMA((3, micro)), pltpu.SemaphoreType.DMA((micro,)), sems, sems,
        ] + scratch,
        compiler_params=pltpu.CompilerParams(
            collective_id=collective_id, has_side_effects=True, vmem_limit_bytes=62 * 2**20),
    )(x, gqkv, gmix, wqkv, vec, p_fc1.reshape(grid + (height, width)), p_fc2.reshape(grid + (height, width)), p_out, gvec)


def finish_kernel(part, ig_in, s_attn, s_fc1, s_fc2, s_vec, ig, g_qkv, g_out, g_fc1, g_fc2, *rest):
    vectors, held, sems = rest[:9], rest[9], rest[10]
    width = s_attn.shape[1]
    micro, rows = held.shape[:2]
    cuts = [(m, pl.ds(h * (rows // 2), rows // 2)) for m in range(micro) for h in range(2)]
    loads = [pltpu.make_async_copy(ig_in.at[c], held.at[c], sems.at[0, i]) for i, c in enumerate(cuts)]
    stores = [pltpu.make_async_copy(held.at[c], ig.at[c], sems.at[1, i]) for i, c in enumerate(cuts)]
    for load in loads:
        load.start()
    for a in range(4):
        own = slice(a * part, (a + 1) * part)
        if a < 3:
            g_qkv[:, a * width : (a + 1) * width] = s_attn[own, :]
        else:
            g_out[...] = s_attn[own, :]
        g_fc1[:, a * width : (a + 1) * width] = s_fc1[own, :]
    g_fc2[...] = s_fc2[0 : 4 * part, :]
    for i in range(8):
        vectors[i][...] = s_vec[i, 0:part]
    vectors[8][...] = s_vec[8, 0 : 4 * part]
    for load, store in zip(loads, stores):
        load.wait()
        store.start()
    for store in stores:
        store.wait()


def finish_call(part, ig, s_attn, s_fc1, s_fc2, s_vec):
    width = s_attn.shape[1]
    vmem, hbm = pl.BlockSpec(memory_space=pltpu.VMEM), pl.BlockSpec(memory_space=pl.ANY)
    shapes = [(part, 3 * width), (part, width), (part, 4 * width), (4 * part, width)] + [(part,)] * 8 + [(4 * part,)]
    return pl.pallas_call(
        functools.partial(finish_kernel, part),
        in_specs=[hbm] + [vmem] * 4,
        out_specs=[hbm] + [vmem] * 13,
        out_shape=[jax.ShapeDtypeStruct(ig.shape, ig.dtype)] + [jax.ShapeDtypeStruct(s, F32) for s in shapes],
        scratch_shapes=[pltpu.VMEM(ig.shape, ig.dtype), pltpu.SemaphoreType.DMA((2, 2 * ig.shape[0]))],
    )(ig, s_attn, s_fc1, s_fc2, s_vec)


def body(inputs, cotangent, w_qkv, w_out, w_fc1, w_fc2, gain1, shift1, q_bias, v_bias, out_bias, gain2, shift2,
         fc1_bias, fc2_bias, image_tokens, image_count):
    n = lax.axis_size("dp")
    part, width = w_out.shape
    hidden = w_fc1.shape[1]
    high = -(-4 * part // 16) * 16
    small = (gain1, shift1, q_bias, v_bias, out_bias, gain2, shift2, fc2_bias, fc1_bias)
    qkv, wqkv, wout, w1, g_fc2, vec = gather_call(n, inputs, w_qkv, w_out, w_fc1, w_fc2, small, 1)
    w2 = g_fc2.reshape(n, high, width)[:, : 4 * part].reshape(hidden, width)
    out, gqkv, gmix, p_fc1, p_fc2, a_out, a_vec = layer_call(
        image_tokens, image_count, inputs, cotangent, qkv, wout, w1, w2, vec, n)
    p_fc2 = jnp.pad(p_fc2.reshape(n, 4 * part, width), ((0, 0), (0, high - 4 * part), (0, 0))).reshape(n * high, width)
    ig, s_attn, s_fc1, s_fc2, s_vec = scatter_call(
        n, inputs, gqkv, gmix, wqkv, vec, p_fc1, p_fc2, a_out, a_vec, 2)
    ig, g_qkv, g_out, g_fc1, g_fc2, *v = finish_call(part, ig, s_attn, s_fc1, s_fc2, s_vec)
    return (out, ig, g_qkv, g_out, g_fc1, g_fc2, *v[:7], v[8], v[7])


def solution(mesh):
    big, mat, one = P(None, "dp", None), P("dp", None), P("dp")
    return jax.shard_map(
        body, mesh=mesh,
        in_specs=(big, big) + (mat,) * 4 + (one,) * 9 + (P(), P()),
        out_specs=(big, big) + (mat,) * 4 + (one,) * 9,
        check_vma=False,
    )
```

```python
import functools

import jax
import jax.numpy as jnp
from jax import lax
from jax.experimental import pallas as pl
from jax.experimental.pallas import tpu as pltpu
from jax.sharding import PartitionSpec as P

F32, BF16 = jnp.float32, jnp.bfloat16
MESH = pl.DeviceIdType.MESH

HEADS = 6
EPS = 1e-06
FAR = -1e30
V_GAIN1, V_SHIFT1, V_QKV, V_OUT, V_GAIN2, V_SHIFT2, V_FC1, V_FC2 = range(8)
G_GAIN1, G_SHIFT1, G_QKV, G_OUT, G_GAIN2, G_SHIFT2, G_FC1, G_FC2 = range(8)


def mm(a, b):
    return jnp.dot(a, b, preferred_element_type=F32)

def mm_t(a, b):
    return lax.dot_general(a, b, (((1,), (1,)), ((), ())), preferred_element_type=F32)

def t_mm(a, b):
    return lax.dot_general(a, b, (((0,), (0,)), ((), ())), preferred_element_type=F32)


def norm_rows(v):
    width = v.shape[1]
    off = v - jnp.sum(v, axis=1, keepdims=True) * (1.0 / width)
    inv = lax.rsqrt(jnp.sum(off * off, axis=1, keepdims=True) * (1.0 / width) + EPS)
    return off * inv, inv


def norm_back(n, inv, t):
    width = n.shape[1]
    a = jnp.sum(t, axis=1, keepdims=True) * (1.0 / width)
    b = jnp.sum(t * n, axis=1, keepdims=True) * (1.0 / width)
    return inv * (t - a - n * b)


def col_sum(v):
    return jnp.sum(v, axis=0, keepdims=True)


def images_per_window(length):
    return jnp.where(length <= 128, 2, 1)


def window(meta, w, wq, wk, rows):
    length, count = meta
    group = images_per_window(length)
    lo = w * (length * group)
    hi = jnp.minimum(lo + length * group, length * count)
    base = (lo // 16) * 16
    sq = pl.multiple_of(jnp.minimum(base, rows - wq), 16)
    sk = pl.multiple_of(jnp.minimum(base, rows - wk), 16)
    return lo, hi, length, sq, sk


def seg_of(start, n, lo, hi, length):
    r = start + lax.broadcasted_iota(jnp.int32, (n, 128), 0)
    inside = jnp.logical_and(r >= lo, r < hi)
    return inside, jnp.where(inside, jnp.where(r >= lo + length, 1, 0), 2)


def halves(v):
    left = lax.broadcasted_iota(jnp.int32, v.shape, 1) < 64
    zero = jnp.zeros_like(v)
    return jnp.where(left, v, zero), jnp.where(left, zero, v)


def attend_fwd(meta, qkv_s, o_s, inv_s, e_s, wq, wk, pairs, width):
    rows = qkv_s.shape[0]
    scale = 0.125 * 1.4426950408889634

    def one(w, carry):
        lo, hi, length, sq, sk = window(meta, w, wq, wk, rows)
        in_q, seg_q = seg_of(sq, wq, lo, hi, length)
        _, seg_k = seg_of(sk, wk, lo, hi, length)
        lane_q = lax.broadcasted_iota(jnp.int32, (wq, 128), 1)
        lane_k = lax.broadcasted_iota(jnp.int32, (wk, 128), 1)
        aug_q = jnp.where(jnp.logical_and(lane_q != seg_q, lane_q < 3), 1.0, 0.0).astype(BF16)
        aug_k = jnp.where(lane_k == seg_k, FAR, 0.0).astype(BF16)
        ones0 = jnp.where(lane_k < 64, 1.0, 0.0).astype(BF16)
        ones1 = jnp.where(lane_k < 64, 0.0, 1.0).astype(BF16)
        for p in range(pairs):
            c = 128 * p
            q2 = qkv_s[pl.ds(sq, wq), c : c + 128]
            k0, k1 = halves(qkv_s[pl.ds(sk, wk), width + c : width + c + 128])
            v0, v1 = halves(qkv_s[pl.ds(sk, wk), 2 * width + c : 2 * width + c + 128])
            left = jnp.concatenate([q2, aug_q], axis=1)
            right = jnp.concatenate(
                [jnp.concatenate([k0, aug_k], axis=1), jnp.concatenate([k1, aug_k], axis=1)], axis=0
            )
            s = mm_t(left, right)
            parts = []
            for h in range(2):
                sh = s[:, h * wk : (h + 1) * wk]
                top = jnp.max(sh, axis=1, keepdims=True)
                parts.append(jnp.exp2((sh - top) * scale).astype(BF16))
            e = jnp.concatenate(parts, axis=1)
            e_s[w * pairs + p] = e
            vals = jnp.concatenate(
                [jnp.concatenate([v0, ones0], axis=1), jnp.concatenate([v1, ones1], axis=1)], axis=0
            )
            both = mm(e, vals)
            inv = 1.0 / both[:, 128:]
            o = (both[:, :128] * inv).astype(BF16)
            dst = (pl.ds(sq, wq), pl.ds(c, 128))
            o_s[dst] = jnp.where(in_q, o, o_s[dst])
            inv_s[dst] = jnp.where(in_q, inv, inv_s[dst])
        return carry

    length, count = meta
    lax.fori_loop(0, jnp.where(length <= 128, (count + 1) // 2, count), one, 0)


def attend_bwd(meta, qkv_s, o_s, inv_s, e_s, go_s, gqkv_s, wq, wk, pairs, width):
    rows = qkv_s.shape[0]

    def one(w, carry):
        lo, hi, length, sq, sk = window(meta, w, wq, wk, rows)
        in_q, _ = seg_of(sq, wq, lo, hi, length)
        in_k, _ = seg_of(sk, wk, lo, hi, length)
        for p in range(pairs):
            c = 128 * p
            e = e_s[w * pairs + p]
            q0, q1 = halves(qkv_s[pl.ds(sq, wq), c : c + 128])
            k0, k1 = halves(qkv_s[pl.ds(sk, wk), width + c : width + c + 128])
            v0, v1 = halves(qkv_s[pl.ds(sk, wk), 2 * width + c : 2 * width + c + 128])
            dst_q = (pl.ds(sq, wq), pl.ds(c, 128))
            go = (go_s[dst_q].astype(F32) * inv_s[dst_q]).astype(BF16)
            prod0, prod1 = halves(go.astype(F32) * o_s[dst_q].astype(F32))
            d = (jnp.sum(prod0, axis=1, keepdims=True), jnp.sum(prod1, axis=1, keepdims=True))
            gp = mm_t(go, jnp.concatenate([v0, v1], axis=0))
            gs = []
            for h in range(2):
                sl = slice(h * wk, (h + 1) * wk)
                gs.append((e[:, sl].astype(F32) * (gp[:, sl] - d[h])).astype(BF16))
            gq = mm(jnp.concatenate(gs, axis=1), jnp.concatenate([k0, k1], axis=0)) * 0.125
            gk = t_mm(jnp.concatenate(gs, axis=0), jnp.concatenate([q0, q1], axis=0)) * 0.125
            gv = t_mm(
                jnp.concatenate([e[:, :wk], e[:, wk:]], axis=0), jnp.concatenate(halves(go), axis=0)
            )
            gqkv_s[dst_q] = jnp.where(in_q, gq.astype(BF16), gqkv_s[dst_q])
            dst_k = (pl.ds(sk, wk), pl.ds(width + c, 128))
            gqkv_s[dst_k] = jnp.where(in_k, gk.astype(BF16), gqkv_s[dst_k])
            dst_v = (pl.ds(sk, wk), pl.ds(2 * width + c, 128))
            gqkv_s[dst_v] = jnp.where(in_k, gv.astype(BF16), gqkv_s[dst_v])
        return carry

    length, count = meta
    lax.fori_loop(0, jnp.where(length <= 128, (count + 1) // 2, count), one, 0)


WIDE = (352, 384)
NARROW = (224, 256)


def fold_matrix(part, count, high):
    rows, cols = 4 * count * part, count * high
    r = lax.broadcasted_iota(jnp.int32, (rows, cols), 0).astype(F32)
    c = lax.broadcasted_iota(jnp.int32, (rows, cols), 1).astype(F32)
    block = jnp.floor((c + 0.5) * (1.0 / high))
    inner = c - block * high
    piece = jnp.floor((inner + 0.5) * (1.0 / part))
    want = piece * (count * part) + block * part + (inner - piece * part)
    return jnp.where(jnp.logical_and(want == r, piece < 4), 1.0, 0.0).astype(BF16)


def unfold(blocks, dsts, part, high):
    count = 96 // part
    pick = fold_matrix(part, count, high)
    for t in range(len(blocks) // count):
        group = jnp.concatenate([blocks[j][...] for j in range(t * count, (t + 1) * count)], axis=0)
        full = mm(pick, group).astype(BF16)
        for a in range(4):
            dsts[a][96 * t : 96 * (t + 1), :] = full[96 * a : 96 * (a + 1), :]


def fold(srcs, blocks, part, high):
    count = 96 // part
    pick = fold_matrix(part, count, high)
    for t in range(len(blocks) // count):
        rows = slice(96 * t, 96 * (t + 1))
        four = jnp.concatenate([s[rows, :].astype(BF16) for s in srcs], axis=0)
        full = t_mm(pick, four).astype(BF16)
        for i in range(count):
            blocks[t * count + i][...] = full[i * high : (i + 1) * high, :]


def unfold_vectors(blocks, vec, part):
    n = len(blocks)
    width = part * n
    lane = lax.broadcasted_iota(jnp.int32, (8, 128), 1)
    total = jnp.zeros((8, width), F32)
    wide = jnp.zeros((8, 4 * width), F32)
    for j in range(n):
        pair = blocks[j][...].astype(F32)
        one = jnp.where(lane < part, pair[0:8], 0.0)
        one = jnp.concatenate([one, jnp.zeros((8, width - 128), F32)], axis=1)
        total = total + pltpu.roll(one, j * part, 1)
        one = jnp.where(lane < 4 * part, pair[8:16], 0.0)
        one = jnp.concatenate([one, jnp.zeros((8, 4 * width - 128), F32)], axis=1)
        wide = wide + pltpu.roll(one, 4 * j * part, 1)
    vec[...] = jnp.zeros_like(vec)
    for i, (row, col) in enumerate(VECTORS):
        vec[row : row + 1, col * width : (col + 1) * width] = total[i : i + 1]
    vec[V_FC1 : V_FC1 + 1, :] = wide[0:1]


def fold_vectors(vec, blocks, part):
    n = len(blocks)
    width = part * n
    eight = jnp.concatenate(
        [vec[row : row + 1, col * width : (col + 1) * width] for row, col in VECTORS], axis=0
    )
    wide = jnp.broadcast_to(vec[V_FC1 : V_FC1 + 1, :], (8, 4 * width))
    for j in range(n):
        blocks[j][0:8, :] = pltpu.roll(eight, (width - j * part) % width, 1)[:, :128]
        blocks[j][8:16, :] = pltpu.roll(wide, (4 * width - 4 * j * part) % (4 * width), 1)[:, :128]


VECTORS = ((V_GAIN1, 0), (V_SHIFT1, 0), (V_QKV, 0), (V_QKV, 2), (V_OUT, 0), (V_GAIN2, 0), (V_SHIFT2, 0), (V_FC2, 0))


def layer_kernel(
    tokens, counts, x_ref, cot_ref, qkv_ref, wout_ref, w1_ref, w2_ref, vec,
    out_ref, gqkv_ref, gmix_ref, p_fc1_ref, p_fc2_ref, a_out, a_vec,
    wout, w1, w2, p_fc1, p_fc2, sems, a_fc1, a_fc2, o_s, inv_s, e1_s, e2_s, h2_s, act_s, gpre_s, gy_s, gb_s, go_s,
    part, phases=("af", "mlp", "wg", "ab"), tile=512, chunk=256,
):
    m = pl.program_id(0)
    me = lax.axis_index("dp")
    rows, width = x_ref.shape[1], x_ref.shape[2]
    hidden = w1.shape[1]
    pairs = HEADS // 2
    length, count = tokens[m, me], counts[m, me]
    meta = (length, count)
    total = length * count
    qkv_s, gqkv_s, gmix_s = qkv_ref.at[0], gqkv_ref.at[0], gmix_ref.at[0]

    loads = [
        pltpu.make_async_copy(a, b, sems.at[i])
        for i, (a, b) in enumerate(((wout_ref, wout), (w1_ref, w1), (w2_ref, w2)))
    ]
    stores = [
        pltpu.make_async_copy(a, b, sems.at[3 + i])
        for i, (a, b) in enumerate(((p_fc1, p_fc1_ref), (p_fc2, p_fc2_ref)))
    ]
    final_step = m == pl.num_programs(0) - 1

    @pl.when(m == 0)
    def _():
        for load in loads:
            load.start()
        for ref in (a_out, a_fc1, a_fc2, a_vec):
            ref[...] = jnp.zeros_like(ref)

    def v(i, n=width):
        return vec[i : i + 1, 0:n]

    def add_vec(i, val):
        a_vec[i : i + 1, 0 : val.shape[1]] += val

    o_s[...] = qkv_s[:, 2 * width :]

    if "af" in phases:
        fwd = functools.partial(attend_fwd, meta, qkv_s, o_s, inv_s)
        @pl.when(length > 256)
        def _():
            fwd(e1_s, *WIDE, pairs, width)
        @pl.when(length <= 256)
        def _():
            fwd(e2_s, *NARROW, pairs, width)

    @pl.when(m == 0)
    def _():
        for load in loads:
            load.wait()

    if "mlp" in phases:
        def mlp(i, c):
            r = pl.ds(pl.multiple_of(i * tile, tile), tile)
            valid = (i * tile + lax.broadcasted_iota(jnp.int32, (tile, 1), 0)) < total
            mixed = x_ref[0, r, :].astype(F32) + mm(o_s[r, :], wout[...]) + v(V_OUT)
            n2, r2 = norm_rows(mixed)
            h2 = (n2 * v(V_GAIN2) + v(V_SHIFT2)).astype(BF16)
            h2_s[r, :] = h2
            gy = jnp.where(valid, cot_ref[0, r, :].astype(F32), 0.0)
            gyl = gy.astype(BF16)
            gy_s[r, :] = gyl
            add_vec(G_FC2, col_sum(gy))
            for f in range(0, hidden, chunk):
                fs = slice(f, f + chunk)
                pre = mm(h2, w1[:, fs]) + vec[V_FC1 : V_FC1 + 1, fs]
                cdf = 0.5 * lax.erf(pre * 0.7071067811865476) + 0.5
                act_s[r, fs] = (pre * cdf).astype(BF16)
                slope = cdf + pre * (jnp.exp(pre * pre * -0.5) * 0.3989422804014327)
                gpre = (slope * mm_t(gyl, w2[fs, :])).astype(BF16)
                gpre_s[r, fs] = gpre
                a_vec[G_FC1 : G_FC1 + 1, fs] += col_sum(gpre.astype(F32))
            final = mixed + mm(act_s[r, :], w2[...]) + v(V_FC2)
            out_ref[0, r, :] = jnp.where(valid, final, 0.0).astype(BF16)
            gh2 = mm_t(gpre_s[r, :], w1[...])
            add_vec(G_GAIN2, col_sum(gh2 * n2))
            add_vec(G_SHIFT2, col_sum(gh2))
            gmix = gy + norm_back(n2, r2, gh2 * v(V_GAIN2))
            gmix_s[r, :] = gmix
            gb = gmix.astype(BF16)
            gb_s[r, :] = gb
            add_vec(G_OUT, col_sum(gb.astype(F32)))
            go_s[r, :] = mm_t(gb, wout[...]).astype(BF16)
            return c
        lax.fori_loop(0, rows // tile, mlp, 0)

    if "wg" in phases:
        a_fc1[...] += t_mm(h2_s[...], gpre_s[...])
        a_fc2[...] += t_mm(gy_s[...], act_s[...])
        a_out[...] += t_mm(o_s[...], gb_s[...])

    @pl.when(final_step)
    def _():
        high = p_fc1.shape[0] // (width // part)
        blocks = [p_fc1.at[j * high : (j + 1) * high, :] for j in range(width // part)]
        fold([a_fc1.at[:, i * width : (i + 1) * width] for i in range(4)], blocks, part, high)
        for i in range(0, hidden, 128):
            p_fc2[i : i + 128, :] = jnp.transpose(a_fc2[:, i : i + 128]).astype(BF16)
        for store in stores:
            store.start()

    gqkv_s[:, : 2 * width] = jnp.zeros((rows, 2 * width), BF16)
    gqkv_s[:, 2 * width :] = go_s[...]

    if "ab" in phases:
        bwd = functools.partial(attend_bwd, meta, qkv_s, o_s, inv_s)
        @pl.when(length > 256)
        def _():
            bwd(e1_s, go_s, gqkv_s, *WIDE, pairs, width)
        @pl.when(length <= 256)
        def _():
            bwd(e2_s, go_s, gqkv_s, *NARROW, pairs, width)

    @pl.when(final_step)
    def _():
        for store in stores:
            store.wait()


def layer_call(tokens, counts, x, cot, qkv, wout, w1, w2, vec, n, **kw):
    micro, rows, width = x.shape
    hidden = w2.shape[0]
    part = width // n
    high = -(-4 * part // 16) * 16
    def per_step(cols):
        return pl.BlockSpec((1, rows, cols), lambda m: (m, 0, 0))
    def whole(shape):
        return pl.BlockSpec(shape, lambda m: (0, 0), pipeline_mode=pl.Buffered(1))
    hbm = pl.BlockSpec(memory_space=pl.ANY)
    bf = lambda n: pltpu.VMEM((rows, n), BF16)
    outs = [(x.shape, BF16), ((micro, rows, 3 * width), BF16), (x.shape, F32)]
    kept = [((n * high, width), BF16), ((hidden, width), BF16), ((width, width), F32), (vec.shape, F32)]
    return pl.pallas_call(
        functools.partial(layer_kernel, part=part, **kw),
        grid=(micro,),
        in_specs=[pl.BlockSpec(memory_space=pltpu.SMEM)] * 2 + [per_step(width), per_step(width), per_step(3 * width)]
        + [hbm] * 3 + [whole(vec.shape)],
        out_specs=[per_step(s[2]) for s, _ in outs] + [hbm] * 2 + [whole(s) for s, _ in kept[2:]],
        out_shape=[jax.ShapeDtypeStruct(s, d) for s, d in outs + kept],
        scratch_shapes=[pltpu.VMEM(a.shape, BF16) for a in (wout, w1, w2)] + [
            pltpu.VMEM(kept[0][0], BF16), pltpu.VMEM(kept[1][0], BF16), pltpu.SemaphoreType.DMA((5,)),
            pltpu.VMEM((width, hidden), F32), pltpu.VMEM((width, hidden), F32),
            bf(width), pltpu.VMEM((rows, width), F32),
            pltpu.VMEM((9, 352, 768), BF16), pltpu.VMEM((15, 224, 512), BF16),
            bf(width), bf(hidden), bf(hidden), bf(width), bf(width), bf(width),
        ],
        compiler_params=pltpu.CompilerParams(vmem_limit_bytes=64 * 2**20 - 2**17),
    )(tokens, counts, x, cot, qkv, wout, w1, w2, vec)


def bit_of(me, b):
    return (me // (1 << b)) % 2


class Place:
    def __init__(self, n):
        self.me = lax.axis_index("dp")
        self.count = n // 8
        self.z, self.y, self.x, self.c = self.me // 8, bit_of(self.me, 2), bit_of(self.me, 1), bit_of(self.me, 0)
        self.over_y = self.me + 4 * (1 - 2 * self.y)
        self.over_x = self.me + 2 * (1 - 2 * self.x)
        self.twin = self.me + (1 - 2 * self.c)
        self.steps = sorted(range(1, self.count), key=lambda k: min(k, self.count - k))

    def ahead(self, k):
        return (self.z + k) % self.count

    def behind(self, k):
        return (self.z + self.count - k) % self.count

    def at(self, z):
        return self.me + 8 * (z - self.z)

    def meet(self):
        barrier = pltpu.get_barrier_semaphore()
        others = [self.over_y, self.over_x, self.twin] + [self.at(self.ahead(k)) for k in range(1, self.count)]
        for device in others:
            pl.semaphore_signal(barrier, inc=1, device_id=(device,), device_id_type=MESH)
        pl.semaphore_wait(barrier, len(others))


LINE, ALONG_X, ALONG_Y, DIAG_X, DIAG_Y, TWIN = range(6)


class Wire:
    def __init__(self, place, cut, send, recv):
        self.place, self.cut, self.send, self.recv, self.started = place, cut, send, recv, []

    def copy(self, kind, k, src, dst, device):
        return pltpu.make_async_remote_copy(
            src_ref=src, dst_ref=dst, send_sem=self.send.at[kind, k], recv_sem=self.recv.at[kind, k],
            device_id=(device,), device_id_type=MESH)

    def push(self, kind, k, src, dst, device):
        copy = self.copy(kind, k, src, dst, device)
        copy.start()
        self.started.append(copy)

    def arrive(self, kind, k, dst):
        self.copy(kind, k, dst, dst, self.place.twin).wait_recv()

    def finish(self):
        for copy in self.started:
            copy.wait_send()

    def columns(self, k, width):
        if self.cut is None:
            return slice(0, width), None
        cut = 128 if (k + self.cut) % 2 else width - 128
        return slice(0, cut), slice(cut, width)


class Gather(Wire):
    def __init__(self, place, ref, cut, send, recv):
        super().__init__(place, cut, send, recv)
        self.ref = ref

    def block(self, k, over_y, over_x, cols=slice(None)):
        p = self.place
        y = 1 - p.y if over_y else p.y
        x = 1 - p.x if over_x else p.x
        return self.ref.at[p.behind(k), y, x, p.c, :, cols]

    def same(self, kind, k, view, device):
        self.push(kind, k, view, view, device)

    def begin(self):
        p = self.place
        for k in p.steps:
            self.same(LINE, k, self.block(0, False, False), p.at(p.ahead(k)))

    def line(self, k):
        view = self.block(k, False, False)
        if k:
            self.arrive(LINE, k, view)
        self.same(ALONG_X, k, view, self.place.over_x)
        self.same(ALONG_Y, k, view, self.place.over_y)

    def plane(self, k):
        first, second = self.columns(k, self.ref.shape[-1])
        self.arrive(ALONG_X, k, self.block(k, False, True))
        self.same(DIAG_Y, k, self.block(k, False, True, first), self.place.over_y)
        self.arrive(ALONG_Y, k, self.block(k, True, False))
        if second is not None:
            self.same(DIAG_X, k, self.block(k, True, False, second), self.place.over_x)

    def corner(self, k):
        first, second = self.columns(k, self.ref.shape[-1])
        self.arrive(DIAG_Y, k, self.block(k, True, True, first))
        if second is not None:
            self.arrive(DIAG_X, k, self.block(k, True, True, second))
        p = self.place
        self.same(TWIN, k, self.ref.at[p.behind(k), :, :, p.c], p.twin)

    def last(self):
        p = self.place
        for k in range(p.count):
            self.arrive(TWIN, k, self.ref.at[p.behind(k), :, :, 1 - p.c])


class Scatter(Wire):
    def __init__(self, place, src, cut, scratch, out, send, recv):
        super().__init__(place, cut, send, recv)
        self.src, self.out = src, out
        self.twins, self.diag_x, self.diag_y, self.from_x, self.from_y, self.lines, self.sums = scratch

    def half(self, k, y, x):
        p = self.place
        z = p.ahead(k)
        return self.src[z, y, x, p.c].astype(F32) + self.twins[z, y, x].astype(F32)

    def begin(self):
        p = self.place
        for k in p.steps + [0]:
            z = p.ahead(k)
            self.push(TWIN, k, self.src.at[z, :, :, 1 - p.c], self.twins.at[z], p.twin)

    def corner(self, k):
        p = self.place
        self.arrive(TWIN, k, self.twins.at[p.ahead(k)])
        first, second = self.columns(k, self.src.shape[-1])
        held = self.sums.at[0, k]
        held[...] = self.half(k, 1 - p.y, 1 - p.x).astype(held.dtype)
        self.push(DIAG_Y, k, held.at[:, first], self.diag_x.at[k, :, first], p.over_y)
        if second is not None:
            self.push(DIAG_X, k, held.at[:, second], self.diag_y.at[k, :, second], p.over_x)

    def plane(self, k):
        p = self.place
        first, second = self.columns(k, self.src.shape[-1])
        self.arrive(DIAG_Y, k, self.diag_x.at[k, :, first])
        held = self.sums.at[1, k]
        total = self.half(k, p.y, 1 - p.x)
        held[:, first] = (total[:, first] + self.diag_x[k, :, first].astype(F32)).astype(held.dtype)
        if second is not None:
            held[:, second] = total[:, second].astype(held.dtype)
        self.push(ALONG_X, k, held, self.from_x.at[k], p.over_x)
        held = self.sums.at[2, k]
        total = self.half(k, 1 - p.y, p.x)
        if second is None:
            held[...] = total.astype(held.dtype)
        else:
            self.arrive(DIAG_X, k, self.diag_y.at[k, :, second])
            held[:, first] = total[:, first].astype(held.dtype)
            held[:, second] = (total[:, second] + self.diag_y[k, :, second].astype(F32)).astype(held.dtype)
        self.push(ALONG_Y, k, held, self.from_y.at[k], p.over_y)

    def line(self, k):
        p = self.place
        self.arrive(ALONG_X, k, self.from_x.at[k])
        self.arrive(ALONG_Y, k, self.from_y.at[k])
        total = self.half(k, p.y, p.x) + self.from_x[k].astype(F32) + self.from_y[k].astype(F32)
        if k == 0:
            self.out[...] = total
            return
        held = self.sums.at[3, k]
        held[...] = total.astype(held.dtype)
        self.push(LINE, k, held, self.lines.at[k], p.at(p.ahead(k)))

    def last(self):
        total = self.out[...]
        for k in self.place.steps:
            self.arrive(LINE, k, self.lines.at[k])
            total = total + self.lines[k].astype(F32)
        self.out[...] = total


def gather_kernel(
    n, tile, x_ref, w_qkv, w_out, w_fc1, w_fc2, *refs,
):
    small = refs[:9]
    qkv_ref, wqkv, wout, w1, g_fc2, vec, x_s, qkv_s, g_attn, g_fc1, g_vec, pad, pad_vec, x_sem, qkv_sem, send, recv = refs[9:]
    place = Place(n)
    micro, rows, width = x_s.shape
    part = width // n
    height = g_fc1.shape[-2]
    loads = [pltpu.make_async_copy(x_ref.at[m], x_s.at[m], x_sem.at[m]) for m in range(micro)]
    for load in loads:
        load.start()
    own = (place.z, place.y, place.x, place.c)
    if height > 4 * part:
        pad[...] = jnp.zeros_like(pad)
    pad_vec[...] = jnp.zeros_like(pad_vec)
    for i in range(8):
        pad_vec[i : i + 1, 0:part] = small[i][...].astype(F32).reshape(1, part)
    pad_vec[8:9, 0 : 4 * part] = small[8][...].astype(F32).reshape(1, 4 * part)
    g_vec[own] = pad_vec[...].astype(BF16)
    def fold_own(dst, four):
        for a, piece in enumerate(four):
            pad[a * part : (a + 1) * part, :] = piece.astype(F32)
        dst[own] = pad[...].astype(BF16)
    fold_own(g_attn, [w_qkv[:, a * width : (a + 1) * width] for a in range(3)] + [w_out[...]])
    fold_own(g_fc1, [w_fc1[:, a * width : (a + 1) * width] for a in range(4)])
    if height > 4 * part:
        fold_own(g_fc2, [w_fc2[a * part : (a + 1) * part, :] for a in range(4)])
    else:
        g_fc2[own] = w_fc2[...]
    place.meet()

    refs = (g_vec, g_attn, g_fc1, g_fc2)
    parts = [Gather(place, ref, cut, send.at[i], recv.at[i]) for i, (ref, cut) in enumerate(zip(refs, (None, 0, 1, 0)))]
    urgent, rest = parts[:2], parts[2:]
    order = [0] + place.steps
    todo = [(p, "line", k) for k in order for p in rest]
    todo += [(p, "plane", k) for k in order for p in rest]
    todo += [(p, "corner", k) for k in order for p in rest]

    def some(count):
        for p, stage, k in todo[:count]:
            getattr(p, stage)(k)
        del todo[:count]

    for p in urgent:
        p.begin()
    for p in urgent:
        p.line(0)
    for k in place.steps:
        for p in urgent:
            p.line(k)
    for p in rest:
        p.begin()
    for k in order:
        for p in urgent:
            p.plane(k)
        some(1)
    for k in order:
        for p in urgent:
            p.corner(k)
        some(1)
    for p in urgent:
        p.last()
    flat = lambda ref: [ref.at[j // 8, (j // 4) % 2, (j // 2) % 2, j % 2] for j in range(n)]
    unfold_vectors(flat(g_vec), vec, part)
    unfold(flat(g_attn), [wqkv.at[:, 0:width], wqkv.at[:, width : 2 * width], wqkv.at[:, 2 * width :], wout], part, height)

    def qkv_part(m, i):
        r = pl.ds(i * tile, tile)
        n1, _ = norm_rows(x_s[m, r, :].astype(F32))
        h1 = (n1 * vec[V_GAIN1 : V_GAIN1 + 1, 0:width] + vec[V_SHIFT1 : V_SHIFT1 + 1, 0:width]).astype(BF16)
        qkv_s[m, r, :] = (mm(h1, wqkv[...]) + vec[V_QKV : V_QKV + 1, 0 : 3 * width]).astype(BF16)

    pieces = rows // tile
    stores = []
    for m in range(micro):
        for i in range(pieces):
            where = (m, pl.ds(i * tile, tile))
            stores.append(pltpu.make_async_copy(qkv_s.at[where], qkv_ref.at[where], qkv_sem.at[m, i]))
    turns = micro * pieces
    each = -(-len(todo) // max(turns, 1))
    for m in range(micro):
        loads[m].wait()
        for i in range(rows // tile):
            qkv_part(m, i)
            stores[m * pieces + i].start()
            some(each)
    some(len(todo))
    rest[0].last()
    unfold(flat(g_fc1), [w1.at[:, i * width : (i + 1) * width] for i in range(4)], part, height)
    rest[1].last()
    for p in parts:
        p.finish()
    for store in stores:
        store.wait()


def gather_call(n, x, w_qkv, w_out, w_fc1, w_fc2, small, collective_id, tile=512):
    micro, rows, width = x.shape
    height = -(-4 * w_out.shape[0] // 16) * 16
    vmem, hbm = pl.BlockSpec(memory_space=pltpu.VMEM), pl.BlockSpec(memory_space=pl.ANY)
    grid = (n // 8, 2, 2, 2)
    sems = pltpu.SemaphoreType.DMA((4, 6, n // 8))
    block = (height, width)
    shapes = [((micro, rows, 3 * width), BF16), ((width, 3 * width), BF16), ((width, width), BF16),
              ((width, 4 * width), BF16), (grid + block, BF16), ((8, 4 * width), F32)]
    return pl.pallas_call(
        functools.partial(gather_kernel, n, tile),
        in_specs=[hbm] + [vmem] * (4 + len(small)),
        out_specs=[hbm] + [vmem] * 5,
        out_shape=[jax.ShapeDtypeStruct(s, d) for s, d in shapes],
        scratch_shapes=[
            pltpu.VMEM(x.shape, BF16), pltpu.VMEM((micro, rows, 3 * width), BF16),
            pltpu.VMEM(grid + block, BF16), pltpu.VMEM(grid + block, BF16), pltpu.VMEM(grid + (16, 128), BF16),
            pltpu.VMEM(block, F32), pltpu.VMEM((16, 128), F32),
            pltpu.SemaphoreType.DMA((micro,)), pltpu.SemaphoreType.DMA((micro, rows // tile)), sems, sems,
        ],
        compiler_params=pltpu.CompilerParams(
            collective_id=collective_id, has_side_effects=True, vmem_limit_bytes=60 * 2**20),
    )(x, w_qkv, w_out, w_fc1, w_fc2, *small)


def scatter_kernel(
    n, tile, x_ref, gqkv_ref, gmix_ref, wqkv, vec, p_fc1, p_fc2, p_out, gvec,
    ig_ref, o_attn, o_fc1, o_fc2, o_vec,
    x_s, gqkv_s, gmix_s, ig_s, n1_s, acc, acc_vec, p_attn, p_vec, in_sem, out_sem, send, recv, *rest,
):
    place = Place(n)
    micro, rows, width = x_s.shape
    part = width // n
    height = p_fc1.shape[-2]
    loads = []
    for m in range(micro):
        pairs = ((x_ref, x_s), (gqkv_ref, gqkv_s), (gmix_ref, gmix_s))
        loads.append([pltpu.make_async_copy(a.at[m], b.at[m], in_sem.at[i, m]) for i, (a, b) in enumerate(pairs)])
        for load in loads[m]:
            load.start()
    place.meet()

    def stream(i, src, cut, out):
        return Scatter(place, src, cut, rest[7 * i : 7 * i + 7], out, send.at[i], recv.at[i])
    fc = [stream(0, p_fc1, 0, o_fc1), stream(1, p_fc2, 1, o_fc2)]
    attn, vecs = stream(2, p_attn, 0, o_attn), stream(3, p_vec, None, o_vec)
    order = place.steps + [0]
    def stages(streams):
        return [(s, stage, k) for stage in ("corner", "plane", "line") for k in order for s in streams]
    todo = stages(fc)

    def some(count):
        for s, stage, k in todo[:count]:
            getattr(s, stage)(k)
        del todo[:count]

    for s in fc:
        s.begin()

    def v(i, cols=width):
        return vec[i : i + 1, 0:cols]

    acc_vec[...] = gvec[...]
    for m in range(micro):
        for load in loads[m][:2]:
            load.wait()
        for i in range(rows // tile):
            r = pl.ds(i * tile, tile)
            n1, _ = norm_rows(x_s[m, r, :].astype(F32))
            n1_s[m, r, :] = n1.astype(BF16)
        g = t_mm(n1_s[m], gqkv_s[m])
        acc[...] = g if m == 0 else acc[...] + g
        acc_vec[V_QKV : V_QKV + 1, 0 : 3 * width] += col_sum(gqkv_s[m].astype(F32))
        some(len(order) * 2 if m == 0 else len(order))
    total = acc[...]
    sums = acc_vec[V_QKV : V_QKV + 1, 0 : 3 * width]
    table = jnp.concatenate([jnp.broadcast_to(v(V_GAIN1), (64, width)), jnp.broadcast_to(v(V_SHIFT1), (64, width))], axis=0)
    table = jnp.transpose(table)
    acc[...] = total * table[:, 0:1] + sums * table[:, 64:65]
    flat = lambda ref: [ref.at[j // 8, (j // 4) % 2, (j // 2) % 2, j % 2] for j in range(n)]
    fold([acc.at[:, 0:width], acc.at[:, width : 2 * width], acc.at[:, 2 * width :], p_out], flat(p_attn), part, height)
    attn.begin()
    dots = jnp.sum(wqkv[...].astype(F32) * total, axis=1, keepdims=True)
    acc_vec[V_GAIN1 : V_GAIN1 + 1, 0:width] += jnp.transpose(jnp.broadcast_to(dots, (width, 128)))[0:1, :]
    one = sums.astype(BF16).astype(F32)
    two = (sums - one).astype(BF16).astype(F32)
    three = sums - one - two
    row = lax.broadcasted_iota(jnp.int32, (16, 3 * width), 0)
    split = jnp.where(row == 0, one, jnp.where(row == 1, two, jnp.where(row == 2, three, 0.0))).astype(BF16)
    acc_vec[V_SHIFT1 : V_SHIFT1 + 1, 0:width] += col_sum(mm_t(split, wqkv[...]))
    fold_vectors(acc_vec, flat(p_vec), part)
    vecs.begin()
    late = [t for pair in zip(stages([attn]), stages([vecs])) for t in pair]
    todo = [t for pair in zip(todo, late) for t in pair] + todo[len(late) :] + late[len(todo) :]

    stores = [pltpu.make_async_copy(ig_s.at[m], ig_ref.at[m], out_sem.at[m]) for m in range(micro)]
    turns = micro * (rows // tile)
    each = -(-len(todo) // turns)
    for m in range(micro):
        loads[m][2].wait()
        for i in range(rows // tile):
            r = pl.ds(i * tile, tile)
            gqkv = gqkv_s[m, r, :]
            gh1 = mm_t(gqkv, wqkv[...])
            n1, r1 = norm_rows(x_s[m, r, :].astype(F32))
            ig_s[m, r, :] = (gmix_s[m, r, :] + norm_back(n1, r1, gh1 * v(V_GAIN1))).astype(BF16)
            some(each)
        stores[m].start()
    some(len(todo))
    for s in fc + [attn, vecs]:
        s.last()
    for s in fc + [attn, vecs]:
        s.finish()
    for store in stores:
        store.wait()


def scatter_call(n, x, gqkv, gmix, wqkv, vec, p_fc1, p_fc2, p_out, gvec, collective_id, tile=512):
    micro, rows, width = x.shape
    height = p_fc1.shape[0] // n
    vmem, hbm = pl.BlockSpec(memory_space=pltpu.VMEM), pl.BlockSpec(memory_space=pl.ANY)
    places = n // 8
    grid = (places, 2, 2, 2)
    scratch = []
    for shape, dtype in [((height, width), BF16)] * 3 + [((16, 128), F32)]:
        scratch += [pltpu.VMEM((places, 2, 2) + shape, dtype)]
        scratch += [pltpu.VMEM((places,) + shape, dtype) for _ in range(5)]
        scratch += [pltpu.VMEM((4, places) + shape, dtype)]
    block = jax.ShapeDtypeStruct((height, width), F32)
    sems = pltpu.SemaphoreType.DMA((4, 6, places))
    return pl.pallas_call(
        functools.partial(scatter_kernel, n, tile),
        in_specs=[hbm] * 3 + [vmem] * 6,
        out_specs=[hbm] + [vmem] * 4,
        out_shape=[jax.ShapeDtypeStruct(x.shape, BF16), block, block, block, jax.ShapeDtypeStruct((16, 128), F32)],
        scratch_shapes=[
            pltpu.VMEM(x.shape, BF16), pltpu.VMEM(gqkv.shape, BF16), pltpu.VMEM(gmix.shape, F32), pltpu.VMEM(x.shape, BF16),
            pltpu.VMEM(x.shape, BF16), pltpu.VMEM((width, 3 * width), F32), pltpu.VMEM(vec.shape, F32),
            pltpu.VMEM(grid + (height, width), BF16), pltpu.VMEM(grid + (16, 128), F32),
            pltpu.SemaphoreType.DMA((3, micro)), pltpu.SemaphoreType.DMA((micro,)), sems, sems,
        ] + scratch,
        compiler_params=pltpu.CompilerParams(
            collective_id=collective_id, has_side_effects=True, vmem_limit_bytes=62 * 2**20),
    )(x, gqkv, gmix, wqkv, vec, p_fc1.reshape(grid + (height, width)), p_fc2.reshape(grid + (height, width)), p_out, gvec)


def finish_kernel(part, ig_in, s_attn, s_fc1, s_fc2, s_vec, ig, g_qkv, g_out, g_fc1, g_fc2, *rest):
    vectors, held, sems = rest[:9], rest[9], rest[10]
    width = s_attn.shape[1]
    micro, rows = held.shape[:2]
    cuts = [(m, pl.ds(h * (rows // 2), rows // 2)) for m in range(micro) for h in range(2)]
    loads = [pltpu.make_async_copy(ig_in.at[c], held.at[c], sems.at[0, i]) for i, c in enumerate(cuts)]
    stores = [pltpu.make_async_copy(held.at[c], ig.at[c], sems.at[1, i]) for i, c in enumerate(cuts)]
    for load in loads:
        load.start()
    for a in range(4):
        own = slice(a * part, (a + 1) * part)
        if a < 3:
            g_qkv[:, a * width : (a + 1) * width] = s_attn[own, :]
        else:
            g_out[...] = s_attn[own, :]
        g_fc1[:, a * width : (a + 1) * width] = s_fc1[own, :]
    g_fc2[...] = s_fc2[0 : 4 * part, :]
    for i in range(8):
        vectors[i][...] = s_vec[i, 0:part]
    vectors[8][...] = s_vec[8, 0 : 4 * part]
    for load, store in zip(loads, stores):
        load.wait()
        store.start()
    for store in stores:
        store.wait()


def finish_call(part, ig, s_attn, s_fc1, s_fc2, s_vec):
    width = s_attn.shape[1]
    vmem, hbm = pl.BlockSpec(memory_space=pltpu.VMEM), pl.BlockSpec(memory_space=pl.ANY)
    shapes = [(part, 3 * width), (part, width), (part, 4 * width), (4 * part, width)] + [(part,)] * 8 + [(4 * part,)]
    return pl.pallas_call(
        functools.partial(finish_kernel, part),
        in_specs=[hbm] + [vmem] * 4,
        out_specs=[hbm] + [vmem] * 13,
        out_shape=[jax.ShapeDtypeStruct(ig.shape, ig.dtype)] + [jax.ShapeDtypeStruct(s, F32) for s in shapes],
        scratch_shapes=[pltpu.VMEM(ig.shape, ig.dtype), pltpu.SemaphoreType.DMA((2, 2 * ig.shape[0]))],
    )(ig, s_attn, s_fc1, s_fc2, s_vec)


def body(inputs, cotangent, w_qkv, w_out, w_fc1, w_fc2, gain1, shift1, q_bias, v_bias, out_bias, gain2, shift2,
         fc1_bias, fc2_bias, image_tokens, image_count):
    n = lax.axis_size("dp")
    part, width = w_out.shape
    hidden = w_fc1.shape[1]
    high = -(-4 * part // 16) * 16
    small = (gain1, shift1, q_bias, v_bias, out_bias, gain2, shift2, fc2_bias, fc1_bias)
    qkv, wqkv, wout, w1, g_fc2, vec = gather_call(n, inputs, w_qkv, w_out, w_fc1, w_fc2, small, 1)
    w2 = g_fc2.reshape(n, high, width)[:, : 4 * part].reshape(hidden, width)
    out, gqkv, gmix, p_fc1, p_fc2, a_out, a_vec = layer_call(
        image_tokens, image_count, inputs, cotangent, qkv, wout, w1, w2, vec, n)
    p_fc2 = jnp.pad(p_fc2.reshape(n, 4 * part, width), ((0, 0), (0, high - 4 * part), (0, 0))).reshape(n * high, width)
    ig, s_attn, s_fc1, s_fc2, s_vec = scatter_call(
        n, inputs, gqkv, gmix, wqkv, vec, p_fc1, p_fc2, a_out, a_vec, 2)
    ig, g_qkv, g_out, g_fc1, g_fc2, *v = finish_call(part, ig, s_attn, s_fc1, s_fc2, s_vec)
    return (out, ig, g_qkv, g_out, g_fc1, g_fc2, *v[:7], v[8], v[7])


def solution(mesh):
    big, mat, one = P(None, "dp", None), P("dp", None), P("dp")
    return jax.shard_map(
        body, mesh=mesh,
        in_specs=(big, big) + (mat,) * 4 + (one,) * 9 + (P(), P()),
        out_specs=(big, big) + (mat,) * 4 + (one,) * 9,
        check_vma=False,
    )
```
